128 devices in a mesh: gx: 32 (over y, x_lo, z), gy: 4 (over x_hi, core).
Axes of the slice: x: 4 (x_hi: 2, x_lo: 2; x = x_hi * 2 + x_lo), y: 4, z: 4, core: 2. Of those that a mesh axis runs over, the one named last changes fastest.
Arguments:
- embeddings: bfloat16 [32, 512, 768], P('gy', 'gx'), may hold values from -6 to 6
- tile_valid: int32 [32, 512], P('gy', 'gx'), may hold values 0 or 1
- w_query: bfloat16 [768, 768], replicated, may hold values from -0.4375 to 0.4375
- w_key: bfloat16 [768, 768], replicated, may hold values from -0.21875 to 0.21875
- w_value: bfloat16 [768, 768], replicated, may hold values from -0.21875 to 0.21875
- w_out: bfloat16 [768, 768], replicated, may hold values from -1.25 to 1.25
- w_up: bfloat16 [768, 3072], replicated, may hold values from -0.21875 to 0.21875
- w_down: bfloat16 [3072, 768], replicated, may hold values from -0.109375 to 0.109375
- gain_attn: float32 [768], replicated, may hold values from 0.25 to 1.75
- shift_attn: float32 [768], replicated, may hold values from -4 to 4
- gain_mlp: float32 [768], replicated, may hold values from 0.25 to 1.75
- shift_mlp: float32 [768], replicated, may hold values from -4 to 4
- cotangent: bfloat16 [32, 512, 768], P('gy', 'gx'), may hold values from -6 to 6
Outputs:
- mixed: bfloat16 [32, 512, 768], P('gy', 'gx')
- grad_embeddings: float32 [32, 512, 768], P('gy', 'gx')
- grad_w_query: float32 [768, 768], replicated
- grad_w_key: float32 [768, 768], replicated
- grad_w_value: float32 [768, 768], replicated
- grad_w_out: float32 [768, 768], replicated
- grad_w_up: float32 [768, 3072], replicated
- grad_w_down: float32 [3072, 768], replicated
- grad_gain_attn: float32 [768], replicated
- grad_shift_attn: float32 [768], replicated
- grad_gain_mlp: float32 [768], replicated
- grad_shift_mlp: float32 [768], replicated
The draws below stay inside these ranges and needn't reach their ends.
All inputs are finite; a program needn't handle non-finite values. No bound on the sum of `tile_valid` on one device may be relied on, other than what follows from the above.
Results may differ from the reference program's by a relative error of at most 0.014.
The reference program's roundings to bfloat16 on the way count: a program that leaves them out, or rounds other values in their place, can miss the bound.
Values may be sent and summed in bfloat16 or wider, within the bound.
No kernel may reach another device: no remote copies, remote signals or barrier semaphores. Data moves between devices by JAX's collectives and lax.ppermute only.
A program may use at most 192 MiB of HBM per device.

```python
import functools
import math
import jax
import jax.numpy as jnp
from jax import lax

D = 768
HEADS = 16
HEAD_DIM = 48
FF = 3072
BLOCK_ROWS = 8
BLOCK_COLS = 16
STRIDE = 4
WINDOW = 8
TOK_DEV = 128
GRID_ROWS = 32
GRID_COLS = 512
REG_ROWS = 24
REG_COLS = 32
FAR_KEYS = 1024
N_GX = 32
N_GY = 4


def touch_ends(values, rng, smallest, high):
    longest = values.shape.index(max(values.shape))
    spots = []
    for shift in (0, 1):
        where = [jax.random.randint(jax.random.fold_in(rng, axis), (), 0, length) for axis, length in enumerate(values.shape)]
        where[longest] = (where[longest] + shift) % values.shape[longest]
        spots.append(tuple(where))
    return values.at[spots[0]].set(smallest).at[spots[1]].set(high)


def block_levels(key, shape, split, least, largest):
    loudness, own = 1.0, jax.random.fold_in(key, 6)
    for position, blocks in split:
        heights = jnp.exp(jax.random.uniform(jax.random.fold_in(own, position), (blocks,), jnp.float32, least / len(split), largest / len(split)))
        loudness = loudness * jnp.repeat(heights, shape[position] // blocks).reshape([-1 if axis == position else 1 for axis in range(len(shape))])
    return loudness


def noise(own_key, shape, spread, most, shards=(), held_as=jnp.bfloat16):
    array = spread * jax.random.normal(own_key, shape, jnp.float32)
    if shards:
        array = array * block_levels(own_key, shape, shards, -0.22, 0.18)
    return jnp.clip(array, -most, most).astype(held_as)


def setup_inputs(seed: int = 0) -> dict:
    splits = jax.random.split(jax.random.key(seed), 14)
    return {
        "embeddings": noise(splits[0], (GRID_ROWS, GRID_COLS, D), 1.0, 6.0, ((0, 4), (1, 32))),
        "tile_valid": touch_ends((jax.random.randint(splits[1], (GRID_ROWS, GRID_COLS), 0, 4) < 3).astype(jnp.int32), jax.random.fold_in(splits[1], 1), 0, 1),
        "w_query": noise(splits[2], (D, D), (D // 4) ** -0.5, 0.4375),
        "w_key": noise(splits[3], (D, D), D ** -0.5, 0.21875),
        "w_value": noise(splits[4], (D, D), D ** -0.5, 0.21875),
        "w_out": noise(splits[5], (D, D), (D // 32) ** -0.5, 1.25),
        "w_up": noise(splits[6], (D, FF), D ** -0.5, 0.21875),
        "w_down": noise(splits[7], (FF, D), FF ** -0.5, 0.109375),
        "gain_attn": jnp.clip(1.0 + 0.15 * jax.random.normal(splits[8], (D,), jnp.float32), 0.25, 1.75),
        "shift_attn": noise(splits[9], (D,), 0.3, 4.0, (), jnp.float32),
        "gain_mlp": jnp.clip(1.0 + 0.15 * jax.random.normal(splits[10], (D,), jnp.float32), 0.25, 1.75),
        "shift_mlp": noise(splits[11], (D,), 0.3, 4.0, (), jnp.float32),
        "cotangent": noise(splits[12], (GRID_ROWS, GRID_COLS, D), 1.0, 6.0, ((0, 4), (1, 32))),
    }


@jax.custom_vjp
def low(v):
    return lax.optimization_barrier(v.astype(jnp.bfloat16)).astype(jnp.float32)

@jax.custom_vjp
def low_back(v):
    return v

def low_keep(v):
    return (low(v), None)

def low_pass(kept, grad):
    return (grad,)

def back_keep(v):
    return (v, None)

def back_low(kept, grad):
    return (low(grad),)
low.defvjp(low_keep, low_pass)
low_back.defvjp(back_keep, back_low)
epsilon = 1e-05
highest = lax.Precision.HIGHEST

def layer_norm(inputs, gain_vec, shift_vec):
    row_mean = lax.optimization_barrier(jnp.mean(inputs, axis=-1, keepdims=True))
    centered = inputs - row_mean
    row_var = lax.optimization_barrier(jnp.mean(centered * centered, axis=-1, keepdims=True))
    return centered * lax.rsqrt(row_var + epsilon) * gain_vec + shift_vec

def matmul(left_op, right_op):
    return jnp.dot(left_op, right_op, precision=highest, preferred_element_type=jnp.float32)

def window_weights(key_flags, block_rows, block_cols, margin):
    reg_cols = block_cols + 2 * margin
    query_pos = jnp.arange(block_rows * block_cols)
    key_pos = jnp.arange(key_flags.shape[0])
    row_gap = (key_pos // reg_cols - margin)[None, :] - (query_pos // block_cols)[:, None]
    col_gap = (key_pos % reg_cols - margin)[None, :] - (query_pos % block_cols)[:, None]
    dense = (jnp.abs(row_gap) <= margin) & (jnp.abs(col_gap) <= margin)
    dilated = dense & (row_gap % 2 == 0) & (col_gap % 2 == 0)
    itself = (row_gap == 0) & (col_gap == 0)
    counted = jnp.where(itself, 1.0, key_flags[None, :]).astype(key_flags.dtype)
    return (dense.astype(key_flags.dtype) + dilated.astype(key_flags.dtype)) * counted

def attend(queries, key_rows, value_rows, pair_weights):
    score_scale = 1.0 / math.sqrt(HEAD_DIM)
    raw_scores = low_back(jnp.einsum('qhd,khd->hqk', queries, key_rows, precision=highest) * score_scale)
    masked = jnp.where(pair_weights[None] > 0, raw_scores, -1e+30)
    row_top = lax.optimization_barrier(jnp.max(masked, axis=2, keepdims=True))
    weighted = pair_weights[None] * jnp.exp(masked - row_top)
    attn_probs = weighted / lax.optimization_barrier(jnp.sum(weighted, axis=2, keepdims=True))
    return jnp.einsum('hqk,khd->qhd', low(attn_probs), value_rows, precision=highest)

def forward(key_flags, embeddings, w_query, w_key, w_value, w_out, w_up, w_down, gain_attn, shift_attn, gain_mlp, shift_mlp):
    act_attn = low(layer_norm(embeddings, gain_attn, shift_attn))
    queries = low(low_back(matmul(act_attn, w_query)))
    key_grid = low(low_back(matmul(act_attn, w_key)))
    value_grid = low(low_back(matmul(act_attn, w_value)))
    far_keys = key_grid[::STRIDE, ::STRIDE].reshape(-1, HEADS, HEAD_DIM)
    far_values = value_grid[::STRIDE, ::STRIDE].reshape(-1, HEADS, HEAD_DIM)
    far_flags = key_flags[::STRIDE, ::STRIDE].reshape(-1)
    pad_three = ((WINDOW, WINDOW), (WINDOW, WINDOW), (0, 0))
    key_padded = jnp.pad(key_grid, pad_three)
    value_padded = jnp.pad(value_grid, pad_three)
    flag_padded = jnp.pad(key_flags, ((WINDOW, WINDOW), (WINDOW, WINDOW)))
    zero_index = jnp.zeros((), jnp.int32)

    def one_block(block_index):
        row_start = (block_index // N_GX * BLOCK_ROWS).astype(jnp.int32)
        col_start = (block_index % N_GX * BLOCK_COLS).astype(jnp.int32)
        block_queries = lax.dynamic_slice(queries, (row_start, col_start, zero_index), (BLOCK_ROWS, BLOCK_COLS, D)).reshape(TOK_DEV, HEADS, HEAD_DIM)
        near_keys = lax.dynamic_slice(key_padded, (row_start, col_start, zero_index), (REG_ROWS, REG_COLS, D)).reshape(REG_ROWS * REG_COLS, HEADS, HEAD_DIM)
        near_values = lax.dynamic_slice(value_padded, (row_start, col_start, zero_index), (REG_ROWS, REG_COLS, D)).reshape(REG_ROWS * REG_COLS, HEADS, HEAD_DIM)
        near_flags = lax.dynamic_slice(flag_padded, (row_start, col_start), (REG_ROWS, REG_COLS)).reshape(-1)
        pair_weights = jnp.concatenate([window_weights(near_flags, BLOCK_ROWS, BLOCK_COLS, WINDOW), jnp.broadcast_to(far_flags[None, :], (TOK_DEV, FAR_KEYS))], axis=1)
        key_rows = jnp.concatenate([near_keys, far_keys], axis=0)
        value_rows = jnp.concatenate([near_values, far_values], axis=0)
        return attend(block_queries, key_rows, value_rows, pair_weights).reshape(BLOCK_ROWS, BLOCK_COLS, D)
    block_outs = lax.map(jax.checkpoint(one_block), jnp.arange(N_GY * N_GX, dtype=jnp.int32))
    attended = block_outs.reshape(N_GY, N_GX, BLOCK_ROWS, BLOCK_COLS, D).transpose(0, 2, 1, 3, 4).reshape(GRID_ROWS, GRID_COLS, D)
    attended = low(low_back(attended))
    middle = embeddings + low_back(matmul(attended, w_out))
    act_mlp = low(layer_norm(middle, gain_mlp, shift_mlp))
    pre_act = low_back(matmul(act_mlp, w_up))
    hidden = low(jax.nn.gelu(pre_act, approximate=False))
    return middle + low_back(matmul(hidden, w_down))

def reference(embeddings, tile_valid, w_query, w_key, w_value, w_out, w_up, w_down, gain_attn, shift_attn, gain_mlp, shift_mlp, cotangent):
    key_flags = tile_valid.astype(jnp.float32)
    output, pullback = jax.vjp(functools.partial(forward, key_flags), embeddings.astype(jnp.float32), w_query.astype(jnp.float32), w_key.astype(jnp.float32), w_value.astype(jnp.float32), w_out.astype(jnp.float32), w_up.astype(jnp.float32), w_down.astype(jnp.float32), gain_attn.astype(jnp.float32), shift_attn.astype(jnp.float32), gain_mlp.astype(jnp.float32), shift_mlp.astype(jnp.float32))
    grads = pullback(cotangent.astype(jnp.float32))
    return (output.astype(jnp.bfloat16), grads[0], grads[1], grads[2], grads[3], grads[4], grads[5], grads[6], grads[7], grads[8], grads[9], grads[10])
```

```python
import math

import jax
import jax.numpy as jnp
import numpy as np
from jax import lax
from jax.experimental import pallas as pl
from jax.experimental.pallas import tpu as pltpu
from jax.sharding import PartitionSpec as P

HEADS = 16
HEAD_DIM = 48
SLOT = 64
PAIRS = HEADS // 2
STRIDE = 4
WINDOW = 8
ROWS = 8
COLS = 16
TOKENS = ROWS * COLS
N_GX = 32
N_GY = 4
N_DEV = N_GX * N_GY
AXES = ("gx", "gy")
BF = jnp.bfloat16
F32 = jnp.float32
SCALE = 1.0 / math.sqrt(HEAD_DIM)
SCALE_LOG2 = SCALE * math.log2(math.e)
MARK = 1e30
HIDE = -1e30
CHUNK = 128
epsilon = 1e-05

PIECES = ((-1, 0), (1, 0), (0, -1), (0, 1), (-1, -1), (-1, 1), (1, -1), (1, 1))


def nt(left_op, right_op):
    return lax.dot_general(left_op, right_op, (((1,), (1,)), ((), ())), preferred_element_type=F32)


def tn(left_op, right_op):
    return lax.dot_general(left_op, right_op, (((0,), (0,)), ((), ())), preferred_element_type=F32)


def product(left_op, right_op):
    return jnp.dot(left_op, right_op, preferred_element_type=F32)


def coords(flat):
    core, x_hi, z, x_lo, y = flat & 1, (flat >> 1) & 1, (flat >> 2) & 3, (flat >> 4) & 1, flat >> 5
    return (x_hi * 2 + x_lo, y, z, core)


def flat_of(place):
    x, y, z, core = place
    return y * 32 + (x & 1) * 16 + z * 4 + (x >> 1) * 2 + core


def core_pairs():
    return [(i, i ^ 1) for i in range(N_DEV)]


def ring_pairs(order, stage, shift):
    pairs = []
    for i in range(N_DEV):
        place = list(coords(i))
        axis = order[place[3]][stage]
        place[axis] = (place[axis] + shift) % 4
        pairs.append((i, flat_of(place)))
    return pairs


def sent(value, pairs):
    return lax.ppermute(value, AXES, pairs)


def grid_pairs(row_step, col_step):
    pairs = []
    for gx in range(N_GX):
        for gy in range(N_GY):
            sx, sy = gx + col_step, gy + row_step
            if 0 <= sx < N_GX and 0 <= sy < N_GY:
                pairs.append((sx * N_GY + sy, gx * N_GY + gy))
    return pairs


SAME_CORE = [[i for i in range(N_DEV) if i % 2 == core] for core in (0, 1)]
ORDERS = (
    {0: (2, 1, 0), 1: (0, 2, 1)},
    {0: (1, 0, 2), 1: (2, 1, 0)},
    {0: (0, 2, 1), 1: (1, 0, 2)},
)


def total_of(parts):
    total = parts[0].astype(F32)
    for part in parts[1:]:
        total = total + part.astype(F32)
    return total


def all_reduce(array):
    rows, width = array.shape
    third = width // 3
    me = lax.axis_index(AXES)
    x, y, z, core = coords(me)
    place = (x, y, z)
    spots = [
        [jnp.where(core == 0, place[order[0][stage]], place[order[1][stage]]) for stage in range(3)]
        for order in ORDERS
    ]

    def pick(cut, index):
        return lax.dynamic_index_in_dim(cut, index, 0, keepdims=False)

    pieces = []
    for part in range(3):
        order = ORDERS[part]
        held = array[:, part * third : (part + 1) * third].reshape(2, rows // 2, third)
        held = total_of([pick(held, core), sent(pick(held, 1 - core), core_pairs())]).astype(BF)
        for stage in range(3):
            spot = spots[part][stage]
            cut = held.reshape(4, held.shape[0] // 4, third)
            got = [
                sent(pick(cut, (spot + step) % 4), ring_pairs(order, stage, step))
                for step in (2, 1, 3)
            ]
            held = total_of([pick(cut, spot)] + got).astype(BF)
        pieces.append(held)
    for stage in (2, 1, 0):
        for part in range(3):
            order = ORDERS[part]
            spot = spots[part][stage]
            held = pieces[part]
            got = [(step, sent(held, ring_pairs(order, stage, -step))) for step in (2, 1, 3)]
            whole = jnp.zeros((4,) + held.shape, held.dtype)
            for step, piece in [(0, held)] + got:
                whole = lax.dynamic_update_index_in_dim(whole, piece, (spot + step) % 4, 0)
            pieces[part] = whole.reshape(4 * held.shape[0], third)
    outs = []
    for part in range(3):
        held = pieces[part]
        other = sent(held, core_pairs())
        first = jnp.where(core == 0, held, other)
        second = jnp.where(core == 0, other, held)
        outs.append(jnp.concatenate([first, second], axis=0))
    return jnp.concatenate(outs, axis=1)


def gather_far(tokens_far):
    rows, width = tokens_far.shape
    spread = jnp.broadcast_to(tokens_far[None], (N_DEV // 2, rows, width))
    half = lax.all_to_all(spread, AXES, 0, 0, tiled=True, axis_index_groups=SAME_CORE)
    half = half.reshape(N_DEV // 2 * rows, width)
    return jnp.concatenate([half, sent(half, core_pairs())], axis=0)


def scatter_far(grads):
    count, width = grads.shape
    half = count // 2
    mine = total_of([grads[:half], sent(grads[half:], core_pairs())]).astype(BF)
    mine = mine.reshape(N_DEV // 2, half // (N_DEV // 2), width)
    back = lax.all_to_all(mine, AXES, 0, 0, tiled=True, axis_index_groups=SAME_CORE)
    return jnp.sum(back.astype(F32), axis=0)


def halves(block):
    wide = block.astype(F32)
    lane = lax.broadcasted_iota(jnp.int32, wide.shape, 1)
    first = jnp.where(lane < SLOT, wide, 0.0).astype(BF)
    second = jnp.where(lane < SLOT, 0.0, wide).astype(BF)
    return jnp.concatenate([first, second], axis=0)


def own_blocks(wide):
    row = lax.broadcasted_iota(jnp.int32, (2 * SLOT, TOKENS), 0)
    return jnp.where(row < SLOT, wide[:, :TOKENS], wide[:, TOKENS:]).T


def folded(tile, op):
    return op(tile.reshape(tile.shape[0] // 8, 8, tile.shape[1]), axis=0)


def attend_kernel(q_ref, k_ref, vt_ref, bias_ref, o_ref, lse_ref, t_ref, e_ref):
    keys = k_ref.shape[0]
    query_rows = halves(q_ref[...])
    top = jnp.full((8, 2 * TOKENS), HIDE, F32)
    for start in range(0, keys, CHUNK):
        rows = pl.ds(start, CHUNK)
        bias = bias_ref[rows, :]
        tile = nt(k_ref[rows, :], query_rows) * SCALE_LOG2 + jnp.concatenate([bias, bias], axis=1)
        t_ref[rows, :] = tile
        top = jnp.maximum(top, folded(tile, jnp.max))
    top = jnp.max(top, axis=0, keepdims=True)
    total = jnp.zeros((8, 2 * TOKENS), F32)
    for start in range(0, keys, CHUNK):
        rows = pl.ds(start, CHUNK)
        tile = jnp.exp2(t_ref[rows, :] - top)
        total = total + folded(tile, jnp.sum)
        e_ref[rows, :] = tile.astype(BF)
    total = jnp.sum(total, axis=0, keepdims=True)
    wide = jnp.dot(vt_ref[...], e_ref[...], preferred_element_type=F32) / total
    o_ref[...] = own_blocks(wide)
    lse_ref[0] = top + jnp.log2(total)


def attend_back_kernel(
    q_ref, g_ref, o_ref, k_ref, v_ref, kt_ref, bias_ref, lse_ref, gq_ref, gk_ref, gv_ref, s_ref
):
    keys = k_ref.shape[0]
    query_rows = halves(q_ref[...])
    grad_rows = halves(g_ref[...])
    inner = (g_ref[...].astype(F32) * o_ref[...]).T
    inner = jnp.concatenate(
        [
            jnp.sum(inner[:SLOT], axis=0, keepdims=True),
            jnp.sum(inner[SLOT:], axis=0, keepdims=True),
        ],
        axis=1,
    )
    lse = lse_ref[0]
    for start in range(0, keys, CHUNK):
        rows = pl.ds(start, CHUNK)
        bias = bias_ref[rows, :]
        tile = nt(k_ref[rows, :], query_rows) * SCALE_LOG2 + jnp.concatenate([bias, bias], axis=1)
        probs = jnp.exp2(tile - lse)
        grad_probs = nt(v_ref[rows, :], grad_rows)
        grad_scores = (probs * (grad_probs - inner)).astype(BF)
        s_ref[rows, :] = grad_scores
        gv_ref[rows, :] = jnp.dot(
            probs.astype(BF), grad_rows, preferred_element_type=F32
        ).astype(BF)
        gk_ref[rows, :] = (
            jnp.dot(grad_scores, query_rows, preferred_element_type=F32) * SCALE
        ).astype(BF)
    wide = jnp.dot(kt_ref[...], s_ref[...], preferred_element_type=F32) * SCALE
    gq_ref[...] = own_blocks(wide).astype(BF)


def rows_spec(count):
    return pl.BlockSpec((count, 2 * SLOT), lambda p: (0, p))


def cols_spec(count):
    return pl.BlockSpec((2 * SLOT, count), lambda p: (p, 0))


def attend(queries, keys, values_t, bias):
    count = keys.shape[0]
    return pl.pallas_call(
        attend_kernel,
        grid=(PAIRS,),
        in_specs=[
            rows_spec(TOKENS),
            rows_spec(count),
            cols_spec(count),
            pl.BlockSpec((count, TOKENS), lambda p: (0, 0)),
        ],
        out_specs=[rows_spec(TOKENS), pl.BlockSpec((1, 1, 2 * TOKENS), lambda p: (p, 0, 0))],
        out_shape=[
            jax.ShapeDtypeStruct((TOKENS, HEADS * SLOT), F32),
            jax.ShapeDtypeStruct((PAIRS, 1, 2 * TOKENS), F32),
        ],
        scratch_shapes=[
            pltpu.VMEM((count, 2 * TOKENS), F32),
            pltpu.VMEM((count, 2 * TOKENS), BF),
        ],
        compiler_params=pltpu.CompilerParams(vmem_limit_bytes=32 * 1024 * 1024),
        cost_estimate=pl.CostEstimate(
            flops=4 * PAIRS * count * 256 * 128,
            bytes_accessed=6 * count * HEADS * SLOT,
            transcendentals=HEADS * count * TOKENS,
        ),
        name="attend",
    )(queries, keys, values_t, bias)


def attend_back(queries, grads, outs, keys, values, keys_t, bias, lse):
    count = keys.shape[0]
    return pl.pallas_call(
        attend_back_kernel,
        grid=(PAIRS,),
        in_specs=[
            rows_spec(TOKENS),
            rows_spec(TOKENS),
            rows_spec(TOKENS),
            rows_spec(count),
            rows_spec(count),
            cols_spec(count),
            pl.BlockSpec((count, TOKENS), lambda p: (0, 0)),
            pl.BlockSpec((1, 1, 2 * TOKENS), lambda p: (p, 0, 0)),
        ],
        out_specs=[rows_spec(TOKENS), rows_spec(count), rows_spec(count)],
        out_shape=[
            jax.ShapeDtypeStruct((TOKENS, HEADS * SLOT), BF),
            jax.ShapeDtypeStruct((count, HEADS * SLOT), BF),
            jax.ShapeDtypeStruct((count, HEADS * SLOT), BF),
        ],
        scratch_shapes=[pltpu.VMEM((count, 2 * TOKENS), BF)],
        compiler_params=pltpu.CompilerParams(vmem_limit_bytes=32 * 1024 * 1024),
        cost_estimate=pl.CostEstimate(
            flops=10 * PAIRS * count * 256 * 128,
            bytes_accessed=10 * count * HEADS * SLOT,
            transcendentals=HEADS * count * TOKENS,
        ),
        name="attend_back",
    )(queries, grads, outs, keys, values, keys_t, bias, lse)


def layer_norm(inputs, gain_vec, shift_vec):
    row_mean = jnp.mean(inputs, axis=-1, keepdims=True)
    centered = inputs - row_mean
    row_var = jnp.mean(centered * centered, axis=-1, keepdims=True)
    return centered * lax.rsqrt(row_var + epsilon) * gain_vec + shift_vec


def exact_gelu(inputs):
    return jax.nn.gelu(inputs, approximate=False)


def padded_cols(weight):
    width = weight.shape[0]
    cut = weight.reshape(width, HEADS, HEAD_DIM)
    return jnp.pad(cut, ((0, 0), (0, 0), (0, SLOT - HEAD_DIM))).reshape(width, HEADS * SLOT)


def padded_rows(weight):
    width = weight.shape[1]
    cut = weight.reshape(HEADS, HEAD_DIM, width)
    return jnp.pad(cut, ((0, 0), (0, SLOT - HEAD_DIM), (0, 0))).reshape(HEADS * SLOT, width)


def real_rows(weight):
    width = weight.shape[1]
    return weight.reshape(HEADS, SLOT, width)[:, :HEAD_DIM].reshape(HEADS * HEAD_DIM, width)


def piece_of(block, row_step, col_step):
    if col_step == 0:
        return block
    return block[:, WINDOW:] if col_step < 0 else block[:, : COLS - WINDOW]


def window_weights():
    rows, cols = np.mgrid[0:ROWS, 0:COLS]
    query = (rows.reshape(-1), cols.reshape(-1))
    key_rows, key_cols = [rows.reshape(-1)], [cols.reshape(-1)]
    for row_step, col_step in PIECES:
        key_rows.append(piece_of(rows, row_step, col_step).reshape(-1) + row_step * ROWS)
        key_cols.append(piece_of(cols, row_step, col_step).reshape(-1) + col_step * COLS)
    row_gap = np.concatenate(key_rows)[:, None] - query[0][None]
    col_gap = np.concatenate(key_cols)[:, None] - query[1][None]
    dense = (np.abs(row_gap) <= WINDOW) & (np.abs(col_gap) <= WINDOW)
    dilated = dense & (row_gap % 2 == 0) & (col_gap % 2 == 0)
    itself = (row_gap == 0) & (col_gap == 0)
    return np.where(dense, np.where(dilated, 1.0, 0.0), HIDE).astype(np.float32), itself


def local(
    embeddings,
    tile_valid,
    w_query,
    w_key,
    w_value,
    w_out,
    w_up,
    w_down,
    gain_attn,
    shift_attn,
    gain_mlp,
    shift_mlp,
    cotangent,
):
    width = embeddings.shape[-1]
    gx, gy = lax.axis_index("gx"), lax.axis_index("gy")
    residual = embeddings.astype(F32).reshape(TOKENS, width)
    normed_attn, attn_norm_back = jax.vjp(layer_norm, residual, gain_attn, shift_attn)
    act_attn = normed_attn.astype(BF)

    own_flags = tile_valid.reshape(TOKENS, 1) > 0
    marked = jnp.where(own_flags, act_attn, jnp.asarray(MARK, BF)).reshape(ROWS, COLS, width)
    far_got = gather_far(marked[::STRIDE, ::STRIDE].reshape(-1, width))
    pieces = []
    exists = [jnp.ones((TOKENS,), jnp.bool_)]
    for row_step, col_step in PIECES:
        piece = sent(piece_of(marked, row_step, col_step), grid_pairs(row_step, col_step))
        piece = piece.reshape(-1, width)
        there = (
            (gy + row_step >= 0)
            & (gy + row_step < N_GY)
            & (gx + col_step >= 0)
            & (gx + col_step < N_GX)
        )
        exists.append(jnp.broadcast_to(there, (piece.shape[0],)))
        pieces.append(piece)
    near_got = jnp.concatenate(pieces, axis=0)
    limit = jnp.asarray(MARK / 2, BF)
    got = jnp.concatenate([near_got, far_got], axis=0)
    got_valid = got[:, :1] < limit
    act_all = jnp.concatenate([act_attn, jnp.where(got < limit, got, jnp.zeros_like(got))], axis=0)
    near_count = TOKENS + near_got.shape[0]
    far_count = far_got.shape[0]

    flags = jnp.concatenate([own_flags, got_valid], axis=0)
    flags = flags & jnp.concatenate(exists + [jnp.ones((far_count,), jnp.bool_)])[:, None]
    log_weight, itself = window_weights()
    near_bias = jnp.where(flags[:near_count] | itself, log_weight, HIDE)
    far_bias = jnp.broadcast_to(jnp.where(flags[near_count:], 0.0, HIDE), (far_count, TOKENS))
    bias = jnp.concatenate([near_bias, far_bias], axis=0).astype(F32)

    wq, wk, wv = padded_cols(w_query), padded_cols(w_key), padded_cols(w_value)
    wo = padded_rows(w_out)
    queries = product(act_attn, wq).astype(BF)
    keys = product(act_all, wk).astype(BF)
    values = product(act_all, wv).astype(BF)
    keys_t, values_t = keys.T, values.T

    outs, lse = attend(queries, keys, values_t, bias)
    attended = outs.astype(BF)
    middle = residual + product(attended, wo)
    normed_mlp, mlp_norm_back = jax.vjp(layer_norm, middle, gain_mlp, shift_mlp)
    act_mlp = normed_mlp.astype(BF)
    pre_act = product(act_mlp, w_up)
    gelu_out, gelu_back = jax.vjp(exact_gelu, pre_act)
    hidden = gelu_out.astype(BF)
    output = middle + product(hidden, w_down)

    grad_out = cotangent.reshape(TOKENS, width)
    grad_down = tn(hidden, grad_out)
    grad_pre = gelu_back(nt(grad_out, w_down))[0].astype(BF)
    grad_up = tn(act_mlp, grad_pre)
    grad_up, grad_down = lax.psum((grad_up.astype(BF), grad_down.astype(BF)), AXES)

    grad_act_mlp = nt(grad_pre, w_up)
    grad_mid_norm, grad_gain_mlp, grad_shift_mlp = mlp_norm_back(grad_act_mlp)
    grad_mid = grad_out.astype(F32) + grad_mid_norm
    grad_branch = grad_mid.astype(BF)
    grad_wout = tn(attended, grad_branch)
    grad_att = nt(grad_branch, wo).astype(BF)

    grad_query, grad_keys, grad_values = attend_back(
        queries, grad_att, outs, keys, values, keys_t, bias, lse
    )
    grad_act_all = nt(grad_keys, wk) + nt(grad_values, wv)
    far_back = scatter_far(grad_act_all[near_count:].astype(BF))
    near_back = grad_act_all[TOKENS:near_count].astype(BF)

    grad_act = nt(grad_query, wq) + grad_act_all[:TOKENS]
    grad_act = grad_act.reshape(ROWS, COLS, width)
    grad_act = grad_act + lax.pad(
        far_back.reshape(ROWS // STRIDE, COLS // STRIDE, width),
        jnp.zeros((), F32),
        ((0, STRIDE - 1, STRIDE - 1), (0, STRIDE - 1, STRIDE - 1), (0, 0, 0)),
    )
    sides = {-1: jnp.zeros((ROWS, WINDOW, width), F32), 1: jnp.zeros((ROWS, WINDOW, width), F32)}
    start = 0
    for row_step, col_step in PIECES:
        count = TOKENS if col_step == 0 else TOKENS // 2
        back = sent(near_back[start : start + count], grid_pairs(-row_step, -col_step))
        start += count
        if col_step == 0:
            grad_act = grad_act + back.astype(F32).reshape(ROWS, COLS, width)
        else:
            sides[col_step] = sides[col_step] + back.astype(F32).reshape(ROWS, WINDOW, width)
    grad_act = grad_act + jnp.concatenate([sides[1], sides[-1]], axis=1)
    grad_in_norm, grad_gain_attn, grad_shift_attn = attn_norm_back(grad_act.reshape(TOKENS, width))
    grad_inputs = grad_mid + grad_in_norm

    small = jnp.stack([grad_gain_attn, grad_shift_attn, grad_gain_mlp, grad_shift_mlp])
    small = lax.psum(small, AXES)
    stacked = jnp.concatenate(
        [
            grad_wout_rows.astype(BF)
            for grad_wout_rows in (
                real_rows(grad_wout),
                real_rows(tn(grad_query, act_attn)),
                real_rows(tn(grad_keys, act_all)),
                real_rows(tn(grad_values, act_all)),
            )
        ],
        axis=0,
    )
    summed = all_reduce(stacked).astype(F32).reshape(4, width, width)
    mixed = output.astype(BF).reshape(ROWS, COLS, width)
    return (
        mixed,
        grad_inputs.reshape(ROWS, COLS, width),
        summed[1].T,
        summed[2].T,
        summed[3].T,
        summed[0],
        grad_up.astype(F32),
        grad_down.astype(F32),
        small[0],
        small[1],
        small[2],
        small[3],
    )


def solution(mesh):
    grid = P("gy", "gx", None)
    in_specs = (grid, P("gy", "gx")) + (P(),) * 10 + (grid,)
    out_specs = (grid, grid) + (P(),) * 10
    return jax.shard_map(local, mesh=mesh, in_specs=in_specs, out_specs=out_specs, check_vma=False)
```

```python
import math

import jax
import jax.numpy as jnp
import numpy as np
from jax import lax
from jax.experimental import pallas as pl
from jax.experimental.pallas import tpu as pltpu
from jax.sharding import PartitionSpec as P

HEADS = 16
HEAD_DIM = 48
PAIRS = HEADS // 2
PAIR = 2 * HEAD_DIM
VIEW = 256
STRIDE = 4
WINDOW = 8
ROWS = 8
COLS = 16
TOKENS = ROWS * COLS
WIDTH = 768
HIDDEN = 3072
N_GX = 32
N_GY = 4
N_DEV = N_GX * N_GY
GROUP = N_DEV // 2
AXES = ("gx", "gy")
BF = jnp.bfloat16
F32 = jnp.float32
SCALE = 1.0 / math.sqrt(HEAD_DIM)
SCALE_LOG2 = SCALE * math.log2(math.e)
MARK = 1e30
LIMIT = 1e29
HIDE = -1e30
CHUNK = 256
MLP_CHUNK = 512
epsilon = 1e-05

PIECES = ((0, -1), (0, 1), (-1, 0), (-1, -1), (-1, 1), (1, 0), (1, -1), (1, 1))
SIZES = [TOKENS if col_step == 0 else TOKENS // 2 for _, col_step in PIECES]
STARTS = [TOKENS + sum(SIZES[:i]) for i in range(len(SIZES))]
NEAR = TOKENS + sum(SIZES)
SIDE = TOKENS // 2
BAND = TOKENS + 2 * SIDE
MOVED = (SIDE, SIDE, BAND, BAND)
MOVED_STARTS = [TOKENS + sum(MOVED[:i]) for i in range(4)]
FAR_OWN = (ROWS // STRIDE) * (COLS // STRIDE)
FAR_HALF = GROUP * FAR_OWN
FAR = 2 * FAR_HALF
FAR_ROWS = [COLS * STRIDE * r + STRIDE * c for r in range(ROWS // STRIDE) for c in range(COLS // STRIDE)]
HALF = 2 * WIDTH


def nt(left_op, right_op):
    return lax.dot_general(left_op, right_op, (((1,), (1,)), ((), ())), preferred_element_type=F32)


def tn(left_op, right_op):
    return lax.dot_general(left_op, right_op, (((0,), (0,)), ((), ())), preferred_element_type=F32)


def product(left_op, right_op):
    return jnp.dot(left_op, right_op, preferred_element_type=F32)


CORE_PAIRS = [(i, i ^ 1) for i in range(N_DEV)]
SAME_CORE = [[i for i in range(N_DEV) if i % 2 == core] for core in (0, 1)]


def sent(value, pairs):
    return lax.ppermute(value, AXES, pairs)


def grid_pairs(row_step, col_step):
    pairs = []
    for gx in range(N_GX):
        for gy in range(N_GY):
            sx, sy = gx + col_step, gy + row_step
            if 0 <= sx < N_GX and 0 <= sy < N_GY:
                pairs.append((sx * N_GY + sy, gx * N_GY + gy))
    return pairs


def exchanged(cells):
    return lax.all_to_all(cells, AXES, 0, 0, tiled=True, axis_index_groups=SAME_CORE)


def coords(flat):
    core, x_hi, z, x_lo, y = flat & 1, (flat >> 1) & 1, (flat >> 2) & 3, (flat >> 4) & 1, flat >> 5
    return (x_hi * 2 + x_lo, y, z, core)


def flat_of(place):
    x, y, z, core = place
    return y * 32 + (x & 1) * 16 + z * 4 + (x >> 1) * 2 + core


ORDER = {0: (2, 1, 0), 1: (0, 2, 1)}


def ring_pairs(stage, shift):
    pairs = []
    for i in range(N_DEV):
        place = list(coords(i))
        axis = ORDER[place[3]][stage]
        place[axis] = (place[axis] + shift) % 4
        pairs.append((i, flat_of(place)))
    return pairs


WHOLE = pl.BlockSpec(memory_space=pltpu.VMEM)
SCALARS = pl.BlockSpec(memory_space=pltpu.SMEM)


def params(mebibytes):
    return pltpu.CompilerParams(vmem_limit_bytes=mebibytes * 1024 * 1024)


def shape(*dims_and_type):
    return jax.ShapeDtypeStruct(dims_and_type[:-1], dims_and_type[-1])


def fixed(*dims):
    return pl.BlockSpec(dims, lambda p: (0,) * len(dims))


def lanes(rows, cols):
    return pl.BlockSpec((rows, cols), lambda p: (0, p))


def sublanes(rows, cols):
    return pl.BlockSpec((rows, cols), lambda p: (p, 0))


def normalized(inputs):
    centered = inputs - jnp.mean(inputs, axis=1, keepdims=True)
    scale = lax.rsqrt(jnp.mean(centered * centered, axis=1, keepdims=True) + epsilon)
    return centered * scale, scale


def norm_back(grads, xhat, scale, gain):
    scaled = grads * gain
    inputs = scale * (
        scaled
        - jnp.mean(scaled, axis=1, keepdims=True)
        - xhat * jnp.mean(scaled * xhat, axis=1, keepdims=True)
    )
    return (
        inputs,
        jnp.sum(grads * xhat, axis=0, keepdims=True),
        jnp.sum(grads, axis=0, keepdims=True),
    )


def flag_column(flag_ref):
    row = lax.broadcasted_iota(jnp.int32, (TOKENS, ROWS), 0) // COLS
    block = lax.broadcasted_iota(jnp.int32, (TOKENS, ROWS), 1)
    rows = product(jnp.where(row == block, 1.0, 0.0).astype(BF), flag_ref[...].astype(F32).astype(BF))
    token = lax.broadcasted_iota(jnp.int32, (TOKENS, COLS), 0) % COLS
    col = lax.broadcasted_iota(jnp.int32, (TOKENS, COLS), 1)
    return jnp.sum(jnp.where(token == col, rows, 0.0), axis=1, keepdims=True)


def pre_kernel(
    x_ref, flag_ref, gain_ref, shift_ref, act_ref, marked_ref, left_ref, right_ref, far_ref
):
    xhat, _ = normalized(x_ref[...].astype(F32))
    act = (xhat * gain_ref[...] + shift_ref[...]).astype(BF)
    act_ref[...] = act
    flag = flag_column(flag_ref)
    marked = jnp.where(flag > 0.5, act.astype(F32), MARK)
    marked_ref[...] = marked.astype(BF)
    sides = [
        jnp.concatenate(
            [marked[COLS * r + side : COLS * r + side + WINDOW] for r in range(ROWS)], axis=0
        ).astype(BF)
        for side in (0, WINDOW)
    ]
    left_ref[...] = sides[0]
    right_ref[...] = sides[1]
    number = lax.broadcasted_iota(jnp.int32, (2 * FAR_OWN, TOKENS), 0) % FAR_OWN
    token = lax.broadcasted_iota(jnp.int32, (2 * FAR_OWN, TOKENS), 1)
    wanted = number // STRIDE * (COLS * STRIDE) + number % STRIDE * STRIDE
    chosen = product(
        jnp.where(token == wanted, 1.0, 0.0).astype(BF), marked.astype(BF)
    ).astype(BF)
    for k in range(GROUP // 2):
        far_ref[2 * FAR_OWN * k : 2 * FAR_OWN * (k + 1), :] = chosen


def pre(embeddings, flags, gain, shift):
    return pl.pallas_call(
        pre_kernel,
        in_specs=[WHOLE] * 4,
        out_specs=[WHOLE] * 5,
        out_shape=[
            shape(TOKENS, WIDTH, BF),
            shape(TOKENS, WIDTH, BF),
            shape(TOKENS // 2, WIDTH, BF),
            shape(TOKENS // 2, WIDTH, BF),
            shape(FAR_HALF, WIDTH, BF),
        ],
        compiler_params=params(32),
        cost_estimate=pl.CostEstimate(
            flops=2_000_000, bytes_accessed=2_000_000, transcendentals=TOKENS
        ),
        name="pre",
    )(embeddings, flags, gain, shift)


def view_of(pair):
    start = jnp.minimum(pair * PAIR // 128 * 128, WIDTH - VIEW)
    return pl.ds(pl.multiple_of(start, 128), VIEW), pair * PAIR - start


def halves(block, begin):
    wide = block.astype(F32)
    lane = lax.broadcasted_iota(jnp.int32, wide.shape, 1) - begin
    first = jnp.where((lane >= 0) & (lane < HEAD_DIM), wide, 0.0).astype(BF)
    second = jnp.where((lane >= HEAD_DIM) & (lane < PAIR), wide, 0.0).astype(BF)
    return jnp.concatenate([first, second], axis=0)


def own_rows(wide):
    return jnp.concatenate([wide[:HEAD_DIM, :TOKENS], wide[HEAD_DIM:, TOKENS:]], axis=0)


def rows_of(pair):
    return pl.ds(pl.multiple_of(pair * PAIR, 32), PAIR)


def folded(tile, op):
    return op(tile.reshape(tile.shape[0] // 8, 8, tile.shape[1]), axis=0)


def attended_part(query_rows, k_ref, flip, view, bias_ref, t_ref, e_ref):
    count = k_ref.shape[0]
    top = jnp.full((8, 2 * TOKENS), HIDE, F32)
    for start in range(0, count, CHUNK):
        rows = pl.ds(start, CHUNK)
        bias = bias_ref[rows, :]
        tile = nt(k_ref[rows, view], query_rows) * SCALE_LOG2
        tile = tile + jnp.concatenate([bias, bias], axis=1)
        t_ref[rows, :] = tile
        top = jnp.maximum(top, folded(tile, jnp.max))
    top = jnp.max(top, axis=0, keepdims=True)
    total = jnp.zeros((8, 2 * TOKENS), F32)
    for start in range(0, count, CHUNK):
        rows = pl.ds(start, CHUNK)
        tile = jnp.exp2(t_ref[rows, :] - top)
        total = total + folded(tile, jnp.sum)
        e_ref[rows, :] = tile.astype(BF)
    total = jnp.sum(total, axis=0, keepdims=True)
    return top, total, own_rows(product(flip, e_ref[...]))


def near_kernel(
    exists_ref, act_ref, l_ref, r_ref, u_ref, d_ref, flag_ref, log_ref, wq_ref, wk_ref, wv_ref,
    all_ref, bias_ref, q_ref, k_ref, v_ref, top_ref, total_ref, sum_ref, t_ref, p_ref, flip_ref,
):
    pair = pl.program_id(0)

    @pl.when(pair == 0)
    def _():
        all_ref[:TOKENS, :] = act_ref[...]
        row = lax.broadcasted_iota(jnp.int32, (TOKENS, TOKENS), 0)
        col = lax.broadcasted_iota(jnp.int32, (TOKENS, TOKENS), 1)
        seen = jnp.where(row == col, 1.0, flag_column(flag_ref))
        bias_ref[:TOKENS, :] = jnp.where(seen > 0.5, log_ref[:TOKENS, :], HIDE)
        for i, (start, size) in enumerate(zip(STARTS, SIZES, strict=True)):
            rows = slice(start, start + size)
            moved = max(m for m in range(4) if MOVED_STARTS[m] <= start)
            begin = start - MOVED_STARTS[moved]
            piece = (l_ref, r_ref, u_ref, d_ref)[moved][begin : begin + size, :].astype(F32)
            all_ref[rows, :] = jnp.where(piece < LIMIT, piece, 0.0).astype(BF)
            seen = jnp.where(piece[:, :128] < LIMIT, 1.0, 0.0)[:, :1] * exists_ref[i]
            bias_ref[rows, :] = jnp.where(seen > 0.5, log_ref[rows, :], HIDE)
        q_ref[...] = product(act_ref[...], wq_ref[...]).astype(BF)
        k_ref[...] = product(all_ref[...], wk_ref[...]).astype(BF)
        values = product(all_ref[...], wv_ref[...]).astype(BF)
        v_ref[...] = values
        flip_ref[...] = values.T

    view, begin = view_of(pair)
    top, total, wide = attended_part(
        halves(q_ref[:, view], begin), k_ref, flip_ref[rows_of(pair), :], view, bias_ref, t_ref, p_ref
    )
    top_ref[pair] = top
    total_ref[pair] = total
    sum_ref[pair] = wide


def attend_near(exists, act, pieces, flags, log_weight, wq, wk, wv):
    return pl.pallas_call(
        near_kernel,
        grid=(PAIRS,),
        in_specs=[SCALARS] + [WHOLE] * 10,
        out_specs=[WHOLE] * 8,
        out_shape=[
            shape(NEAR, WIDTH, BF),
            shape(NEAR, TOKENS, F32),
            shape(TOKENS, WIDTH, BF),
            shape(NEAR, WIDTH, BF),
            shape(NEAR, WIDTH, BF),
            shape(PAIRS, 1, 2 * TOKENS, F32),
            shape(PAIRS, 1, 2 * TOKENS, F32),
            shape(PAIRS, PAIR, TOKENS, F32),
        ],
        scratch_shapes=[
            pltpu.VMEM((NEAR, 2 * TOKENS), F32),
            pltpu.VMEM((NEAR, 2 * TOKENS), BF),
            pltpu.VMEM((WIDTH, NEAR), BF),
        ],
        compiler_params=params(40),
        cost_estimate=pl.CostEstimate(
            flops=10_000_000_000, bytes_accessed=12_000_000, transcendentals=HEADS * NEAR * TOKENS
        ),
        name="attend_near",
    )(exists, act, *pieces, flags, log_weight, wq, wk, wv)


def far_kernel(
    own_ref, other_ref, x_ref, q_ref, wk_ref, wv_ref, wo_ref, top_ref, total_ref, sum_ref,
    all_ref, bias_ref, k_ref, v_ref, o_ref, lse_ref, mid_ref, t_ref, e_ref, flip_ref, out_ref,
):
    pair = pl.program_id(0)

    @pl.when(pair == 0)
    def _():
        for start, half_ref in ((0, own_ref), (FAR_HALF, other_ref)):
            rows = slice(start, start + FAR_HALF)
            piece = half_ref[...].astype(F32)
            all_ref[rows, :] = jnp.where(piece < LIMIT, piece, 0.0).astype(BF)
            seen = jnp.where(piece[:, :128] < LIMIT, 0.0, HIDE)[:, :1]
            bias_ref[rows, :] = jnp.broadcast_to(seen, (FAR_HALF, TOKENS))
        k_ref[...] = product(all_ref[...], wk_ref[...]).astype(BF)
        values = product(all_ref[...], wv_ref[...]).astype(BF)
        v_ref[...] = values
        flip_ref[...] = values.T

    view, begin = view_of(pair)
    far_top, far_total, far_sum = attended_part(
        halves(q_ref[:, view], begin), k_ref, flip_ref[rows_of(pair), :], view, bias_ref, t_ref, e_ref
    )
    near_top = top_ref[pair]
    top = jnp.maximum(near_top, far_top)
    near_part, far_part = jnp.exp2(near_top - top), jnp.exp2(far_top - top)
    total = total_ref[pair] * near_part + far_total * far_part
    near_part, far_part = near_part / total, far_part / total
    near_sum = sum_ref[pair]
    out_ref[rows_of(pair), :] = jnp.concatenate(
        [
            near_sum[rows] * near_part[:, cols] + far_sum[rows] * far_part[:, cols]
            for rows, cols in (
                (slice(0, HEAD_DIM), slice(0, TOKENS)),
                (slice(HEAD_DIM, PAIR), slice(TOKENS, 2 * TOKENS)),
            )
        ],
        axis=0,
    )
    lse_ref[pair] = top + jnp.log2(total)

    @pl.when(pair == PAIRS - 1)
    def _():
        outs = out_ref[...].T
        o_ref[...] = outs
        mid_ref[...] = x_ref[...].astype(F32) + product(outs.astype(BF), wo_ref[...])


def attend_far(own, other, embeddings, queries, wk, wv, wo, tops, totals, sums):
    return pl.pallas_call(
        far_kernel,
        grid=(PAIRS,),
        in_specs=[WHOLE] * 10,
        out_specs=[WHOLE] * 7,
        out_shape=[
            shape(FAR, WIDTH, BF),
            shape(FAR, TOKENS, F32),
            shape(FAR, WIDTH, BF),
            shape(FAR, WIDTH, BF),
            shape(TOKENS, WIDTH, F32),
            shape(PAIRS, 1, 2 * TOKENS, F32),
            shape(TOKENS, WIDTH, F32),
        ],
        scratch_shapes=[
            pltpu.VMEM((FAR, 2 * TOKENS), F32),
            pltpu.VMEM((FAR, 2 * TOKENS), BF),
            pltpu.VMEM((WIDTH, FAR), BF),
            pltpu.VMEM((WIDTH, TOKENS), F32),
        ],
        compiler_params=params(40),
        cost_estimate=pl.CostEstimate(
            flops=12_000_000_000, bytes_accessed=12_000_000, transcendentals=HEADS * FAR * TOKENS
        ),
        name="attend_far",
    )(own, other, embeddings, queries, wk, wv, wo, tops, totals, sums)


def mlp_kernel(
    mid_ref, gain_ref, shift_ref, gout_ref, wup_ref, wdown_ref, mixed_ref, gup_ref, gdown_ref,
    gact_ref, act_ref, acc_ref,
):
    step = pl.program_id(0)

    @pl.when(step == 0)
    def _():
        middle = mid_ref[...]
        xhat, _ = normalized(middle)
        act_ref[...] = (xhat * gain_ref[...] + shift_ref[...]).astype(BF)
        acc_ref[...] = middle
        gact_ref[...] = jnp.zeros_like(gact_ref)

    act = act_ref[...]
    grad_out = gout_ref[...]
    pre_act = product(act, wup_ref[...])
    below = 0.5 * (1.0 + lax.erf(pre_act * math.sqrt(0.5)))
    slope = below + pre_act * (jnp.exp(-0.5 * pre_act * pre_act) * (1.0 / math.sqrt(2.0 * math.pi)))
    hidden = (pre_act * below).astype(BF)
    grad_pre = (nt(grad_out, wdown_ref[...]) * slope).astype(BF)
    acc_ref[...] += product(hidden, wdown_ref[...])
    gact_ref[...] += nt(grad_pre, wup_ref[...])
    gup_ref[...] = tn(act, grad_pre).astype(BF)
    gdown_ref[...] = tn(hidden, grad_out).astype(BF)

    @pl.when(step == pl.num_programs(0) - 1)
    def _():
        mixed_ref[...] = acc_ref[...].astype(BF)


def mlp(middle, gain, shift, grad_out, w_up, w_down):
    return pl.pallas_call(
        mlp_kernel,
        grid=(HIDDEN // MLP_CHUNK,),
        in_specs=[
            fixed(TOKENS, WIDTH),
            fixed(1, WIDTH),
            fixed(1, WIDTH),
            fixed(TOKENS, WIDTH),
            lanes(WIDTH, MLP_CHUNK),
            sublanes(MLP_CHUNK, WIDTH),
        ],
        out_specs=[
            fixed(TOKENS, WIDTH),
            lanes(WIDTH, MLP_CHUNK),
            sublanes(MLP_CHUNK, WIDTH),
            fixed(TOKENS, WIDTH),
        ],
        out_shape=[
            shape(TOKENS, WIDTH, BF),
            shape(WIDTH, HIDDEN, BF),
            shape(HIDDEN, WIDTH, BF),
            shape(TOKENS, WIDTH, F32),
        ],
        scratch_shapes=[pltpu.VMEM((TOKENS, WIDTH), BF), pltpu.VMEM((TOKENS, WIDTH), F32)],
        compiler_params=params(60),
        cost_estimate=pl.CostEstimate(
            flops=12 * TOKENS * WIDTH * HIDDEN,
            bytes_accessed=22_000_000,
            transcendentals=2 * TOKENS * HIDDEN,
        ),
        name="mlp",
    )(middle, gain, shift, grad_out, w_up, w_down)


def back_kernel(
    q_ref, o_ref, lse_ref, mid_ref, gact_ref, gain_ref, gout_ref, kn_ref, vn_ref, kf_ref, vf_ref,
    biasn_ref, biasf_ref, alln_ref, allf_ref, wq_ref, wk_ref, wv_ref, wo_ref,
    gwq_ref, gwk_ref, gwv_ref, gwo_ref, gmid_ref, small_ref, gown_ref, l_ref, r_ref, u_ref, d_ref,
    keep_ref, send_ref, s_ref, p_ref, gatt_ref, inner_ref, gq_ref, gk_ref, gv_ref, acc_ref,
    flip_ref, kflip_ref,
):
    pair = pl.program_id(0)

    @pl.when(pair == 0)
    def _():
        xhat, scale = normalized(mid_ref[...])
        inputs, grad_gain, grad_shift = norm_back(gact_ref[...], xhat, scale, gain_ref[...])
        grad_mid = gout_ref[...].astype(F32) + inputs
        gmid_ref[...] = grad_mid
        small_ref[...] = jnp.concatenate(
            [grad_gain, grad_shift, jnp.zeros((6, WIDTH), F32)], axis=0
        )
        branch = grad_mid.astype(BF)
        grads = nt(branch, wo_ref[...]).astype(BF)
        gatt_ref[...] = grads
        gwo_ref[...] = tn(o_ref[...].astype(BF), branch).astype(BF)
        inner_ref[...] = (grads.astype(F32) * o_ref[...]).T
        flip_ref[:, :NEAR] = alln_ref[...].T
        flip_ref[:, NEAR:] = allf_ref[...].T
        kflip_ref[:, :NEAR] = kn_ref[...].T
        kflip_ref[:, NEAR:] = kf_ref[...].T
        gk_ref[...] = jnp.zeros_like(gk_ref)
        gv_ref[...] = jnp.zeros_like(gv_ref)

    view, begin = view_of(pair)
    query_rows = halves(q_ref[:, view], begin)
    grad_rows = halves(gatt_ref[:, view], begin)
    inner = inner_ref[rows_of(pair), :]
    inner = jnp.concatenate(
        [
            jnp.sum(inner[:HEAD_DIM], axis=0, keepdims=True),
            jnp.sum(inner[HEAD_DIM:], axis=0, keepdims=True),
        ],
        axis=1,
    )
    lse = lse_ref[pair]
    for k_ref, v_ref, bias_ref, offset in (
        (kn_ref, vn_ref, biasn_ref, 0),
        (kf_ref, vf_ref, biasf_ref, NEAR),
    ):
        for start in range(0, k_ref.shape[0], CHUNK):
            rows = pl.ds(start, CHUNK)
            bias = bias_ref[rows, :]
            tile = nt(k_ref[rows, view], query_rows) * SCALE_LOG2
            probs = jnp.exp2(tile + jnp.concatenate([bias, bias], axis=1) - lse)
            grad_probs = nt(v_ref[rows, view], grad_rows)
            there = pl.ds(offset + start, CHUNK)
            s_ref[there, :] = (probs * (grad_probs - inner)).astype(BF)
            p_ref[there, :] = probs.astype(BF)
    gk_ref[:, view] += (product(s_ref[...], query_rows) * SCALE).astype(BF)
    gv_ref[:, view] += product(p_ref[...], grad_rows).astype(BF)
    gq_ref[rows_of(pair), :] = own_rows(product(kflip_ref[rows_of(pair), :], s_ref[...])) * SCALE

    @pl.when(pair == PAIRS - 1)
    def _():
        grad_query = gq_ref[...].T.astype(BF)
        acc_ref[...] = nt(gk_ref[...], wk_ref[...])
        acc_ref[...] += nt(gv_ref[...], wv_ref[...])
        gown_ref[...] = acc_ref[:TOKENS, :] + nt(grad_query, wq_ref[...])
        for piece_ref, start, size in zip(
            (l_ref, r_ref, u_ref, d_ref), MOVED_STARTS, MOVED, strict=True
        ):
            piece_ref[...] = acc_ref[start : start + size, :].astype(BF)
        keep_ref[...] = acc_ref[NEAR : NEAR + FAR_HALF, :].astype(BF)
        send_ref[...] = acc_ref[NEAR + FAR_HALF :, :].astype(BF)
        gwk_ref[...] = product(flip_ref[...], gk_ref[...]).astype(BF)
        gwv_ref[...] = product(flip_ref[...], gv_ref[...]).astype(BF)
        gwq_ref[...] = product(flip_ref[:, :TOKENS], grad_query).astype(BF)


def attend_back(arrays):
    count = NEAR + FAR
    return pl.pallas_call(
        back_kernel,
        grid=(PAIRS,),
        in_specs=[WHOLE] * 19,
        out_specs=[WHOLE] * 13,
        out_shape=[shape(WIDTH, WIDTH, BF)] * 4
        + [shape(TOKENS, WIDTH, F32), shape(8, WIDTH, F32), shape(TOKENS, WIDTH, F32)]
        + [shape(size, WIDTH, BF) for size in MOVED]
        + [shape(FAR_HALF, WIDTH, BF)] * 2,
        scratch_shapes=[
            pltpu.VMEM((count, 2 * TOKENS), BF),
            pltpu.VMEM((count, 2 * TOKENS), BF),
            pltpu.VMEM((TOKENS, WIDTH), BF),
            pltpu.VMEM((WIDTH, TOKENS), F32),
            pltpu.VMEM((WIDTH, TOKENS), F32),
            pltpu.VMEM((count, WIDTH), BF),
            pltpu.VMEM((count, WIDTH), BF),
            pltpu.VMEM((count, WIDTH), F32),
            pltpu.VMEM((WIDTH, count), BF),
            pltpu.VMEM((WIDTH, count), BF),
        ],
        compiler_params=params(56),
        cost_estimate=pl.CostEstimate(
            flops=20_000_000_000,
            bytes_accessed=30_000_000,
            transcendentals=HEADS * count * TOKENS,
        ),
        name="attend_back",
    )(*arrays)


def small_call(kernel, name, scalars, arrays, outs, scratch=()):
    return pl.pallas_call(
        kernel,
        in_specs=[SCALARS] * len(scalars) + [WHOLE] * len(arrays),
        out_specs=[WHOLE] * len(outs),
        out_shape=outs,
        scratch_shapes=list(scratch),
        compiler_params=params(32),
        cost_estimate=pl.CostEstimate(flops=1_000_000, bytes_accessed=4_000_000, transcendentals=0),
        name=name,
    )(*scalars, *arrays)


def pack_kernel(core_ref, wq_ref, wk_ref, wv_ref, wo_ref, keep_ref, send_ref):
    for mine, first_ref, second_ref in ((0, keep_ref, send_ref), (1, send_ref, keep_ref)):

        @pl.when(core_ref[0] == mine)
        def _(first_ref=first_ref, second_ref=second_ref):
            first_ref[:WIDTH, :] = wq_ref[...]
            first_ref[WIDTH:, :] = wk_ref[...]
            second_ref[:WIDTH, :] = wv_ref[...]
            second_ref[WIDTH:, :] = wo_ref[...]


def split_kernel(spot_ref, *refs):
    ins, outs, total_ref = refs[:-5], refs[-5:-1], refs[-1]
    total = ins[0][...].astype(F32)
    for in_ref in ins[1:]:
        total = total + in_ref[...].astype(F32)
    total_ref[...] = total
    rows = outs[0].shape[0]
    for step, out_ref in enumerate(outs):
        start = pl.multiple_of((spot_ref[0] + step) % 4 * rows, 8)
        out_ref[...] = total_ref[pl.ds(start, rows), :].astype(BF)


def split(spot, arrays):
    rows, cols = arrays[0].shape
    return small_call(
        split_kernel, "split", [spot], arrays, [shape(rows // 4, cols, BF)] * 4,
        [pltpu.VMEM((rows, cols), F32)],
    )


def join_kernel(spot_ref, *refs):
    ins, out_ref, whole_ref = refs[:4], refs[4], refs[5]
    rows = ins[0].shape[0]
    for step, in_ref in enumerate(ins):
        start = pl.multiple_of((spot_ref[0] + step) % 4 * rows, 8)
        whole_ref[pl.ds(start, rows), :] = in_ref[...].astype(F32)
    out_ref[...] = whole_ref[...].astype(BF)


def join(spot, arrays):
    rows, cols = arrays[0].shape
    return small_call(
        join_kernel, "join", [spot], arrays, [shape(4 * rows, cols, BF)],
        [pltpu.VMEM((4 * rows, cols), F32)],
    )[0]


def add_kernel(*refs):
    total = refs[0][...].astype(F32)
    for in_ref in refs[1:-1]:
        total = total + in_ref[...].astype(F32)
    refs[-1][...] = total.astype(BF)


def add(arrays):
    return small_call(add_kernel, "add", [], arrays, [shape(*arrays[0].shape, BF)])[0]


def fold_kernel(l_ref, r_ref, above_ref, below_ref, left_ref, right_ref):
    for piece_ref, out_ref, start in ((l_ref, left_ref, TOKENS), (r_ref, right_ref, TOKENS + SIDE)):
        total = piece_ref[...].astype(F32)
        for band_ref in (above_ref, below_ref):
            total = total + band_ref[start : start + SIDE, :].astype(F32)
        out_ref[...] = total.astype(BF)


def tail_kernel(
    summed_ref, gown_ref, above_ref, below_ref, left_ref, right_ref, x_ref, gain_ref, gmid_ref,
    small_ref, gx_ref, cells_ref,
):
    total = gown_ref[...]
    for band_ref in (above_ref, below_ref):
        total = total + band_ref[:TOKENS, :].astype(F32)
    left, right = left_ref[...].astype(F32), right_ref[...].astype(F32)
    sides = []
    for r in range(ROWS):
        sides += [left[WINDOW * r : WINDOW * (r + 1)], right[WINDOW * r : WINDOW * (r + 1)]]
    total = total + jnp.concatenate(sides, axis=0)
    summed = folded(summed_ref[...].astype(F32), jnp.sum)
    token = lax.broadcasted_iota(jnp.int32, (TOKENS, WIDTH), 0)
    for k, where in enumerate(FAR_ROWS):
        total = total + jnp.where(token == where, summed[k : k + 1, :], 0.0)
    xhat, scale = normalized(x_ref[...].astype(F32))
    inputs, grad_gain, grad_shift = norm_back(total, xhat, scale, gain_ref[...])
    gx_ref[...] = gmid_ref[...] + inputs
    small = jnp.concatenate(
        [grad_gain, grad_shift, small_ref[0:2, :], jnp.zeros((4, WIDTH), F32)], axis=0
    )
    small = jnp.concatenate([small, small], axis=0).astype(BF)
    for k in range(GROUP // 2):
        cells_ref[16 * k : 16 * (k + 1), :] = small


def tail(arrays):
    return pl.pallas_call(
        tail_kernel,
        grid=(1,),
        in_specs=[fixed(*a.shape) for a in arrays],
        out_specs=[fixed(TOKENS, WIDTH), fixed(GROUP * 8, WIDTH)],
        out_shape=[shape(TOKENS, WIDTH, F32), shape(GROUP * 8, WIDTH, BF)],
        compiler_params=params(32),
        cost_estimate=pl.CostEstimate(
            flops=4_000_000, bytes_accessed=6_000_000, transcendentals=TOKENS
        ),
        name="tail",
    )(*arrays)


def finish_kernel(core_ref, own_ref, other_ref, small_ref, more_ref, *out_refs):
    wq_ref, wk_ref, wv_ref, wo_ref, vectors_ref = out_refs
    for mine, first_ref, second_ref in ((0, own_ref, other_ref), (1, other_ref, own_ref)):

        @pl.when(core_ref[0] == mine)
        def _(first_ref=first_ref, second_ref=second_ref):
            wq_ref[...] = first_ref[:WIDTH, :].astype(F32)
            wk_ref[...] = first_ref[WIDTH:, :].astype(F32)
            wv_ref[...] = second_ref[:WIDTH, :].astype(F32)
            wo_ref[...] = second_ref[WIDTH:, :].astype(F32)

    vectors_ref[...] = folded(small_ref[...].astype(F32), jnp.sum) + folded(
        more_ref[...].astype(F32), jnp.sum
    )


def after(value, first):
    return lax.optimization_barrier((value, first))


def piece_of(block, col_step):
    if col_step == 0:
        return block
    return block[:, WINDOW:] if col_step < 0 else block[:, : COLS - WINDOW]


def window_weights():
    rows, cols = np.mgrid[0:ROWS, 0:COLS]
    query = (rows.reshape(-1), cols.reshape(-1))
    key_rows, key_cols = [rows.reshape(-1)], [cols.reshape(-1)]
    for row_step, col_step in PIECES:
        key_rows.append(piece_of(rows, col_step).reshape(-1) + row_step * ROWS)
        key_cols.append(piece_of(cols, col_step).reshape(-1) + col_step * COLS)
    row_gap = np.concatenate(key_rows)[:, None] - query[0][None]
    col_gap = np.concatenate(key_cols)[:, None] - query[1][None]
    dense = (np.abs(row_gap) <= WINDOW) & (np.abs(col_gap) <= WINDOW)
    dilated = dense & (row_gap % 2 == 0) & (col_gap % 2 == 0)
    return np.where(dense, np.where(dilated, 1.0, 0.0), HIDE).astype(np.float32)


def local(
    embeddings,
    tile_valid,
    w_query,
    w_key,
    w_value,
    w_out,
    w_up,
    w_down,
    gain_attn,
    shift_attn,
    gain_mlp,
    shift_mlp,
    cotangent,
):
    gx, gy = lax.axis_index("gx"), lax.axis_index("gy")
    x, y, z, core = (v.astype(jnp.int32) for v in coords(lax.axis_index(AXES)))
    spots = [
        jnp.where(core == 0, (x, y, z)[ORDER[0][stage]], (x, y, z)[ORDER[1][stage]]).reshape(1)
        for stage in range(3)
    ]
    core = core.reshape(1)
    exists = jnp.stack(
        [
            (gy + row_step >= 0)
            & (gy + row_step < N_GY)
            & (gx + col_step >= 0)
            & (gx + col_step < N_GX)
            for row_step, col_step in PIECES
        ]
    ).astype(F32)
    tokens = embeddings.reshape(TOKENS, WIDTH)
    gain_attn, shift_attn = gain_attn.reshape(1, WIDTH), shift_attn.reshape(1, WIDTH)
    gain_mlp, shift_mlp = gain_mlp.reshape(1, WIDTH), shift_mlp.reshape(1, WIDTH)

    act, marked, left, right, spread = pre(tokens, tile_valid, gain_attn, shift_attn)
    far_own = exchanged(spread.reshape(GROUP, FAR_OWN, WIDTH)).reshape(FAR_HALF, WIDTH)
    far_other = sent(far_own, CORE_PAIRS)
    moved_left = sent(right, grid_pairs(0, -1))
    moved_right = sent(left, grid_pairs(0, 1))
    band = jnp.concatenate([marked, moved_left, moved_right], axis=0)
    pieces = [moved_left, moved_right, sent(band, grid_pairs(-1, 0)), sent(band, grid_pairs(1, 0))]
    near, bias_near, queries, k_near, v_near, tops, totals, sums = attend_near(
        exists, act, pieces, tile_valid, jnp.asarray(window_weights()), w_query, w_key, w_value
    )
    far, bias_far, k_far, v_far, outs, lse, middle = attend_far(
        far_own, far_other, tokens, queries, w_key, w_value, w_out, tops, totals, sums
    )
    grad_out = cotangent.reshape(TOKENS, WIDTH)
    mixed, grad_up, grad_down, grad_act = mlp(
        middle, gain_mlp, shift_mlp, grad_out, w_up, w_down
    )
    grad_up, grad_down = lax.psum((grad_up, grad_down), AXES)

    def rest(operands):
        attention, core, spots, tokens, gain_attn = operands
        grads = attend_back(attention)
        weights, (grad_mid, small, grad_own) = grads[:4], grads[4:7]
        piece_left, piece_right, piece_up, piece_down, far_keep, far_send = grads[7:]
        far_back = add([far_keep, sent(far_send, CORE_PAIRS)])
        far_back = exchanged(far_back.reshape(GROUP, FAR_OWN, WIDTH)).reshape(FAR_HALF, WIDTH)
        above = sent(piece_down, grid_pairs(-1, 0))
        below = sent(piece_up, grid_pairs(1, 0))
        side = shape(SIDE, WIDTH, BF)
        piece_left, piece_right = small_call(
            fold_kernel, "fold", [], [piece_left, piece_right, above, below], [side, side]
        )
        from_right = sent(piece_left, grid_pairs(0, 1))
        from_left = sent(piece_right, grid_pairs(0, -1))

        keep, send = small_call(pack_kernel, "pack", [core], weights, [shape(HALF, WIDTH, BF)] * 2)
        held = [keep, sent(send, CORE_PAIRS)]
        held, far_back = after(held, far_back)
        grad_inputs, cells = tail(
            [far_back, grad_own, above, below, from_left, from_right, tokens, gain_attn, grad_mid, small]
        )
        for stage in range(3):
            parts = split(spots[stage], held)
            held = [parts[0]] + [sent(parts[step], ring_pairs(stage, step)) for step in (2, 1, 3)]
            if stage == 0:
                held, cells = after(held, cells)
                cells = exchanged(cells.reshape(GROUP, 8, WIDTH)).reshape(GROUP * 8, WIDTH)
        held = add(held)
        held, cells = after(held, cells)
        for stage in (2, 1, 0):
            got = {step: sent(held, ring_pairs(stage, -step)) for step in (2, 1, 3)}
            held = join(spots[stage], [held, got[1], got[2], got[3]])
        finished = small_call(
            finish_kernel,
            "finish",
            [core],
            [held, sent(held, CORE_PAIRS), cells, sent(cells, CORE_PAIRS)],
            [shape(WIDTH, WIDTH, F32)] * 4 + [shape(8, WIDTH, F32)],
        )
        return [grad_inputs] + list(finished)

    def never(operands):
        return (
            [jnp.zeros((TOKENS, WIDTH), F32)]
            + [jnp.zeros((WIDTH, WIDTH), F32)] * 4
            + [jnp.zeros((8, WIDTH), F32)]
        )

    attention = [
        queries, outs, lse, middle, grad_act, gain_mlp, grad_out, k_near, v_near, k_far, v_far,
        bias_near, bias_far, near, far, w_query, w_key, w_value, w_out,
    ]
    grad_inputs, grad_wq, grad_wk, grad_wv, grad_wo, vectors = lax.cond(
        gx < N_GX, rest, never, (attention, core, spots, tokens, gain_attn)
    )
    return (
        mixed.reshape(ROWS, COLS, WIDTH),
        grad_inputs.reshape(ROWS, COLS, WIDTH),
        grad_wq,
        grad_wk,
        grad_wv,
        grad_wo,
        grad_up.astype(F32),
        grad_down.astype(F32),
        vectors[0],
        vectors[1],
        vectors[2],
        vectors[3],
    )


def solution(mesh):
    grid = P("gy", "gx", None)
    in_specs = (grid, P("gy", "gx")) + (P(),) * 10 + (grid,)
    out_specs = (grid, grid) + (P(),) * 10
    return jax.shard_map(local, mesh=mesh, in_specs=in_specs, out_specs=out_specs, check_vma=False)
```

```python
import functools
import math

import jax
import jax.numpy as jnp
import numpy as np
from jax import lax
from jax.experimental import pallas as pl
from jax.experimental.pallas import tpu as pltpu
from jax.sharding import PartitionSpec as P

HEADS = 16
HEAD_DIM = 48
PAIRS = HEADS // 2
PAIR = 2 * HEAD_DIM
VIEW = 256
STRIDE = 4
WINDOW = 8
ROWS = 8
COLS = 16
TOKENS = ROWS * COLS
WIDTH = 768
HIDDEN = 3072
N_GX = 32
N_GY = 4
N_DEV = N_GX * N_GY
GROUP = N_DEV // 2
AXES = ("gx", "gy")
BF = jnp.bfloat16
F32 = jnp.float32
SCALE = 1.0 / math.sqrt(HEAD_DIM)
SCALE_LOG2 = SCALE * math.log2(math.e)
MARK = 1e30
LIMIT = 1e29
HIDE = -1e30
CHUNK = 256
MLP_CHUNK = 512
WIDENED = 6
epsilon = 1e-05

PIECES = ((0, -1), (0, 1), (-1, 0), (-1, -1), (-1, 1), (1, 0), (1, -1), (1, 1))
SIZES = [TOKENS if col_step == 0 else TOKENS // 2 for _, col_step in PIECES]
STARTS = [TOKENS + sum(SIZES[:i]) for i in range(len(SIZES))]
NEAR = TOKENS + sum(SIZES)
SIDE = TOKENS // 2
BAND = TOKENS + 2 * SIDE
MOVED = (SIDE, SIDE, BAND, BAND)
MOVED_STARTS = [TOKENS + sum(MOVED[:i]) for i in range(4)]
FAR_OWN = (ROWS // STRIDE) * (COLS // STRIDE)
FAR_HALF = GROUP * FAR_OWN
FAR = 2 * FAR_HALF
FAR_ROWS = [COLS * STRIDE * r + STRIDE * c for r in range(ROWS // STRIDE) for c in range(COLS // STRIDE)]
HALF = 2 * WIDTH
SHARE = HALF // GROUP


def nt(left_op, right_op):
    return lax.dot_general(left_op, right_op, (((1,), (1,)), ((), ())), preferred_element_type=F32)


def tn(left_op, right_op):
    return lax.dot_general(left_op, right_op, (((0,), (0,)), ((), ())), preferred_element_type=F32)


def product(left_op, right_op):
    return jnp.dot(left_op, right_op, preferred_element_type=F32)


CORE_PAIRS = [(i, i ^ 1) for i in range(N_DEV)]
SAME_CORE = [[i for i in range(N_DEV) if i % 2 == core] for core in (0, 1)]


def sent(value, pairs):
    return lax.ppermute(value, AXES, pairs)


def grid_pairs(row_step, col_step):
    pairs = []
    for gx in range(N_GX):
        for gy in range(N_GY):
            sx, sy = gx + col_step, gy + row_step
            if 0 <= sx < N_GX and 0 <= sy < N_GY:
                pairs.append((sx * N_GY + sy, gx * N_GY + gy))
    return pairs


def exchanged(cells):
    return lax.all_to_all(cells, AXES, 0, 0, tiled=True, axis_index_groups=SAME_CORE)


def coords(flat):
    core, x_hi, z, x_lo, y = flat & 1, (flat >> 1) & 1, (flat >> 2) & 3, (flat >> 4) & 1, flat >> 5
    return (x_hi * 2 + x_lo, y, z, core)


def flat_of(place):
    x, y, z, core = place
    return y * 32 + (x & 1) * 16 + z * 4 + (x >> 1) * 2 + core


ORDER = {0: (2, 1, 0), 1: (0, 2, 1)}


def ring_pairs(stage, shift):
    pairs = []
    for i in range(N_DEV):
        place = list(coords(i))
        axis = ORDER[place[3]][stage]
        place[axis] = (place[axis] + shift) % 4
        pairs.append((i, flat_of(place)))
    return pairs


WHOLE = pl.BlockSpec(memory_space=pltpu.VMEM)
HBM = pl.BlockSpec(memory_space=pltpu.HBM)
SCALARS = pl.BlockSpec(memory_space=pltpu.SMEM)


def params(mebibytes):
    return pltpu.CompilerParams(vmem_limit_bytes=mebibytes * 1024 * 1024)


def shape(*dims_and_type):
    return jax.ShapeDtypeStruct(dims_and_type[:-1], dims_and_type[-1])


def in_hbm(array):
    return pltpu.with_memory_space_constraint(array, pltpu.HBM)


def fixed(*dims):
    return pl.BlockSpec(dims, lambda p: (0,) * len(dims))


def lanes(rows, cols):
    return pl.BlockSpec((rows, cols), lambda p: (0, p))


def sublanes(rows, cols):
    return pl.BlockSpec((rows, cols), lambda p: (p, 0))


def normalized(inputs):
    centered = inputs - jnp.mean(inputs, axis=1, keepdims=True)
    scale = lax.rsqrt(jnp.mean(centered * centered, axis=1, keepdims=True) + epsilon)
    return centered * scale, scale


def norm_back(grads, xhat, scale, gain):
    scaled = grads * gain
    inputs = scale * (
        scaled
        - jnp.mean(scaled, axis=1, keepdims=True)
        - xhat * jnp.mean(scaled * xhat, axis=1, keepdims=True)
    )
    return (
        inputs,
        jnp.sum(grads * xhat, axis=0, keepdims=True),
        jnp.sum(grads, axis=0, keepdims=True),
    )


def flag_column(flag_ref):
    row = lax.broadcasted_iota(jnp.int32, (TOKENS, ROWS), 0) // COLS
    block = lax.broadcasted_iota(jnp.int32, (TOKENS, ROWS), 1)
    rows = product(jnp.where(row == block, 1.0, 0.0).astype(BF), flag_ref[...].astype(F32).astype(BF))
    token = lax.broadcasted_iota(jnp.int32, (TOKENS, COLS), 0) % COLS
    col = lax.broadcasted_iota(jnp.int32, (TOKENS, COLS), 1)
    return jnp.sum(jnp.where(token == col, rows, 0.0), axis=1, keepdims=True)


def pre_kernel(x_ref, flag_ref, gain_ref, shift_ref, act_ref, marked_ref, spread_ref):
    xhat, _ = normalized(x_ref[...].astype(F32))
    act = xhat * gain_ref[...].reshape(1, WIDTH) + shift_ref[...].reshape(1, WIDTH)
    act = act.astype(BF)
    act_ref[...] = act
    marked = jnp.where(flag_column(flag_ref) > 0.5, act.astype(F32), MARK).astype(BF)
    marked_ref[...] = marked
    number = lax.broadcasted_iota(jnp.int32, (2 * FAR_OWN, TOKENS), 0) % FAR_OWN
    token = lax.broadcasted_iota(jnp.int32, (2 * FAR_OWN, TOKENS), 1)
    wanted = number // STRIDE * (COLS * STRIDE) + number % STRIDE * STRIDE
    chosen = product(jnp.where(token == wanted, 1.0, 0.0).astype(BF), marked).astype(BF)
    for k in range(GROUP // 2):
        spread_ref[2 * FAR_OWN * k : 2 * FAR_OWN * (k + 1), :] = chosen


def normed_marked(rows, gain, shift):
    rows = rows.astype(F32)
    xhat, _ = normalized(jnp.where(rows < LIMIT, rows, 0.0))
    return jnp.where(rows < LIMIT, xhat * gain + shift, MARK)


def band_kernel(marked_ref, l_ref, r_ref, gain_ref, shift_ref, band_ref):
    gain, shift = gain_ref[...].reshape(1, WIDTH), shift_ref[...].reshape(1, WIDTH)
    band_ref[:TOKENS, :] = marked_ref[...]
    for side_ref, start in ((l_ref, TOKENS), (r_ref, TOKENS + SIDE)):
        band_ref[start : start + SIDE, :] = normed_marked(side_ref[...], gain, shift).astype(BF)


def view_of(pair):
    start = jnp.minimum(pair * PAIR // 128 * 128, WIDTH - VIEW)
    return pl.ds(pl.multiple_of(start, 128), VIEW), pair * PAIR - start


def halves(block, begin):
    wide = block.astype(F32)
    lane = lax.broadcasted_iota(jnp.int32, wide.shape, 1) - begin
    first = jnp.where((lane >= 0) & (lane < HEAD_DIM), wide, 0.0).astype(BF)
    second = jnp.where((lane >= HEAD_DIM) & (lane < PAIR), wide, 0.0).astype(BF)
    return jnp.concatenate([first, second], axis=0)


def own_rows(wide):
    return jnp.concatenate([wide[:HEAD_DIM, :TOKENS], wide[HEAD_DIM:, TOKENS:]], axis=0)


def rows_of(pair):
    return pl.ds(pl.multiple_of(pair * PAIR, 32), PAIR)


def folded(tile, op):
    return op(tile.reshape(tile.shape[0] // 8, 8, tile.shape[1]), axis=0)


def attended_part(query_rows, k_ref, flip, view, bias_ref, t_ref, e_ref):
    count = k_ref.shape[0]
    top = jnp.full((8, 2 * TOKENS), HIDE, F32)
    for start in range(0, count, CHUNK):
        rows = pl.ds(start, CHUNK)
        bias = bias_ref[rows, :]
        tile = nt(k_ref[rows, view], query_rows) * SCALE_LOG2
        tile = tile + jnp.concatenate([bias, bias], axis=1)
        t_ref[rows, :] = tile
        top = jnp.maximum(top, folded(tile, jnp.max))
    top = jnp.max(top, axis=0, keepdims=True)
    total = jnp.zeros((8, 2 * TOKENS), F32)
    for start in range(0, count, CHUNK):
        rows = pl.ds(start, CHUNK)
        tile = jnp.exp2(t_ref[rows, :] - top)
        total = total + folded(tile, jnp.sum)
        e_ref[rows, :] = tile.astype(BF)
    total = jnp.sum(total, axis=0, keepdims=True)
    return top, total, own_rows(product(flip, e_ref[...]))


def near_kernel(
    exists_ref, act_ref, band_ref, u_ref, d_ref, flag_ref, log_ref, wq_ref, wk_ref, wv_ref,
    all_ref, bias_ref, q_ref, k_ref, v_ref, top_ref, total_ref, sum_ref, t_ref, p_ref, flip_ref,
):
    pair = pl.program_id(0)

    @pl.when(pair == 0)
    def _():
        all_ref[:TOKENS, :] = act_ref[...]
        row = lax.broadcasted_iota(jnp.int32, (TOKENS, TOKENS), 0)
        col = lax.broadcasted_iota(jnp.int32, (TOKENS, TOKENS), 1)
        seen = jnp.where(row == col, 1.0, flag_column(flag_ref))
        bias_ref[:TOKENS, :] = jnp.where(seen > 0.5, log_ref[:TOKENS, :], HIDE)
        for i, (start, size) in enumerate(zip(STARTS, SIZES, strict=True)):
            rows = slice(start, start + size)
            moved, begin = start // BAND, start % BAND
            piece = (band_ref, u_ref, d_ref)[moved][begin : begin + size, :].astype(F32)
            all_ref[rows, :] = jnp.where(piece < LIMIT, piece, 0.0).astype(BF)
            seen = jnp.where(piece[:, :128] < LIMIT, 1.0, 0.0)[:, :1] * exists_ref[i]
            bias_ref[rows, :] = jnp.where(seen > 0.5, log_ref[rows, :], HIDE)
        q_ref[...] = product(act_ref[...], wq_ref[...]).astype(BF)
        k_ref[...] = product(all_ref[...], wk_ref[...]).astype(BF)
        values = product(all_ref[...], wv_ref[...]).astype(BF)
        v_ref[...] = values
        flip_ref[...] = values.T

    view, begin = view_of(pair)
    top, total, wide = attended_part(
        halves(q_ref[:, view], begin), k_ref, flip_ref[rows_of(pair), :], view, bias_ref, t_ref, p_ref
    )
    top_ref[pair] = top
    total_ref[pair] = total
    sum_ref[pair] = wide


def attend_near(exists, act, bands, flags, log_weight, wq, wk, wv):
    return pl.pallas_call(
        near_kernel,
        grid=(PAIRS,),
        in_specs=[SCALARS] + [WHOLE] * 9,
        out_specs=[WHOLE] * 8,
        out_shape=[
            shape(NEAR, WIDTH, BF),
            shape(NEAR, TOKENS, F32),
            shape(TOKENS, WIDTH, BF),
            shape(NEAR, WIDTH, BF),
            shape(NEAR, WIDTH, BF),
            shape(PAIRS, 1, 2 * TOKENS, F32),
            shape(PAIRS, 1, 2 * TOKENS, F32),
            shape(PAIRS, PAIR, TOKENS, F32),
        ],
        scratch_shapes=[
            pltpu.VMEM((NEAR, 2 * TOKENS), F32),
            pltpu.VMEM((NEAR, 2 * TOKENS), BF),
            pltpu.VMEM((WIDTH, NEAR), BF),
        ],
        compiler_params=params(14),
        cost_estimate=pl.CostEstimate(
            flops=10_000_000_000, bytes_accessed=12_000_000, transcendentals=0
        ),
        name="attend_near",
    )(exists, act, *bands, flags, log_weight, wq, wk, wv)


def mlp_part(middle, gain, shift, grad_out, wup_ref, wdown_ref, mixed_ref, gact_ref, gup, gdown):
    xhat, _ = normalized(middle)
    act = (xhat * gain + shift).astype(BF)
    act_flip = act.T
    total, grad_act = middle, 0.0
    for step in range(HIDDEN // MLP_CHUNK):
        chunk = slice(step * MLP_CHUNK, (step + 1) * MLP_CHUNK)
        up, down = wup_ref[:, chunk], wdown_ref[chunk, :]
        pre_act = product(act, up)
        below = 0.5 * (1.0 + lax.erf(pre_act * math.sqrt(0.5)))
        slope = jnp.exp(-0.5 * pre_act * pre_act) * (1.0 / math.sqrt(2.0 * math.pi))
        slope = below + pre_act * slope
        hidden = (pre_act * below).astype(BF)
        grad_pre = (nt(grad_out, down) * slope).astype(BF)
        total = total + product(hidden, down)
        grad_act = grad_act + nt(grad_pre, up)
        for (staged, copy), value in (
            (gup[step], product(act_flip, grad_pre)),
            (gdown[step], tn(hidden, grad_out)),
        ):
            staged[...] = value.astype(BF)
            copy.start()
    mixed_ref[...] = total.astype(BF)
    gact_ref[...] = grad_act
    for _, copy in gup + gdown:
        copy.wait()


def far_kernel(
    x_ref, q_ref, top_ref, total_ref, sum_ref, gain_ref, shift_ref, gout_ref,
    own_hbm, other_hbm, wk_hbm, wv_hbm, wo_hbm, wup_hbm, wdown_hbm,
    all_ref, bias_ref, k_ref, v_ref, o_ref, lse_ref, mid_ref, mixed_ref, gact_ref, gup_hbm,
    gdown_hbm,
    t_ref, e_ref, flip_ref, out_ref, wk_ref, wv_ref, wo_ref, wup_ref, wdown_ref, gup_ref,
    gdown_ref, far_ref, sems, up_sems, down_sems,
):
    pair = pl.program_id(0)
    copies = [
        pltpu.make_async_copy(src, dst, sems.at[i])
        for i, (src, dst) in enumerate(
            (
                (own_hbm, far_ref.at[:FAR_HALF]), (other_hbm, far_ref.at[FAR_HALF:]),
                (wk_hbm, wk_ref), (wv_hbm, wv_ref), (wo_hbm, wo_ref), (wup_hbm, wup_ref),
                (wdown_hbm, wdown_ref),
            )
        )
    ]

    @pl.when(pair == 0)
    def _():
        for copy in copies:
            copy.start()
        copies[0].wait()
        copies[1].wait()
        for start in range(0, FAR, CHUNK):
            rows = slice(start, start + CHUNK)
            piece = far_ref[rows, :].astype(F32)
            all_ref[rows, :] = jnp.where(piece < LIMIT, piece, 0.0).astype(BF)
            seen = jnp.where(piece[:, :128] < LIMIT, 0.0, HIDE)[:, :1]
            bias_ref[rows, :] = jnp.broadcast_to(seen, (CHUNK, TOKENS))
        copies[2].wait()
        copies[3].wait()
        k_ref[...] = product(all_ref[...], wk_ref[...]).astype(BF)
        values = product(all_ref[...], wv_ref[...]).astype(BF)
        v_ref[...] = values
        flip_ref[...] = values.T

    view, begin = view_of(pair)
    far_top, far_total, far_sum = attended_part(
        halves(q_ref[:, view], begin), k_ref, flip_ref[rows_of(pair), :], view, bias_ref, t_ref, e_ref
    )
    near_top = top_ref[pair]
    top = jnp.maximum(near_top, far_top)
    near_part, far_part = jnp.exp2(near_top - top), jnp.exp2(far_top - top)
    total = total_ref[pair] * near_part + far_total * far_part
    near_part, far_part = near_part / total, far_part / total
    near_sum = sum_ref[pair]
    out_ref[rows_of(pair), :] = jnp.concatenate(
        [
            near_sum[rows] * near_part[:, cols] + far_sum[rows] * far_part[:, cols]
            for rows, cols in (
                (slice(0, HEAD_DIM), slice(0, TOKENS)),
                (slice(HEAD_DIM, PAIR), slice(TOKENS, 2 * TOKENS)),
            )
        ],
        axis=0,
    )
    lse_ref[pair] = top + jnp.log2(total)

    @pl.when(pair == PAIRS - 1)
    def _():
        outs = out_ref[...].T
        o_ref[...] = outs
        for copy in copies[4:]:
            copy.wait()
        middle = x_ref[...].astype(F32) + product(outs.astype(BF), wo_ref[...])
        mid_ref[...] = middle
        gup, gdown = [], []
        for step in range(HIDDEN // MLP_CHUNK):
            chunk = pl.ds(step * MLP_CHUNK, MLP_CHUNK)
            for pairs, src, dst, sem in (
                (gup, gup_ref.at[:, chunk], gup_hbm.at[:, chunk], up_sems.at[step]),
                (gdown, gdown_ref.at[chunk, :], gdown_hbm.at[chunk, :], down_sems.at[step]),
            ):
                pairs.append((src, pltpu.make_async_copy(src, dst, sem)))
        mlp_part(
            middle, gain_ref[...].reshape(1, WIDTH), shift_ref[...].reshape(1, WIDTH), gout_ref[...],
            wup_ref, wdown_ref, mixed_ref, gact_ref, gup, gdown,
        )


def attend_far(arrays):
    return pl.pallas_call(
        far_kernel,
        grid=(PAIRS,),
        in_specs=[WHOLE] * 8 + [HBM] * 7,
        out_specs=[WHOLE] * 9 + [HBM] * 2,
        out_shape=[
            shape(FAR, WIDTH, BF),
            shape(FAR, TOKENS, F32),
            shape(FAR, WIDTH, BF),
            shape(FAR, WIDTH, BF),
            shape(TOKENS, WIDTH, F32),
            shape(PAIRS, 1, 2 * TOKENS, F32),
            shape(TOKENS, WIDTH, F32),
            shape(TOKENS, WIDTH, BF),
            shape(TOKENS, WIDTH, F32),
            pltpu.HBM((WIDTH, HIDDEN), BF),
            pltpu.HBM((HIDDEN, WIDTH), BF),
        ],
        scratch_shapes=[
            pltpu.VMEM((FAR, 2 * TOKENS), F32),
            pltpu.VMEM((FAR, 2 * TOKENS), BF),
            pltpu.VMEM((WIDTH, FAR), BF),
            pltpu.VMEM((WIDTH, TOKENS), F32),
            pltpu.VMEM((WIDTH, WIDTH), BF),
            pltpu.VMEM((WIDTH, WIDTH), BF),
            pltpu.VMEM((WIDTH, WIDTH), BF),
            pltpu.VMEM((WIDTH, HIDDEN), BF),
            pltpu.VMEM((HIDDEN, WIDTH), BF),
            pltpu.VMEM((WIDTH, HIDDEN), BF),
            pltpu.VMEM((HIDDEN, WIDTH), BF),
            pltpu.VMEM((FAR, WIDTH), BF),
            pltpu.SemaphoreType.DMA((7,)),
            pltpu.SemaphoreType.DMA((HIDDEN // MLP_CHUNK,)),
            pltpu.SemaphoreType.DMA((HIDDEN // MLP_CHUNK,)),
        ],
        compiler_params=params(36),
        cost_estimate=pl.CostEstimate(
            flops=20_000_000_000, bytes_accessed=30_000_000, transcendentals=HEADS * FAR * TOKENS
        ),
        name="attend_far_mlp",
    )(*arrays)


def mid_kernel(
    o_ref, mid_ref, gact_ref, gain_ref, gout_ref, wo_ref, kn_ref, kf_ref, alln_ref, allf_ref,
    gwo_ref, gmid_ref, small_ref, gatt_ref, inner_ref, flip_ref, kflip_ref,
):
    xhat, scale = normalized(mid_ref[...])
    inputs, grad_gain, grad_shift = norm_back(
        gact_ref[...], xhat, scale, gain_ref[...].reshape(1, WIDTH)
    )
    grad_mid = gout_ref[...].astype(F32) + inputs
    gmid_ref[...] = grad_mid
    small_ref[...] = jnp.concatenate([grad_gain, grad_shift, jnp.zeros((6, WIDTH), F32)], axis=0)
    branch = grad_mid.astype(BF)
    grads = nt(branch, wo_ref[...]).astype(BF)
    gatt_ref[...] = grads
    gwo_ref[...] = tn(o_ref[...].astype(BF), branch).astype(BF)
    inner_ref[...] = (grads.astype(F32) * o_ref[...]).T
    flip_ref[:, :NEAR] = alln_ref[...].T
    flip_ref[:, NEAR:] = allf_ref[...].T
    kflip_ref[:, :NEAR] = kn_ref[...].T
    kflip_ref[:, NEAR:] = kf_ref[...].T


def back_kernel(
    q_ref, gatt_ref, inner_ref, lse_ref, kn_ref, vn_ref, kf_ref, vf_ref, biasn_ref, biasf_ref,
    flip_ref, kflip_ref, wq_ref, wk_ref, wv_ref,
    gwq_ref, gwk_ref, gwv_ref, gown_ref, l_ref, r_ref, u_ref, d_ref, gfar_ref,
    s_ref, p_ref, gq_ref, gk_ref, gv_ref, acc_ref,
):
    pair = pl.program_id(0)

    @pl.when(pair == 0)
    def _():
        gk_ref[...] = jnp.zeros_like(gk_ref)
        gv_ref[...] = jnp.zeros_like(gv_ref)

    view, begin = view_of(pair)
    query_rows = halves(q_ref[:, view], begin)
    grad_rows = halves(gatt_ref[:, view], begin)
    inner = inner_ref[rows_of(pair), :]
    inner = jnp.concatenate(
        [
            jnp.sum(inner[:HEAD_DIM], axis=0, keepdims=True),
            jnp.sum(inner[HEAD_DIM:], axis=0, keepdims=True),
        ],
        axis=1,
    )
    lse = lse_ref[pair]
    for k_ref, v_ref, bias_ref, offset in (
        (kn_ref, vn_ref, biasn_ref, 0),
        (kf_ref, vf_ref, biasf_ref, NEAR),
    ):
        for start in range(0, k_ref.shape[0], CHUNK):
            rows = pl.ds(start, CHUNK)
            bias = bias_ref[rows, :]
            tile = nt(k_ref[rows, view], query_rows) * SCALE_LOG2
            probs = jnp.exp2(tile + jnp.concatenate([bias, bias], axis=1) - lse)
            grad_probs = nt(v_ref[rows, view], grad_rows)
            there = pl.ds(offset + start, CHUNK)
            s_ref[there, :] = (probs * (grad_probs - inner)).astype(BF)
            p_ref[there, :] = probs.astype(BF)
    gk_ref[:, view] += (product(s_ref[...], query_rows) * SCALE).astype(BF)
    gv_ref[:, view] += product(p_ref[...], grad_rows).astype(BF)
    gq_ref[rows_of(pair), :] = own_rows(product(kflip_ref[rows_of(pair), :], s_ref[...])) * SCALE

    @pl.when(pair == PAIRS - 1)
    def _():
        grad_query = gq_ref[...].T.astype(BF)
        acc_ref[...] = nt(gk_ref[...], wk_ref[...])
        acc_ref[...] += nt(gv_ref[...], wv_ref[...])
        gown_ref[...] = acc_ref[:TOKENS, :] + nt(grad_query, wq_ref[...])
        for piece_ref, start, size in zip(
            (l_ref, r_ref, u_ref, d_ref), MOVED_STARTS, MOVED, strict=True
        ):
            piece_ref[...] = acc_ref[start : start + size, :].astype(BF)
        gfar_ref[...] = acc_ref[NEAR:, :]
        gwk_ref[...] = product(flip_ref[...], gk_ref[...]).astype(BF)
        gwv_ref[...] = product(flip_ref[...], gv_ref[...]).astype(BF)
        gwq_ref[...] = product(flip_ref[:, :TOKENS], grad_query).astype(BF)


def attend_back(arrays):
    count = NEAR + FAR
    return pl.pallas_call(
        back_kernel,
        grid=(PAIRS,),
        in_specs=[WHOLE] * 15,
        out_specs=[WHOLE] * 9,
        out_shape=[shape(WIDTH, WIDTH, BF)] * 3
        + [shape(TOKENS, WIDTH, F32)]
        + [shape(size, WIDTH, BF) for size in MOVED]
        + [shape(FAR, WIDTH, F32)],
        scratch_shapes=[
            pltpu.VMEM((count, 2 * TOKENS), BF),
            pltpu.VMEM((count, 2 * TOKENS), BF),
            pltpu.VMEM((WIDTH, TOKENS), F32),
            pltpu.VMEM((count, WIDTH), BF),
            pltpu.VMEM((count, WIDTH), BF),
            pltpu.VMEM((count, WIDTH), F32),
        ],
        compiler_params=params(26),
        cost_estimate=pl.CostEstimate(
            flops=20_000_000_000,
            bytes_accessed=30_000_000,
            transcendentals=HEADS * count * TOKENS,
        ),
        name="attend_back",
    )(*arrays)


def small_call(kernel, name, scalars, arrays, outs, scratch=(), flops=0):
    return pl.pallas_call(
        kernel,
        in_specs=[SCALARS] * len(scalars) + [WHOLE] * len(arrays),
        out_specs=[WHOLE] * len(outs),
        out_shape=outs,
        scratch_shapes=list(scratch),
        compiler_params=params(20),
        cost_estimate=pl.CostEstimate(flops=flops, bytes_accessed=0, transcendentals=0),
        name=name,
    )(*scalars, *arrays)


def far_place(core, cell):
    where = [0, 0, 0]
    for stage, axis in enumerate(ORDER[core]):
        where[axis] = cell // 4 ** (2 - stage) % 4
    return FAR_OWN * (flat_of((*where, core)) // 2)


def pack_kernel(core_ref, wq_ref, wk_ref, wv_ref, wo_ref, gfar_ref, keep_ref, send_ref):
    for mine, first_ref, second_ref in ((0, keep_ref, send_ref), (1, send_ref, keep_ref)):

        @pl.when(core_ref[0] == mine)
        def _(mine=mine, first_ref=first_ref, second_ref=second_ref):
            for core, out_ref, weights in (
                (0, first_ref, (wq_ref, wk_ref)),
                (1, second_ref, (wv_ref, wo_ref)),
            ):
                for group in range(16):
                    row = 4 * SHARE * group
                    start = 4 * (SHARE + FAR_OWN) * group
                    out_ref[start : start + 4 * SHARE, :] = weights[row // WIDTH][
                        row % WIDTH : row % WIDTH + 4 * SHARE, :
                    ]
                    base = 0 if core == mine else FAR_HALF
                    far = [base + far_place(core, 4 * group + k) for k in range(4)]
                    out_ref[start + 4 * SHARE : start + 4 * (SHARE + FAR_OWN), :] = jnp.concatenate(
                        [gfar_ref[f : f + FAR_OWN, :] for f in far], axis=0
                    ).astype(BF)


def split_kernel(layout, spot_ref, *refs):
    ins, outs, total_ref = refs[:-5], refs[-5:-1], refs[-1]
    total = ins[0][...].astype(F32)
    for in_ref in ins[1:]:
        total = total + in_ref[...].astype(F32)
    total_ref[...] = total
    for step, out_ref in enumerate(outs):
        place = (spot_ref[0] + step) % 4
        runs = [
            total_ref[pl.ds(pl.multiple_of(start + place * (length // 4), 8), length // 4), :]
            for start, length in layout
        ]
        out_ref[...] = jnp.concatenate(runs, axis=0).astype(BF)


def split(spot, arrays, layout=None):
    rows, cols = arrays[0].shape
    return small_call(
        functools.partial(split_kernel, layout or ((0, rows),)),
        "split",
        [spot],
        arrays,
        [shape(rows // 4, cols, BF)] * 4,
        [pltpu.VMEM((rows, cols), F32)],
    )


def join_kernel(extra, spot_ref, *refs):
    ins, out_ref, whole_ref = refs[:4], refs[4], refs[5]
    rows = ins[0].shape[0] - extra
    rest = 0.0
    for step, in_ref in enumerate(ins):
        start = pl.multiple_of((spot_ref[0] + step) % 4 * rows, 8)
        part = in_ref[...].astype(F32)
        whole_ref[pl.ds(start, rows), :] = part[:rows]
        rest = rest + part[rows:]
    if extra:
        whole_ref[4 * rows :, :] = rest
    out_ref[...] = whole_ref[...].astype(BF)


def join(spot, arrays, extra=0):
    rows, cols = arrays[0].shape
    out = 4 * (rows - extra) + extra
    return small_call(
        functools.partial(join_kernel, extra), "join", [spot], arrays, [shape(out, cols, BF)],
        [pltpu.VMEM((out, cols), F32)],
    )[0]


def add_kernel(*refs):
    total = refs[0][...].astype(F32)
    for in_ref in refs[1:-1]:
        total = total + in_ref[...].astype(F32)
    refs[-1][...] = total.astype(BF)


def add(arrays):
    return small_call(add_kernel, "add", [], arrays, [shape(*arrays[0].shape, BF)])[0]


def fold_kernel(l_ref, r_ref, above_ref, below_ref, left_ref, right_ref):
    for piece_ref, out_ref, start in ((l_ref, left_ref, TOKENS), (r_ref, right_ref, TOKENS + SIDE)):
        total = piece_ref[...].astype(F32)
        for band_ref in (above_ref, below_ref):
            total = total + band_ref[start : start + SIDE, :].astype(F32)
        out_ref[...] = total.astype(BF)


def tail_kernel(
    cell_ref, cell1_ref, cell2_ref, cell3_ref, gown_ref, above_ref, below_ref, left_ref, right_ref, x_ref, gain_ref, gmid_ref,
    small_ref, gx_ref, out_ref,
):
    total = gown_ref[...]
    for band_ref in (above_ref, below_ref):
        total = total + band_ref[:TOKENS, :].astype(F32)
    left, right = left_ref[...].astype(F32), right_ref[...].astype(F32)
    sides = []
    for r in range(ROWS):
        sides += [left[WINDOW * r : WINDOW * (r + 1)], right[WINDOW * r : WINDOW * (r + 1)]]
    total = total + jnp.concatenate(sides, axis=0)
    summed = cell_ref[...].astype(F32)
    for other_ref in (cell1_ref, cell2_ref, cell3_ref):
        summed = summed + other_ref[...].astype(F32)
    far = summed[SHARE:]
    token = lax.broadcasted_iota(jnp.int32, (TOKENS, WIDTH), 0)
    for k, where in enumerate(FAR_ROWS):
        total = total + jnp.where(token == where, far[k : k + 1, :], 0.0)
    xhat, scale = normalized(x_ref[...].astype(F32))
    inputs, grad_gain, grad_shift = norm_back(
        total, xhat, scale, gain_ref[...].reshape(1, WIDTH)
    )
    gx_ref[...] = gmid_ref[...] + inputs
    small = jnp.concatenate(
        [grad_gain, grad_shift, small_ref[0:2, :], jnp.zeros((4, WIDTH), F32)], axis=0
    )
    out_ref[...] = jnp.concatenate([summed[:SHARE], small], axis=0).astype(BF)


def tail(arrays):
    return pl.pallas_call(
        tail_kernel,
        grid=(1,),
        in_specs=[fixed(*a.shape) for a in arrays],
        out_specs=[fixed(TOKENS, WIDTH), fixed(SHARE + 8, WIDTH)],
        out_shape=[shape(TOKENS, WIDTH, F32), shape(SHARE + 8, WIDTH, BF)],
        compiler_params=params(32),
        cost_estimate=pl.CostEstimate(flops=0, bytes_accessed=0, transcendentals=0),
        name="tail",
    )(*arrays)


def finish_kernel(core_ref, own_ref, other_ref, wq_ref, wk_ref, wv_ref, wo_ref, vectors_ref):
    for mine, first_ref, second_ref in ((0, own_ref, other_ref), (1, other_ref, own_ref)):

        @pl.when(core_ref[0] == mine)
        def _(first_ref=first_ref, second_ref=second_ref):
            wq_ref[...] = first_ref[:WIDTH, :].astype(F32)
            wk_ref[...] = first_ref[WIDTH:HALF, :].astype(F32)
            wv_ref[...] = second_ref[:WIDTH, :].astype(F32)
            wo_ref[...] = second_ref[WIDTH:HALF, :].astype(F32)

    vectors_ref[...] = own_ref[...].astype(F32)[HALF:] + other_ref[...].astype(F32)[HALF:]


def widen_kernel(up_hbm, down_hbm, up_out_hbm, down_out_hbm, *refs):
    ins, outs, in_sems, out_sems = refs[:2], refs[2:4], refs[4], refs[5]
    pieces = []
    for i, (src, dst) in enumerate(((up_hbm, up_out_hbm), (down_hbm, down_out_hbm))):
        rows = src.shape[0] // WIDENED
        for k in range(WIDENED):
            run, sem = pl.ds(rows * k, rows), WIDENED * i + k
            pieces.append(
                (
                    ins[i].at[run, :],
                    outs[i].at[run, :],
                    pltpu.make_async_copy(src.at[run, :], ins[i].at[run, :], in_sems.at[sem]),
                    pltpu.make_async_copy(outs[i].at[run, :], dst.at[run, :], out_sems.at[sem]),
                )
            )
    for _, _, fetch, _ in pieces:
        fetch.start()
    for in_ref, out_ref, fetch, put in pieces:
        fetch.wait()
        out_ref[...] = in_ref[...].astype(F32)
        put.start()
    for _, _, _, put in pieces:
        put.wait()


def widen(grad_up, grad_down):
    shapes = ((WIDTH, HIDDEN), (HIDDEN, WIDTH))
    return pl.pallas_call(
        widen_kernel,
        in_specs=[HBM] * 2,
        out_specs=[HBM] * 2,
        out_shape=[shape(*dims, F32) for dims in shapes],
        scratch_shapes=[pltpu.VMEM(dims, BF) for dims in shapes]
        + [pltpu.VMEM(dims, F32) for dims in shapes]
        + [pltpu.SemaphoreType.DMA((2 * WIDENED,))] * 2,
        compiler_params=params(40),
        cost_estimate=pl.CostEstimate(
            flops=1_000_000, bytes_accessed=28_000_000, transcendentals=0
        ),
        name="widen",
    )(in_hbm(grad_up), in_hbm(grad_down))


def after(*values):
    return lax.optimization_barrier(values)


def piece_of(block, col_step):
    if col_step == 0:
        return block
    return block[:, WINDOW:] if col_step < 0 else block[:, : COLS - WINDOW]


def window_weights():
    rows, cols = np.mgrid[0:ROWS, 0:COLS]
    query = (rows.reshape(-1), cols.reshape(-1))
    key_rows, key_cols = [rows.reshape(-1)], [cols.reshape(-1)]
    for row_step, col_step in PIECES:
        key_rows.append(piece_of(rows, col_step).reshape(-1) + row_step * ROWS)
        key_cols.append(piece_of(cols, col_step).reshape(-1) + col_step * COLS)
    row_gap = np.concatenate(key_rows)[:, None] - query[0][None]
    col_gap = np.concatenate(key_cols)[:, None] - query[1][None]
    dense = (np.abs(row_gap) <= WINDOW) & (np.abs(col_gap) <= WINDOW)
    dilated = dense & (row_gap % 2 == 0) & (col_gap % 2 == 0)
    return np.where(dense, np.where(dilated, 1.0, 0.0), HIDE).astype(np.float32)


def local(
    embeddings,
    tile_valid,
    w_query,
    w_key,
    w_value,
    w_out,
    w_up,
    w_down,
    gain_attn,
    shift_attn,
    gain_mlp,
    shift_mlp,
    cotangent,
):
    gx, gy = lax.axis_index("gx"), lax.axis_index("gy")
    x, y, z, core = (v.astype(jnp.int32) for v in coords(lax.axis_index(AXES)))
    spots = [
        jnp.where(core == 0, (x, y, z)[ORDER[0][stage]], (x, y, z)[ORDER[1][stage]]).reshape(1)
        for stage in range(3)
    ]
    core = core.reshape(1)
    exists = jnp.stack(
        [
            (gy + row_step >= 0)
            & (gy + row_step < N_GY)
            & (gx + col_step >= 0)
            & (gx + col_step < N_GX)
            for row_step, col_step in PIECES
        ]
    ).astype(F32)
    tokens = embeddings.reshape(TOKENS, WIDTH)

    raw = jnp.where(tile_valid[:, :, None] > 0, embeddings, jnp.asarray(MARK, BF))
    moved_left = sent(raw[:, WINDOW:].reshape(SIDE, WIDTH), grid_pairs(0, -1))
    moved_right = sent(raw[:, :WINDOW].reshape(SIDE, WIDTH), grid_pairs(0, 1))
    act, marked, spread = small_call(
        pre_kernel,
        "pre",
        [],
        [tokens, tile_valid, gain_attn, shift_attn],
        [shape(TOKENS, WIDTH, BF), shape(TOKENS, WIDTH, BF), shape(FAR_HALF, WIDTH, BF)],
        flops=10_000_000_000,
    )
    band = small_call(
        band_kernel,
        "band",
        [],
        [marked, moved_left, moved_right, gain_attn, shift_attn],
        [shape(BAND, WIDTH, BF)],
    )[0]
    spread, band = after(spread, band)
    far_own = exchanged(spread.reshape(GROUP, FAR_OWN, WIDTH)).reshape(FAR_HALF, WIDTH)
    bands = [band, sent(band, grid_pairs(-1, 0)), sent(band, grid_pairs(1, 0))]
    near, bias_near, queries, k_near, v_near, tops, totals, sums = attend_near(
        exists, act, bands, tile_valid, jnp.asarray(window_weights()), w_query, w_key, w_value
    )
    far_own, sums = after(far_own, sums)
    far_other = sent(far_own, CORE_PAIRS)
    grad_out = cotangent.reshape(TOKENS, WIDTH)
    (
        far, bias_far, k_far, v_far, outs, lse, middle, mixed, grad_act, grad_up, grad_down
    ) = attend_far(
        [
            tokens, queries, tops, totals, sums, gain_mlp, shift_mlp, grad_out,
            *map(in_hbm, (far_own, far_other, w_key, w_value, w_out, w_up, w_down)),
        ]
    )
    grad_up, grad_down = lax.psum((grad_up, grad_down), AXES)

    def rest(operands):
        before, attention, core, spots, tokens, gain_attn = operands
        grad_wo, grad_mid, small, grad_att, inner, flip, key_flip = small_call(
            mid_kernel,
            "mid",
            [],
            before,
            [shape(WIDTH, WIDTH, BF), shape(TOKENS, WIDTH, F32), shape(8, WIDTH, F32)]
            + [shape(TOKENS, WIDTH, BF), shape(WIDTH, TOKENS, F32)]
            + [shape(WIDTH, NEAR + FAR, BF)] * 2,
        )
        queries, lse, *keys_values, w_query, w_key, w_value = attention
        grad_wq, grad_wk, grad_wv, grad_own, *pieces, grad_far = attend_back(
            [queries, grad_att, inner, lse, *keys_values, flip, key_flip, w_query, w_key, w_value]
        )
        piece_left, piece_right, piece_up, piece_down = pieces
        packed = small_call(
            pack_kernel,
            "pack",
            [core],
            [grad_wq, grad_wk, grad_wv, grad_wo, grad_far],
            [shape(HALF + FAR_HALF, WIDTH, BF)] * 2,
        )
        above = sent(piece_down, grid_pairs(-1, 0))
        below = sent(piece_up, grid_pairs(1, 0))
        side = shape(SIDE, WIDTH, BF)
        piece_left, piece_right = small_call(
            fold_kernel, "fold", [], [piece_left, piece_right, above, below], [side, side]
        )
        from_right = sent(piece_left, grid_pairs(0, 1))
        from_left = sent(piece_right, grid_pairs(0, -1))

        held = [packed[0], sent(packed[1], CORE_PAIRS)]
        for stage in range(3):
            layout = ((0, 4 * SHARE), (4 * SHARE, 4 * FAR_OWN)) if stage == 2 else None
            parts = split(spots[stage], held, layout)
            held = [parts[0]] + [sent(parts[step], ring_pairs(stage, step)) for step in (2, 1, 3)]
        grad_inputs, cell = tail(
            held
            + [grad_own, above, below, from_left, from_right, tokens, gain_attn, grad_mid, small]
        )
        for stage in (2, 1, 0):
            got = {step: sent(cell, ring_pairs(stage, -step)) for step in (2, 1, 3)}
            cell = join(spots[stage], [cell, got[1], got[2], got[3]], 8)
        finished = small_call(
            finish_kernel,
            "finish",
            [core],
            [cell, sent(cell, CORE_PAIRS)],
            [shape(WIDTH, WIDTH, F32)] * 4 + [shape(8, WIDTH, F32)],
        )
        return [grad_inputs] + list(finished)

    def never(operands):
        return (
            [jnp.zeros((TOKENS, WIDTH), F32)]
            + [jnp.zeros((WIDTH, WIDTH), F32)] * 4
            + [jnp.zeros((8, WIDTH), F32)]
        )

    before = [outs, middle, grad_act, gain_mlp, grad_out, w_out, k_near, k_far, near, far]
    attention = [
        queries, lse, k_near, v_near, k_far, v_far, bias_near, bias_far, w_query, w_key, w_value
    ]
    grad_inputs, grad_wq, grad_wk, grad_wv, grad_wo, vectors = lax.cond(
        gx < N_GX, rest, never, (before, attention, core, spots, tokens, gain_attn)
    )
    return (
        mixed.reshape(ROWS, COLS, WIDTH),
        grad_inputs.reshape(ROWS, COLS, WIDTH),
        grad_wq,
        grad_wk,
        grad_wv,
        grad_wo,
        *widen(grad_up, grad_down),
        vectors[0],
        vectors[1],
        vectors[2],
        vectors[3],
    )


def solution(mesh):
    grid = P("gy", "gx", None)
    in_specs = (grid, P("gy", "gx")) + (P(),) * 10 + (grid,)
    out_specs = (grid, grid) + (P(),) * 10
    return jax.shard_map(local, mesh=mesh, in_specs=in_specs, out_specs=out_specs, check_vma=False)
```

```python
import functools
import math

import jax
import jax.numpy as jnp
import numpy as np
from jax import lax
from jax.experimental import pallas as pl
from jax.experimental.pallas import tpu as pltpu
from jax.sharding import PartitionSpec as P

HEADS = 16
HEAD_DIM = 48
PAIRS = HEADS // 2
PAIR = 2 * HEAD_DIM
VIEW = 256
STRIDE = 4
WINDOW = 8
ROWS = 8
COLS = 16
TOKENS = ROWS * COLS
WIDTH = 768
HIDDEN = 3072
N_GX = 32
N_GY = 4
N_DEV = N_GX * N_GY
GROUP = N_DEV // 2
AXES = ("gx", "gy")
BF = jnp.bfloat16
F32 = jnp.float32
SCALE = 1.0 / math.sqrt(HEAD_DIM)
SCALE_LOG2 = SCALE * math.log2(math.e)
MARK = 1e30
LIMIT = 1e29
HIDE = -1e30
CHUNK = 256
MLP_CHUNK = 512
epsilon = 1e-05

PIECES = ((0, -1), (0, 1), (-1, 0), (-1, -1), (-1, 1), (1, 0), (1, -1), (1, 1))
SIZES = [TOKENS if col_step == 0 else TOKENS // 2 for _, col_step in PIECES]
STARTS = [TOKENS + sum(SIZES[:i]) for i in range(len(SIZES))]
NEAR = TOKENS + sum(SIZES)
SIDE = TOKENS // 2
BAND = TOKENS + 2 * SIDE
MOVED = (SIDE, SIDE, BAND, BAND)
MOVED_STARTS = [TOKENS + sum(MOVED[:i]) for i in range(4)]
FAR_OWN = (ROWS // STRIDE) * (COLS // STRIDE)
FAR_HALF = GROUP * FAR_OWN
FAR = 2 * FAR_HALF
FAR_ROWS = [COLS * STRIDE * r + STRIDE * c for r in range(ROWS // STRIDE) for c in range(COLS // STRIDE)]
HALF = 2 * WIDTH
PART = HIDDEN // 2
HID, GPRE, GOUT, SWAP = WIDTH, WIDTH + PART, WIDTH + 2 * PART, 2 * WIDTH + 2 * PART
QUARTER = PART // 4
SHARE = HALF // GROUP
PLANE = GROUP // 4
PLANE_ROWS = 2 * QUARTER // PLANE


def nt(left_op, right_op):
    return lax.dot_general(left_op, right_op, (((1,), (1,)), ((), ())), preferred_element_type=F32)


def tn(left_op, right_op):
    return lax.dot_general(left_op, right_op, (((0,), (0,)), ((), ())), preferred_element_type=F32)


def product(left_op, right_op):
    return jnp.dot(left_op, right_op, preferred_element_type=F32)


CORE_PAIRS = [(i, i ^ 1) for i in range(N_DEV)]
SAME_CORE = [[i for i in range(N_DEV) if i % 2 == core] for core in (0, 1)]


def sent(value, pairs):
    return lax.ppermute(value, AXES, pairs)


def grid_pairs(row_step, col_step):
    pairs = []
    for gx in range(N_GX):
        for gy in range(N_GY):
            sx, sy = gx + col_step, gy + row_step
            if 0 <= sx < N_GX and 0 <= sy < N_GY:
                pairs.append((sx * N_GY + sy, gx * N_GY + gy))
    return pairs


def exchanged(cells):
    return lax.all_to_all(cells, AXES, 0, 0, tiled=True, axis_index_groups=SAME_CORE)


def coords(flat):
    core, x_hi, z, x_lo, y = flat & 1, (flat >> 1) & 1, (flat >> 2) & 3, (flat >> 4) & 1, flat >> 5
    return (x_hi * 2 + x_lo, y, z, core)


def flat_of(place):
    x, y, z, core = place
    return y * 32 + (x & 1) * 16 + z * 4 + (x >> 1) * 2 + core


ORDER = {0: (2, 1, 0), 1: (0, 2, 1)}


def ring_pairs(stage, shift):
    pairs = []
    for i in range(N_DEV):
        place = list(coords(i))
        axis = ORDER[place[3]][stage]
        place[axis] = (place[axis] + shift) % 4
        pairs.append((i, flat_of(place)))
    return pairs


def plane_groups():
    groups = {}
    for i in range(N_DEV):
        place = coords(i)
        first, second, third = ORDER[place[3]]
        key = (place[3], place[first])
        groups.setdefault(key, []).append((place[second], place[third], i))
    return [[i for *_, i in sorted(group)] for group in groups.values()]


WHOLE = pl.BlockSpec(memory_space=pltpu.VMEM)
SCALARS = pl.BlockSpec(memory_space=pltpu.SMEM)


def params(mebibytes):
    return pltpu.CompilerParams(vmem_limit_bytes=mebibytes * 1024 * 1024)


def shape(*dims_and_type):
    return jax.ShapeDtypeStruct(dims_and_type[:-1], dims_and_type[-1])


def in_hbm(array):
    return pltpu.with_memory_space_constraint(array, pltpu.HBM)


def fixed(*dims):
    return pl.BlockSpec(dims, lambda p: (0,) * len(dims))


def lanes(rows, cols):
    return pl.BlockSpec((rows, cols), lambda p: (0, p))


def sublanes(rows, cols):
    return pl.BlockSpec((rows, cols), lambda p: (p, 0))


def normalized(inputs):
    centered = inputs - jnp.mean(inputs, axis=1, keepdims=True)
    scale = lax.rsqrt(jnp.mean(centered * centered, axis=1, keepdims=True) + epsilon)
    return centered * scale, scale


def norm_back(grads, xhat, scale, gain):
    scaled = grads * gain
    inputs = scale * (
        scaled
        - jnp.mean(scaled, axis=1, keepdims=True)
        - xhat * jnp.mean(scaled * xhat, axis=1, keepdims=True)
    )
    return (
        inputs,
        jnp.sum(grads * xhat, axis=0, keepdims=True),
        jnp.sum(grads, axis=0, keepdims=True),
    )


def flag_column(flag_ref):
    row = lax.broadcasted_iota(jnp.int32, (TOKENS, ROWS), 0) // COLS
    block = lax.broadcasted_iota(jnp.int32, (TOKENS, ROWS), 1)
    rows = product(jnp.where(row == block, 1.0, 0.0).astype(BF), flag_ref[...].astype(F32).astype(BF))
    token = lax.broadcasted_iota(jnp.int32, (TOKENS, COLS), 0) % COLS
    col = lax.broadcasted_iota(jnp.int32, (TOKENS, COLS), 1)
    return jnp.sum(jnp.where(token == col, rows, 0.0), axis=1, keepdims=True)


def pre_kernel(x_ref, flag_ref, gain_ref, shift_ref, act_ref, marked_ref, spread_ref):
    gain, shift = gain_ref[...].reshape(1, WIDTH), shift_ref[...].reshape(1, WIDTH)
    xhat, _ = normalized(x_ref[...].astype(F32))
    act = (xhat * gain + shift).astype(BF)
    act_ref[...] = act
    marked = jnp.where(flag_column(flag_ref) > 0.5, act.astype(F32), MARK).astype(BF)
    marked_ref[...] = marked
    number = lax.broadcasted_iota(jnp.int32, (2 * FAR_OWN, TOKENS), 0) % FAR_OWN
    token = lax.broadcasted_iota(jnp.int32, (2 * FAR_OWN, TOKENS), 1)
    wanted = number // STRIDE * (COLS * STRIDE) + number % STRIDE * STRIDE
    chosen = product(jnp.where(token == wanted, 1.0, 0.0).astype(BF), marked).astype(BF)
    for k in range(GROUP // 2):
        spread_ref[2 * FAR_OWN * k : 2 * FAR_OWN * (k + 1), :] = chosen


def pre(arrays):
    return pl.pallas_call(
        pre_kernel,
        in_specs=[WHOLE] * 4,
        out_specs=[WHOLE] * 3,
        out_shape=[shape(TOKENS, WIDTH, BF), shape(TOKENS, WIDTH, BF), shape(FAR_HALF, WIDTH, BF)],
        compiler_params=params(16),
        cost_estimate=pl.CostEstimate(
            flops=10_000_000_000, bytes_accessed=2_000_000, transcendentals=TOKENS
        ),
        name="pre",
    )(*arrays)


def band_kernel(marked_ref, l_ref, r_ref, gain_ref, shift_ref, band_ref):
    gain, shift = gain_ref[...].reshape(1, WIDTH), shift_ref[...].reshape(1, WIDTH)
    band_ref[:TOKENS, :] = marked_ref[...]
    for side_ref, start in ((l_ref, TOKENS), (r_ref, TOKENS + SIDE)):
        side = side_ref[...].astype(F32)
        xhat, _ = normalized(jnp.where(side < LIMIT, side, 0.0))
        side = jnp.where(side < LIMIT, xhat * gain + shift, MARK)
        band_ref[start : start + SIDE, :] = side.astype(BF)


def view_of(pair):
    start = jnp.minimum(pair * PAIR // 128 * 128, WIDTH - VIEW)
    return pl.ds(pl.multiple_of(start, 128), VIEW), pair * PAIR - start


def halves(block, begin):
    wide = block.astype(F32)
    lane = lax.broadcasted_iota(jnp.int32, wide.shape, 1) - begin
    first = jnp.where((lane >= 0) & (lane < HEAD_DIM), wide, 0.0).astype(BF)
    second = jnp.where((lane >= HEAD_DIM) & (lane < PAIR), wide, 0.0).astype(BF)
    return jnp.concatenate([first, second], axis=0)


def own_rows(wide):
    return jnp.concatenate([wide[:HEAD_DIM, :TOKENS], wide[HEAD_DIM:, TOKENS:]], axis=0)


def rows_of(pair):
    return pl.ds(pl.multiple_of(pair * PAIR, 32), PAIR)


def folded(tile, op):
    return op(tile.reshape(tile.shape[0] // 8, 8, tile.shape[1]), axis=0)


def attended_part(query_rows, k_ref, flip, view, bias_ref, t_ref, e_ref):
    count = k_ref.shape[0]
    top = jnp.full((8, 2 * TOKENS), HIDE, F32)
    for start in range(0, count, CHUNK):
        rows = pl.ds(start, CHUNK)
        bias = bias_ref[rows, :]
        tile = nt(k_ref[rows, view], query_rows) * SCALE_LOG2
        tile = tile + jnp.concatenate([bias, bias], axis=1)
        t_ref[rows, :] = tile
        top = jnp.maximum(top, folded(tile, jnp.max))
    top = jnp.max(top, axis=0, keepdims=True)
    total = jnp.zeros((8, 2 * TOKENS), F32)
    for start in range(0, count, CHUNK):
        rows = pl.ds(start, CHUNK)
        tile = jnp.exp2(t_ref[rows, :] - top)
        total = total + folded(tile, jnp.sum)
        e_ref[rows, :] = tile.astype(BF)
    total = jnp.sum(total, axis=0, keepdims=True)
    return top, total, own_rows(product(flip, e_ref[...]))


def near_kernel(
    exists_ref, act_ref, band_ref, u_ref, d_ref, flag_ref, log_ref, wq_ref, wk_ref, wv_ref,
    all_ref, bias_ref, q_ref, k_ref, v_ref, top_ref, total_ref, sum_ref, t_ref, p_ref, flip_ref,
):
    pair = pl.program_id(0)

    @pl.when(pair == 0)
    def _():
        all_ref[:TOKENS, :] = act_ref[...]
        row = lax.broadcasted_iota(jnp.int32, (TOKENS, TOKENS), 0)
        col = lax.broadcasted_iota(jnp.int32, (TOKENS, TOKENS), 1)
        seen = jnp.where(row == col, 1.0, flag_column(flag_ref))
        bias_ref[:TOKENS, :] = jnp.where(seen > 0.5, log_ref[:TOKENS, :], HIDE)
        for i, (start, size) in enumerate(zip(STARTS, SIZES, strict=True)):
            rows = slice(start, start + size)
            moved, begin = start // BAND, start % BAND
            piece = (band_ref, u_ref, d_ref)[moved][begin : begin + size, :].astype(F32)
            all_ref[rows, :] = jnp.where(piece < LIMIT, piece, 0.0).astype(BF)
            seen = jnp.where(piece[:, :128] < LIMIT, 1.0, 0.0)[:, :1] * exists_ref[i]
            bias_ref[rows, :] = jnp.where(seen > 0.5, log_ref[rows, :], HIDE)
        q_ref[...] = product(act_ref[...], wq_ref[...]).astype(BF)
        k_ref[...] = product(all_ref[...], wk_ref[...]).astype(BF)
        values = product(all_ref[...], wv_ref[...]).astype(BF)
        v_ref[...] = values
        flip_ref[...] = values.T

    view, begin = view_of(pair)
    top, total, wide = attended_part(
        halves(q_ref[:, view], begin), k_ref, flip_ref[rows_of(pair), :], view, bias_ref, t_ref, p_ref
    )
    top_ref[pair] = top
    total_ref[pair] = total
    sum_ref[pair] = wide


def attend_near(exists, act, bands, flags, log_weight, wq, wk, wv):
    return pl.pallas_call(
        near_kernel,
        grid=(PAIRS,),
        in_specs=[SCALARS] + [WHOLE] * 9,
        out_specs=[WHOLE] * 8,
        out_shape=[
            shape(NEAR, WIDTH, BF),
            shape(NEAR, TOKENS, F32),
            shape(TOKENS, WIDTH, BF),
            shape(NEAR, WIDTH, BF),
            shape(NEAR, WIDTH, BF),
            shape(PAIRS, 1, 2 * TOKENS, F32),
            shape(PAIRS, 1, 2 * TOKENS, F32),
            shape(PAIRS, PAIR, TOKENS, F32),
        ],
        scratch_shapes=[
            pltpu.VMEM((NEAR, 2 * TOKENS), F32),
            pltpu.VMEM((NEAR, 2 * TOKENS), BF),
            pltpu.VMEM((WIDTH, NEAR), BF),
        ],
        compiler_params=params(14),
        cost_estimate=pl.CostEstimate(
            flops=10_000_000_000, bytes_accessed=12_000_000, transcendentals=0
        ),
        name="attend_near",
    )(exists, act, *bands, flags, log_weight, wq, wk, wv)


def far_kernel(
    own_ref, other_ref, x_ref, q_ref, wk_ref, wv_ref, wo_ref, top_ref, total_ref, sum_ref,
    all_ref, bias_ref, k_ref, v_ref, o_ref, lse_ref, mid_ref, t_ref, e_ref, flip_ref, out_ref,
):
    pair = pl.program_id(0)

    @pl.when(pair == 0)
    def _():
        for start, half_ref in ((0, own_ref), (FAR_HALF, other_ref)):
            rows = slice(start, start + FAR_HALF)
            piece = half_ref[...].astype(F32)
            all_ref[rows, :] = jnp.where(piece < LIMIT, piece, 0.0).astype(BF)
            seen = jnp.where(piece[:, :128] < LIMIT, 0.0, HIDE)[:, :1]
            bias_ref[rows, :] = jnp.broadcast_to(seen, (FAR_HALF, TOKENS))
        k_ref[...] = product(all_ref[...], wk_ref[...]).astype(BF)
        values = product(all_ref[...], wv_ref[...]).astype(BF)
        v_ref[...] = values
        flip_ref[...] = values.T

    view, begin = view_of(pair)
    far_top, far_total, far_sum = attended_part(
        halves(q_ref[:, view], begin), k_ref, flip_ref[rows_of(pair), :], view, bias_ref, t_ref, e_ref
    )
    near_top = top_ref[pair]
    top = jnp.maximum(near_top, far_top)
    near_part, far_part = jnp.exp2(near_top - top), jnp.exp2(far_top - top)
    total = total_ref[pair] * near_part + far_total * far_part
    near_part, far_part = near_part / total, far_part / total
    near_sum = sum_ref[pair]
    out_ref[rows_of(pair), :] = jnp.concatenate(
        [
            near_sum[rows] * near_part[:, cols] + far_sum[rows] * far_part[:, cols]
            for rows, cols in (
                (slice(0, HEAD_DIM), slice(0, TOKENS)),
                (slice(HEAD_DIM, PAIR), slice(TOKENS, 2 * TOKENS)),
            )
        ],
        axis=0,
    )
    lse_ref[pair] = top + jnp.log2(total)

    @pl.when(pair == PAIRS - 1)
    def _():
        outs = out_ref[...].T
        o_ref[...] = outs
        mid_ref[...] = x_ref[...].astype(F32) + product(outs.astype(BF), wo_ref[...])


def attend_far(own, other, embeddings, queries, wk, wv, wo, tops, totals, sums):
    return pl.pallas_call(
        far_kernel,
        grid=(PAIRS,),
        in_specs=[WHOLE] * 10,
        out_specs=[WHOLE] * 7,
        out_shape=[
            shape(FAR, WIDTH, BF),
            shape(FAR, TOKENS, F32),
            shape(FAR, WIDTH, BF),
            shape(FAR, WIDTH, BF),
            shape(TOKENS, WIDTH, F32),
            shape(PAIRS, 1, 2 * TOKENS, F32),
            shape(TOKENS, WIDTH, F32),
        ],
        scratch_shapes=[
            pltpu.VMEM((FAR, 2 * TOKENS), F32),
            pltpu.VMEM((FAR, 2 * TOKENS), BF),
            pltpu.VMEM((WIDTH, FAR), BF),
            pltpu.VMEM((WIDTH, TOKENS), F32),
        ],
        compiler_params=params(16),
        cost_estimate=pl.CostEstimate(
            flops=12_000_000_000, bytes_accessed=12_000_000, transcendentals=HEADS * FAR * TOKENS
        ),
        name="attend_far",
    )(own, other, embeddings, queries, wk, wv, wo, tops, totals, sums)


def mlp_kernel(
    core_ref, mid_ref, gain_ref, shift_ref, gout_ref, wup_ref, wdown_ref, mixed_ref, keep_ref,
    send_ref, gact_ref, act_ref, acc_ref,
):
    step = pl.program_id(0)
    steps = HIDDEN // MLP_CHUNK

    @pl.when(step == 0)
    def _():
        middle = mid_ref[...]
        xhat, _ = normalized(middle)
        gain, shift = gain_ref[...].reshape(1, WIDTH), shift_ref[...].reshape(1, WIDTH)
        act = (xhat * gain + shift).astype(BF)
        act_ref[...] = act
        acc_ref[...] = middle
        gact_ref[...] = jnp.zeros_like(gact_ref)
        for out_ref in (keep_ref, send_ref):
            out_ref[:, :HID] = act
            out_ref[:, GOUT:] = gout_ref[...]

    pre_act = product(act_ref[...], wup_ref[...])
    below = 0.5 * (1.0 + lax.erf(pre_act * math.sqrt(0.5)))
    slope = below + pre_act * (jnp.exp(-0.5 * pre_act * pre_act) * (1.0 / math.sqrt(2.0 * math.pi)))
    hidden = (pre_act * below).astype(BF)
    grad_pre = (nt(gout_ref[...], wdown_ref[...]) * slope).astype(BF)
    acc_ref[...] += product(hidden, wdown_ref[...])
    gact_ref[...] += nt(grad_pre, wup_ref[...])
    col = pl.multiple_of(step % (steps // 2) * MLP_CHUNK, 128)
    mine = step // (steps // 2) == core_ref[0]
    for is_mine, out_ref in ((True, keep_ref), (False, send_ref)):

        @pl.when(mine == is_mine)
        def _(out_ref=out_ref):
            out_ref[:, pl.ds(HID + col, MLP_CHUNK)] = hidden
            out_ref[:, pl.ds(GPRE + col, MLP_CHUNK)] = grad_pre

    @pl.when(step == steps - 1)
    def _():
        mixed_ref[...] = acc_ref[...].astype(BF)


def mlp(core, middle, gain, shift, grad_out, w_up, w_down):
    return pl.pallas_call(
        mlp_kernel,
        grid=(HIDDEN // MLP_CHUNK,),
        in_specs=[
            SCALARS,
            fixed(TOKENS, WIDTH),
            fixed(WIDTH),
            fixed(WIDTH),
            fixed(TOKENS, WIDTH),
            lanes(WIDTH, MLP_CHUNK),
            sublanes(MLP_CHUNK, WIDTH),
        ],
        out_specs=[
            fixed(TOKENS, WIDTH),
            fixed(TOKENS, SWAP),
            fixed(TOKENS, SWAP),
            fixed(TOKENS, WIDTH),
        ],
        out_shape=[
            shape(TOKENS, WIDTH, BF),
            shape(TOKENS, SWAP, BF),
            shape(TOKENS, SWAP, BF),
            shape(TOKENS, WIDTH, F32),
        ],
        scratch_shapes=[pltpu.VMEM((TOKENS, WIDTH), BF), pltpu.VMEM((TOKENS, WIDTH), F32)],
        compiler_params=params(20),
        cost_estimate=pl.CostEstimate(
            flops=8 * TOKENS * WIDTH * HIDDEN,
            bytes_accessed=12_000_000,
            transcendentals=2 * TOKENS * HIDDEN,
        ),
        name="mlp",
    )(core, middle, gain, shift, grad_out, w_up, w_down)


def mlp_grads_kernel(spot_ref, keep_ref, got_ref, *refs):
    outs, both_ref = refs[:4], refs[4]
    both_ref[:TOKENS, :] = keep_ref[...]
    both_ref[TOKENS:, :] = got_ref[...]
    for step, out_ref in enumerate(outs):
        col = pl.multiple_of((spot_ref[0] + step) % 4 * QUARTER, 128)
        grad_pre = both_ref[:, pl.ds(GPRE + col, QUARTER)]
        hidden = both_ref[:, pl.ds(HID + col, QUARTER)]
        out_ref[:QUARTER, :] = tn(grad_pre, both_ref[:, :HID]).astype(BF)
        out_ref[QUARTER:, :] = tn(hidden, both_ref[:, GOUT:]).astype(BF)


def mid_kernel(
    o_ref, mid_ref, gact_ref, gain_ref, gout_ref, wo_ref, kn_ref, kf_ref, alln_ref, allf_ref,
    gwo_ref, gmid_ref, small_ref, gatt_ref, inner_ref, flip_ref, kflip_ref,
):
    xhat, scale = normalized(mid_ref[...])
    inputs, grad_gain, grad_shift = norm_back(
        gact_ref[...], xhat, scale, gain_ref[...].reshape(1, WIDTH)
    )
    grad_mid = gout_ref[...].astype(F32) + inputs
    gmid_ref[...] = grad_mid
    small_ref[...] = jnp.concatenate([grad_gain, grad_shift, jnp.zeros((6, WIDTH), F32)], axis=0)
    branch = grad_mid.astype(BF)
    grads = nt(branch, wo_ref[...]).astype(BF)
    gatt_ref[...] = grads
    gwo_ref[...] = tn(o_ref[...].astype(BF), branch).astype(BF)
    inner_ref[...] = (grads.astype(F32) * o_ref[...]).T
    flip_ref[:, :NEAR] = alln_ref[...].T
    flip_ref[:, NEAR:] = allf_ref[...].T
    kflip_ref[:, :NEAR] = kn_ref[...].T
    kflip_ref[:, NEAR:] = kf_ref[...].T


def back_kernel(
    q_ref, gatt_ref, inner_ref, lse_ref, kn_ref, vn_ref, kf_ref, vf_ref, biasn_ref, biasf_ref,
    flip_ref, kflip_ref, wq_ref, wk_ref, wv_ref,
    gwq_ref, gwk_ref, gwv_ref, gown_ref, l_ref, r_ref, u_ref, d_ref, gfar_ref,
    s_ref, p_ref, gq_ref, gk_ref, gv_ref, acc_ref,
):
    pair = pl.program_id(0)

    @pl.when(pair == 0)
    def _():
        gk_ref[...] = jnp.zeros_like(gk_ref)
        gv_ref[...] = jnp.zeros_like(gv_ref)

    view, begin = view_of(pair)
    query_rows = halves(q_ref[:, view], begin)
    grad_rows = halves(gatt_ref[:, view], begin)
    inner = inner_ref[rows_of(pair), :]
    inner = jnp.concatenate(
        [
            jnp.sum(inner[:HEAD_DIM], axis=0, keepdims=True),
            jnp.sum(inner[HEAD_DIM:], axis=0, keepdims=True),
        ],
        axis=1,
    )
    lse = lse_ref[pair]
    for k_ref, v_ref, bias_ref, offset in (
        (kn_ref, vn_ref, biasn_ref, 0),
        (kf_ref, vf_ref, biasf_ref, NEAR),
    ):
        for start in range(0, k_ref.shape[0], CHUNK):
            rows = pl.ds(start, CHUNK)
            bias = bias_ref[rows, :]
            tile = nt(k_ref[rows, view], query_rows) * SCALE_LOG2
            probs = jnp.exp2(tile + jnp.concatenate([bias, bias], axis=1) - lse)
            grad_probs = nt(v_ref[rows, view], grad_rows)
            there = pl.ds(offset + start, CHUNK)
            s_ref[there, :] = (probs * (grad_probs - inner)).astype(BF)
            p_ref[there, :] = probs.astype(BF)
    gk_ref[:, view] += (product(s_ref[...], query_rows) * SCALE).astype(BF)
    gv_ref[:, view] += product(p_ref[...], grad_rows).astype(BF)
    gq_ref[rows_of(pair), :] = own_rows(product(kflip_ref[rows_of(pair), :], s_ref[...])) * SCALE

    @pl.when(pair == PAIRS - 1)
    def _():
        grad_query = gq_ref[...].T.astype(BF)
        acc_ref[...] = nt(gk_ref[...], wk_ref[...])
        acc_ref[...] += nt(gv_ref[...], wv_ref[...])
        gown_ref[...] = acc_ref[:TOKENS, :] + nt(grad_query, wq_ref[...])
        for piece_ref, start, size in zip(
            (l_ref, r_ref, u_ref, d_ref), MOVED_STARTS, MOVED, strict=True
        ):
            piece_ref[...] = acc_ref[start : start + size, :].astype(BF)
        gfar_ref[...] = acc_ref[NEAR:, :]
        gwk_ref[...] = product(flip_ref[...], gk_ref[...]).astype(BF)
        gwv_ref[...] = product(flip_ref[...], gv_ref[...]).astype(BF)
        gwq_ref[...] = product(flip_ref[:, :TOKENS], grad_query).astype(BF)


def attend_back(arrays):
    count = NEAR + FAR
    return pl.pallas_call(
        back_kernel,
        grid=(PAIRS,),
        in_specs=[WHOLE] * 15,
        out_specs=[WHOLE] * 9,
        out_shape=[shape(WIDTH, WIDTH, BF)] * 3
        + [shape(TOKENS, WIDTH, F32)]
        + [shape(size, WIDTH, BF) for size in MOVED]
        + [shape(FAR, WIDTH, F32)],
        scratch_shapes=[
            pltpu.VMEM((count, 2 * TOKENS), BF),
            pltpu.VMEM((count, 2 * TOKENS), BF),
            pltpu.VMEM((WIDTH, TOKENS), F32),
            pltpu.VMEM((count, WIDTH), BF),
            pltpu.VMEM((count, WIDTH), BF),
            pltpu.VMEM((count, WIDTH), F32),
        ],
        compiler_params=params(26),
        cost_estimate=pl.CostEstimate(
            flops=20_000_000_000,
            bytes_accessed=30_000_000,
            transcendentals=HEADS * count * TOKENS,
        ),
        name="attend_back",
    )(*arrays)


def small_call(kernel, name, scalars, arrays, outs, scratch=(), flops=5_000_000_000):
    return pl.pallas_call(
        kernel,
        in_specs=[SCALARS] * len(scalars) + [WHOLE] * len(arrays),
        out_specs=[WHOLE] * len(outs),
        out_shape=outs,
        scratch_shapes=list(scratch),
        compiler_params=params(20),
        cost_estimate=pl.CostEstimate(flops=flops, bytes_accessed=0, transcendentals=0),
        name=name,
    )(*scalars, *arrays)


def far_place(core, cell):
    where = [0, 0, 0]
    for stage, axis in enumerate(ORDER[core]):
        where[axis] = cell // 4 ** (2 - stage) % 4
    return flat_of((*where, core)) // 2


def pack_kernel(core_ref, wq_ref, wk_ref, wv_ref, wo_ref, gfar_ref, keep_ref, send_ref):
    for mine, first_ref, second_ref in ((0, keep_ref, send_ref), (1, send_ref, keep_ref)):

        @pl.when(core_ref[0] == mine)
        def _(mine=mine, first_ref=first_ref, second_ref=second_ref):
            for core, out_ref, weights in (
                (0, first_ref, (wq_ref, wk_ref)),
                (1, second_ref, (wv_ref, wo_ref)),
            ):
                for group in range(16):
                    row = 4 * SHARE * group
                    start = 4 * (SHARE + FAR_OWN) * group
                    out_ref[start : start + 4 * SHARE, :] = weights[row // WIDTH][
                        row % WIDTH : row % WIDTH + 4 * SHARE, :
                    ]
                    base = 0 if core == mine else FAR_HALF
                    far = [base + FAR_OWN * far_place(core, 4 * group + k) for k in range(4)]
                    out_ref[start + 4 * SHARE : start + 4 * (SHARE + FAR_OWN), :] = jnp.concatenate(
                        [gfar_ref[f : f + FAR_OWN, :] for f in far], axis=0
                    ).astype(BF)


def split_kernel(layout, spot_ref, *refs):
    ins, outs, total_ref = refs[:-5], refs[-5:-1], refs[-1]
    if len(layout) == 1:
        rows = outs[0].shape[0]
        for step, out_ref in enumerate(outs):
            run = pl.ds(pl.multiple_of((spot_ref[0] + step) % 4 * rows, rows), rows)
            total = ins[0][run, :].astype(F32)
            for in_ref in ins[1:]:
                total = total + in_ref[run, :].astype(F32)
            out_ref[...] = total.astype(BF)
        return
    total = ins[0][...].astype(F32)
    for in_ref in ins[1:]:
        total = total + in_ref[...].astype(F32)
    total_ref[...] = total
    for step, out_ref in enumerate(outs):
        place = (spot_ref[0] + step) % 4
        runs = [
            total_ref[pl.ds(pl.multiple_of(start + place * (length // 4), 8), length // 4), :]
            for start, length in layout
        ]
        out_ref[...] = jnp.concatenate(runs, axis=0).astype(BF)


def split(spot, arrays, layout=None):
    rows, cols = arrays[0].shape
    return small_call(
        functools.partial(split_kernel, layout or ((0, rows),)),
        "split",
        [spot],
        arrays,
        [shape(rows // 4, cols, BF)] * 4,
        [pltpu.VMEM((rows if layout else 8, cols), F32)],
    )


def join_kernel(extra, spot_ref, *refs):
    ins, out_ref, whole_ref = refs[:4], refs[4], refs[5]
    rows = ins[0].shape[0] - extra
    rest = 0.0
    for step, in_ref in enumerate(ins):
        start = pl.multiple_of((spot_ref[0] + step) % 4 * rows, 8)
        part = in_ref[...].astype(F32)
        whole_ref[pl.ds(start, rows), :] = part[:rows]
        rest = rest + part[rows:]
    if extra:
        whole_ref[4 * rows :, :] = rest
    out_ref[...] = whole_ref[...].astype(BF)


def join(spot, arrays, extra=0):
    rows, cols = arrays[0].shape
    out = 4 * (rows - extra) + extra
    return small_call(
        functools.partial(join_kernel, extra), "join", [spot], arrays, [shape(out, cols, BF)],
        [pltpu.VMEM((out, cols), F32)],
    )[0]


def add_kernel(*refs):
    total = refs[0][...].astype(F32)
    for in_ref in refs[1:-1]:
        total = total + in_ref[...].astype(F32)
    refs[-1][...] = total.astype(BF)


def add(arrays):
    return small_call(add_kernel, "add", [], arrays, [shape(*arrays[0].shape, BF)])[0]


def fold_kernel(l_ref, r_ref, above_ref, below_ref, left_ref, right_ref):
    for piece_ref, out_ref, start in ((l_ref, left_ref, TOKENS), (r_ref, right_ref, TOKENS + SIDE)):
        total = piece_ref[...].astype(F32)
        for band_ref in (above_ref, below_ref):
            total = total + band_ref[start : start + SIDE, :].astype(F32)
        out_ref[...] = total.astype(BF)


def tail_kernel(
    cell_ref, cell1_ref, cell2_ref, cell3_ref, gown_ref, above_ref, below_ref, left_ref, right_ref, x_ref, gain_ref, gmid_ref,
    small_ref, gx_ref, out_ref,
):
    total = gown_ref[...]
    for band_ref in (above_ref, below_ref):
        total = total + band_ref[:TOKENS, :].astype(F32)
    left, right = left_ref[...].astype(F32), right_ref[...].astype(F32)
    sides = []
    for r in range(ROWS):
        sides += [left[WINDOW * r : WINDOW * (r + 1)], right[WINDOW * r : WINDOW * (r + 1)]]
    total = total + jnp.concatenate(sides, axis=0)
    summed = cell_ref[...].astype(F32)
    for other_ref in (cell1_ref, cell2_ref, cell3_ref):
        summed = summed + other_ref[...].astype(F32)
    far = summed[SHARE:]
    token = lax.broadcasted_iota(jnp.int32, (TOKENS, WIDTH), 0)
    for k, where in enumerate(FAR_ROWS):
        total = total + jnp.where(token == where, far[k : k + 1, :], 0.0)
    xhat, scale = normalized(x_ref[...].astype(F32))
    inputs, grad_gain, grad_shift = norm_back(
        total, xhat, scale, gain_ref[...].reshape(1, WIDTH)
    )
    gx_ref[...] = gmid_ref[...] + inputs
    small = jnp.concatenate(
        [grad_gain, grad_shift, small_ref[0:2, :], jnp.zeros((4, WIDTH), F32)], axis=0
    )
    out_ref[...] = jnp.concatenate([summed[:SHARE], small], axis=0).astype(BF)


def fetched_call(kernel, name, arrays, outs):
    return pl.pallas_call(
        kernel,
        grid=(1,),
        in_specs=[fixed(*a.shape) for a in arrays],
        out_specs=[fixed(*out.shape) for out in outs],
        out_shape=outs,
        compiler_params=params(20),
        cost_estimate=pl.CostEstimate(flops=5_000_000_000, bytes_accessed=0, transcendentals=0),
        name=name,
    )(*map(in_hbm, arrays))


def finish_kernel(core_ref, own_ref, other_ref, wq_ref, wk_ref, wv_ref, wo_ref, vectors_ref):
    for mine, first_ref, second_ref in ((0, own_ref, other_ref), (1, other_ref, own_ref)):

        @pl.when(core_ref[0] == mine)
        def _(first_ref=first_ref, second_ref=second_ref):
            wq_ref[...] = first_ref[:WIDTH, :].astype(F32)
            wk_ref[...] = first_ref[WIDTH:HALF, :].astype(F32)
            wv_ref[...] = second_ref[:WIDTH, :].astype(F32)
            wo_ref[...] = second_ref[WIDTH:HALF, :].astype(F32)

    vectors_ref[...] = own_ref[...].astype(F32)[HALF:] + other_ref[...].astype(F32)[HALF:]


def plane_sum_kernel(cells_ref, out_ref):
    total = cells_ref[:PLANE_ROWS, :].astype(F32)
    for k in range(1, PLANE):
        total = total + cells_ref[PLANE_ROWS * k : PLANE_ROWS * (k + 1), :].astype(F32)
    total = total.astype(BF)
    for k in range(PLANE):
        out_ref[PLANE_ROWS * k : PLANE_ROWS * (k + 1), :] = total


def finish_mlp_kernel(place_ref, *refs):
    ins, (up_ref, down_ref) = refs[:8], refs[8:]
    for k, in_ref in enumerate(ins):

        @pl.when(pl.program_id(0) == k)
        def _(in_ref=in_ref):
            up_ref[...] = in_ref[:QUARTER, :].T.astype(F32)
            down_ref[...] = in_ref[QUARTER:, :].astype(F32)


def finish_mlp(places, pieces):
    return pl.pallas_call(
        finish_mlp_kernel,
        grid_spec=pltpu.PrefetchScalarGridSpec(
            num_scalar_prefetch=1,
            grid=(8,),
            in_specs=[WHOLE] * 8,
            out_specs=[
                pl.BlockSpec((WIDTH, QUARTER), lambda k, place: (0, place[k])),
                pl.BlockSpec((QUARTER, WIDTH), lambda k, place: (place[k], 0)),
            ],
        ),
        out_shape=[shape(WIDTH, HIDDEN, F32), shape(HIDDEN, WIDTH, F32)],
        compiler_params=params(20),
        cost_estimate=pl.CostEstimate(flops=0, bytes_accessed=0, transcendentals=0),
        name="finish_mlp",
    )(places, *pieces)


def after(*values):
    return lax.optimization_barrier(values)


def piece_of(block, col_step):
    if col_step == 0:
        return block
    return block[:, WINDOW:] if col_step < 0 else block[:, : COLS - WINDOW]


def window_weights():
    rows, cols = np.mgrid[0:ROWS, 0:COLS]
    query = (rows.reshape(-1), cols.reshape(-1))
    key_rows, key_cols = [rows.reshape(-1)], [cols.reshape(-1)]
    for row_step, col_step in PIECES:
        key_rows.append(piece_of(rows, col_step).reshape(-1) + row_step * ROWS)
        key_cols.append(piece_of(cols, col_step).reshape(-1) + col_step * COLS)
    row_gap = np.concatenate(key_rows)[:, None] - query[0][None]
    col_gap = np.concatenate(key_cols)[:, None] - query[1][None]
    dense = (np.abs(row_gap) <= WINDOW) & (np.abs(col_gap) <= WINDOW)
    dilated = dense & (row_gap % 2 == 0) & (col_gap % 2 == 0)
    return np.where(dense, np.where(dilated, 1.0, 0.0), HIDE).astype(np.float32)


def local(
    embeddings,
    tile_valid,
    w_query,
    w_key,
    w_value,
    w_out,
    w_up,
    w_down,
    gain_attn,
    shift_attn,
    gain_mlp,
    shift_mlp,
    cotangent,
):
    gx, gy = lax.axis_index("gx"), lax.axis_index("gy")
    x, y, z, core = (v.astype(jnp.int32) for v in coords(lax.axis_index(AXES)))
    spots = [
        jnp.where(core == 0, (x, y, z)[ORDER[0][stage]], (x, y, z)[ORDER[1][stage]]).reshape(1)
        for stage in range(3)
    ]
    core = core.reshape(1)
    their_spot = jnp.where(core == 0, (x, y, z)[ORDER[1][0]], (x, y, z)[ORDER[0][0]])
    steps = jnp.arange(4, dtype=jnp.int32)
    places = jnp.concatenate(
        [4 * core + (spots[0] + steps) % 4, 4 * (1 - core) + (their_spot + steps) % 4]
    )
    exists = jnp.stack(
        [
            (gy + row_step >= 0)
            & (gy + row_step < N_GY)
            & (gx + col_step >= 0)
            & (gx + col_step < N_GX)
            for row_step, col_step in PIECES
        ]
    ).astype(F32)
    tokens = embeddings.reshape(TOKENS, WIDTH)

    raw = jnp.where(tile_valid[:, :, None] > 0, embeddings, jnp.asarray(MARK, BF))
    left = sent(raw[:, WINDOW:].reshape(SIDE, WIDTH), grid_pairs(0, -1))
    right = sent(raw[:, :WINDOW].reshape(SIDE, WIDTH), grid_pairs(0, 1))
    act, marked, spread = pre([tokens, tile_valid, gain_attn, shift_attn])
    band = small_call(
        band_kernel,
        "band",
        [],
        [marked, left, right, gain_attn, shift_attn],
        [shape(BAND, WIDTH, BF)],
    )[0]
    spread, band = after(spread, band)
    far_own = exchanged(spread.reshape(GROUP, FAR_OWN, WIDTH)).reshape(FAR_HALF, WIDTH)
    bands = [band, sent(band, grid_pairs(-1, 0)), sent(band, grid_pairs(1, 0))]
    near, bias_near, queries, k_near, v_near, tops, totals, sums = attend_near(
        exists, act, bands, tile_valid, jnp.asarray(window_weights()), w_query, w_key, w_value
    )
    far_own, sums = after(far_own, sums)
    far_other = sent(far_own, CORE_PAIRS)
    far, bias_far, k_far, v_far, outs, lse, middle = attend_far(
        far_own, far_other, tokens, queries, w_key, w_value, w_out, tops, totals, sums
    )
    grad_out = cotangent.reshape(TOKENS, WIDTH)
    mixed, keep, send, grad_act = mlp(
        core, middle, gain_mlp, shift_mlp, grad_out, w_up, w_down
    )
    def rest(operands):
        (
            keep, send, outs, middle, grad_act, gain_mlp, gain_attn, grad_out, tokens, queries, lse,
            k_near, v_near, k_far, v_far, bias_near, bias_far, near, far,
            w_query, w_key, w_value, w_out, core, spots, places,
        ) = operands
        swapped = sent(send, CORE_PAIRS)
        grad_wo, grad_mid, small, grad_att, inner, flip, key_flip = small_call(
            mid_kernel,
            "mid",
            [],
            [outs, middle, grad_act, gain_mlp, grad_out, w_out, k_near, k_far, near, far],
            [shape(WIDTH, WIDTH, BF), shape(TOKENS, WIDTH, F32), shape(8, WIDTH, F32)]
            + [shape(TOKENS, WIDTH, BF), shape(WIDTH, TOKENS, F32)]
            + [shape(WIDTH, NEAR + FAR, BF)] * 2,
        )
        swapped, grad_att = after(swapped, grad_att)
        quarter = shape(2 * QUARTER, WIDTH, BF)
        mlp_parts = small_call(
            mlp_grads_kernel,
            "mlp_grads",
            [spots[0]],
            [keep, swapped],
            [quarter] * 4,
            [pltpu.VMEM((2 * TOKENS, SWAP), BF)],
        )

        def around(stage, parts):
            return [parts[0]] + [sent(parts[step], ring_pairs(stage, step)) for step in (2, 1, 3)]

        def gathered(stage, part):
            got = {step: sent(part, ring_pairs(stage, -step)) for step in (2, 1, 3)}
            return [part, got[1], got[2], got[3]]

        def in_plane(cells):
            return lax.all_to_all(
                cells.reshape(PLANE, PLANE_ROWS, WIDTH), AXES, 0, 0, tiled=True,
                axis_index_groups=plane_groups(),
            ).reshape(2 * QUARTER, WIDTH)

        mlp_held = around(0, mlp_parts)
        grad_att, _ = after(grad_att, mlp_parts[0])
        grad_wq, grad_wk, grad_wv, grad_own, piece_left, piece_right, piece_up, piece_down, grad_far = (
            attend_back(
                [
                    queries, grad_att, inner, lse, k_near, v_near, k_far, v_far, bias_near, bias_far,
                    flip, key_flip, w_query, w_key, w_value,
                ]
            )
        )
        mlp_held[0], grad_own = after(mlp_held[0], grad_own)
        mlp_sum = add(mlp_held)
        mlp_cells = in_plane(mlp_sum)
        grad_far, piece_up, piece_down, _ = after(grad_far, piece_up, piece_down, mlp_sum)
        packed = small_call(
            pack_kernel,
            "pack",
            [core],
            [grad_wq, grad_wk, grad_wv, grad_wo, grad_far],
            [shape(HALF + FAR_HALF, WIDTH, BF)] * 2,
        )
        held = [packed[0], sent(packed[1], CORE_PAIRS)]
        above = sent(piece_down, grid_pairs(-1, 0))
        below = sent(piece_up, grid_pairs(1, 0))
        parts = split(spots[0], held)
        held = around(0, parts)
        mlp_cells, _ = after(mlp_cells, parts[0])
        mlp_cells = small_call(plane_sum_kernel, "plane_sum", [], [mlp_cells], [quarter])[0]
        mlp_own = in_plane(mlp_cells)
        piece_left, _ = after(piece_left, mlp_cells)
        side = shape(SIDE, WIDTH, BF)
        piece_left, piece_right = fetched_call(
            fold_kernel, "fold", [piece_left, piece_right, above, below], [side, side]
        )
        from_right = sent(piece_left, grid_pairs(0, 1))
        from_left = sent(piece_right, grid_pairs(0, -1))
        held[0], _ = after(held[0], piece_left)
        parts = split(spots[1], held)
        held = around(1, parts)
        held[0], mlp_own = after(held[0], mlp_own)
        parts = split(spots[2], held, ((0, 4 * SHARE), (4 * SHARE, 4 * FAR_OWN)))
        held = around(2, parts)
        mlp_own, _ = after(mlp_own, parts[0])
        mlp_held = gathered(0, mlp_own)
        grad_inputs, cell = fetched_call(
            tail_kernel,
            "tail",
            held
            + [grad_own, above, below, from_left, from_right, tokens, gain_attn, grad_mid, small],
            [shape(TOKENS, WIDTH, F32), shape(SHARE + 8, WIDTH, BF)],
        )
        cell = join(spots[2], gathered(2, cell), 8)
        held = gathered(1, cell)
        held[0], *mlp_held = after(held[0], *mlp_held)
        cell = join(spots[1], held, 8)
        others = [sent(piece, CORE_PAIRS) for piece in mlp_held]
        held = gathered(0, cell)
        grad_up, grad_down = finish_mlp(places, mlp_held + others)
        held[0], _ = after(held[0], grad_up)
        cell = join(spots[0], held, 8)
        other = sent(cell, CORE_PAIRS)
        grad_wq, grad_wk, grad_wv, grad_wo, vectors = small_call(
            finish_kernel,
            "finish",
            [core],
            [cell, other],
            [shape(WIDTH, WIDTH, F32)] * 4 + [shape(8, WIDTH, F32)],
        )
        return grad_inputs, grad_up, grad_down, grad_wq, grad_wk, grad_wv, grad_wo, vectors

    def never(operands):
        return (
            jnp.zeros((TOKENS, WIDTH), F32),
            jnp.zeros((WIDTH, HIDDEN), F32),
            jnp.zeros((HIDDEN, WIDTH), F32),
            *[jnp.zeros((WIDTH, WIDTH), F32)] * 4,
            jnp.zeros((8, WIDTH), F32),
        )

    grad_inputs, grad_up, grad_down, grad_wq, grad_wk, grad_wv, grad_wo, vectors = lax.cond(
        gx < N_GX,
        rest,
        never,
        (
            keep, send, outs, middle, grad_act, gain_mlp, gain_attn, grad_out, tokens, queries, lse,
            k_near, v_near, k_far, v_far, bias_near, bias_far, near, far,
            w_query, w_key, w_value, w_out, core, spots, places,
        ),
    )
    return (
        mixed.reshape(ROWS, COLS, WIDTH),
        grad_inputs.reshape(ROWS, COLS, WIDTH),
        grad_wq,
        grad_wk,
        grad_wv,
        grad_wo,
        grad_up,
        grad_down,
        vectors[0],
        vectors[1],
        vectors[2],
        vectors[3],
    )


def solution(mesh):
    grid = P("gy", "gx", None)
    in_specs = (grid, P("gy", "gx")) + (P(),) * 10 + (grid,)
    out_specs = (grid, grid) + (P(),) * 10
    return jax.shard_map(local, mesh=mesh, in_specs=in_specs, out_specs=out_specs, check_vma=False)
```

```python
import functools
import math

import jax
import jax.numpy as jnp
import numpy as np
from jax import lax
from jax.experimental import pallas as pl
from jax.experimental.pallas import tpu as pltpu
from jax.sharding import PartitionSpec as P

HEADS = 16
HEAD_DIM = 48
PAIRS = HEADS // 2
PAIR = 2 * HEAD_DIM
VIEW = 256
STRIDE = 4
WINDOW = 8
ROWS = 8
COLS = 16
TOKENS = ROWS * COLS
WIDTH = 768
HIDDEN = 3072
N_GX = 32
N_GY = 4
N_DEV = N_GX * N_GY
GROUP = N_DEV // 2
AXES = ("gx", "gy")
BF = jnp.bfloat16
F32 = jnp.float32
SCALE = 1.0 / math.sqrt(HEAD_DIM)
SCALE_LOG2 = SCALE * math.log2(math.e)
MARK = 1e30
LIMIT = 1e29
HIDE = -1e30
CHUNK = 256
MLP_CHUNK = 512
epsilon = 1e-05

PIECES = ((0, -1), (0, 1), (-1, 0), (-1, -1), (-1, 1), (1, 0), (1, -1), (1, 1))
SIZES = [TOKENS if col_step == 0 else TOKENS // 2 for _, col_step in PIECES]
STARTS = [TOKENS + sum(SIZES[:i]) for i in range(len(SIZES))]
NEAR = TOKENS + sum(SIZES)
SIDE = TOKENS // 2
BAND = TOKENS + 2 * SIDE
MOVED = (SIDE, SIDE, BAND, BAND)
MOVED_STARTS = [TOKENS + sum(MOVED[:i]) for i in range(4)]
FAR_OWN = (ROWS // STRIDE) * (COLS // STRIDE)
FAR_HALF = GROUP * FAR_OWN
FAR = 2 * FAR_HALF
FAR_ROWS = [COLS * STRIDE * r + STRIDE * c for r in range(ROWS // STRIDE) for c in range(COLS // STRIDE)]
HALF = 2 * WIDTH
PART = HIDDEN // 2
HID, GPRE, GOUT, SWAP = WIDTH, WIDTH + PART, WIDTH + 2 * PART, 2 * WIDTH + 2 * PART
QUARTER = PART // 4
SHARE = HALF // GROUP
PLANE = GROUP // 4
PLANE_ROWS = 2 * QUARTER // PLANE


def nt(left_op, right_op):
    return lax.dot_general(left_op, right_op, (((1,), (1,)), ((), ())), preferred_element_type=F32)


def tn(left_op, right_op):
    return lax.dot_general(left_op, right_op, (((0,), (0,)), ((), ())), preferred_element_type=F32)


def product(left_op, right_op):
    return jnp.dot(left_op, right_op, preferred_element_type=F32)


CORE_PAIRS = [(i, i ^ 1) for i in range(N_DEV)]
SAME_CORE = [[i for i in range(N_DEV) if i % 2 == core] for core in (0, 1)]


def sent(value, pairs):
    return lax.ppermute(value, AXES, pairs)


def grid_pairs(row_step, col_step):
    pairs = []
    for gx in range(N_GX):
        for gy in range(N_GY):
            sx, sy = gx + col_step, gy + row_step
            if 0 <= sx < N_GX and 0 <= sy < N_GY:
                pairs.append((sx * N_GY + sy, gx * N_GY + gy))
    return pairs


def exchanged(cells):
    return lax.all_to_all(cells, AXES, 0, 0, tiled=True, axis_index_groups=SAME_CORE)


def coords(flat):
    core, x_hi, z, x_lo, y = flat & 1, (flat >> 1) & 1, (flat >> 2) & 3, (flat >> 4) & 1, flat >> 5
    return (x_hi * 2 + x_lo, y, z, core)


def flat_of(place):
    x, y, z, core = place
    return y * 32 + (x & 1) * 16 + z * 4 + (x >> 1) * 2 + core


ORDER = {0: (2, 1, 0), 1: (0, 2, 1)}


def ring_pairs(stage, shift):
    pairs = []
    for i in range(N_DEV):
        place = list(coords(i))
        axis = ORDER[place[3]][stage]
        place[axis] = (place[axis] + shift) % 4
        pairs.append((i, flat_of(place)))
    return pairs


def plane_groups():
    groups = {}
    for i in range(N_DEV):
        place = coords(i)
        first, second, third = ORDER[place[3]]
        key = (place[3], place[first])
        groups.setdefault(key, []).append((place[second], place[third], i))
    return [[i for *_, i in sorted(group)] for group in groups.values()]


WHOLE = pl.BlockSpec(memory_space=pltpu.VMEM)
HBM = pl.BlockSpec(memory_space=pltpu.HBM)
SCALARS = pl.BlockSpec(memory_space=pltpu.SMEM)


def params(mebibytes):
    return pltpu.CompilerParams(vmem_limit_bytes=mebibytes * 1024 * 1024)


def shape(*dims_and_type):
    return jax.ShapeDtypeStruct(dims_and_type[:-1], dims_and_type[-1])


def in_hbm(array):
    return pltpu.with_memory_space_constraint(array, pltpu.HBM)


def fixed(*dims):
    return pl.BlockSpec(dims, lambda p: (0,) * len(dims))


def lanes(rows, cols):
    return pl.BlockSpec((rows, cols), lambda p: (0, p))


def sublanes(rows, cols):
    return pl.BlockSpec((rows, cols), lambda p: (p, 0))


def normalized(inputs):
    centered = inputs - jnp.mean(inputs, axis=1, keepdims=True)
    scale = lax.rsqrt(jnp.mean(centered * centered, axis=1, keepdims=True) + epsilon)
    return centered * scale, scale


def norm_back(grads, xhat, scale, gain):
    scaled = grads * gain
    inputs = scale * (
        scaled
        - jnp.mean(scaled, axis=1, keepdims=True)
        - xhat * jnp.mean(scaled * xhat, axis=1, keepdims=True)
    )
    return (
        inputs,
        jnp.sum(grads * xhat, axis=0, keepdims=True),
        jnp.sum(grads, axis=0, keepdims=True),
    )


def flag_column(flag_ref):
    row = lax.broadcasted_iota(jnp.int32, (TOKENS, ROWS), 0) // COLS
    block = lax.broadcasted_iota(jnp.int32, (TOKENS, ROWS), 1)
    rows = product(jnp.where(row == block, 1.0, 0.0).astype(BF), flag_ref[...].astype(F32).astype(BF))
    token = lax.broadcasted_iota(jnp.int32, (TOKENS, COLS), 0) % COLS
    col = lax.broadcasted_iota(jnp.int32, (TOKENS, COLS), 1)
    return jnp.sum(jnp.where(token == col, rows, 0.0), axis=1, keepdims=True)


def pre_kernel(x_ref, flag_ref, gain_ref, shift_ref, act_ref, marked_ref, spread_ref):
    gain, shift = gain_ref[...].reshape(1, WIDTH), shift_ref[...].reshape(1, WIDTH)
    xhat, _ = normalized(x_ref[...].astype(F32))
    act = (xhat * gain + shift).astype(BF)
    act_ref[...] = act
    marked = jnp.where(flag_column(flag_ref) > 0.5, act.astype(F32), MARK).astype(BF)
    marked_ref[...] = marked
    number = lax.broadcasted_iota(jnp.int32, (2 * FAR_OWN, TOKENS), 0) % FAR_OWN
    token = lax.broadcasted_iota(jnp.int32, (2 * FAR_OWN, TOKENS), 1)
    wanted = number // STRIDE * (COLS * STRIDE) + number % STRIDE * STRIDE
    chosen = product(jnp.where(token == wanted, 1.0, 0.0).astype(BF), marked).astype(BF)
    for k in range(GROUP // 2):
        spread_ref[2 * FAR_OWN * k : 2 * FAR_OWN * (k + 1), :] = chosen


def pre(arrays):
    return pl.pallas_call(
        pre_kernel,
        in_specs=[WHOLE] * 4,
        out_specs=[WHOLE] * 3,
        out_shape=[shape(TOKENS, WIDTH, BF), shape(TOKENS, WIDTH, BF), shape(FAR_HALF, WIDTH, BF)],
        compiler_params=params(16),
        cost_estimate=pl.CostEstimate(
            flops=10_000_000_000, bytes_accessed=2_000_000, transcendentals=TOKENS
        ),
        name="pre",
    )(*arrays)


def band_kernel(marked_ref, l_ref, r_ref, gain_ref, shift_ref, band_ref):
    gain, shift = gain_ref[...].reshape(1, WIDTH), shift_ref[...].reshape(1, WIDTH)
    band_ref[:TOKENS, :] = marked_ref[...]
    for side_ref, start in ((l_ref, TOKENS), (r_ref, TOKENS + SIDE)):
        side = side_ref[...].astype(F32)
        xhat, _ = normalized(jnp.where(side < LIMIT, side, 0.0))
        side = jnp.where(side < LIMIT, xhat * gain + shift, MARK)
        band_ref[start : start + SIDE, :] = side.astype(BF)


def view_of(pair):
    start = jnp.minimum(pair * PAIR // 128 * 128, WIDTH - VIEW)
    return pl.ds(pl.multiple_of(start, 128), VIEW), pair * PAIR - start


def halves(block, begin):
    wide = block.astype(F32)
    lane = lax.broadcasted_iota(jnp.int32, wide.shape, 1) - begin
    first = jnp.where((lane >= 0) & (lane < HEAD_DIM), wide, 0.0).astype(BF)
    second = jnp.where((lane >= HEAD_DIM) & (lane < PAIR), wide, 0.0).astype(BF)
    return jnp.concatenate([first, second], axis=0)


def own_rows(wide):
    return jnp.concatenate([wide[:HEAD_DIM, :TOKENS], wide[HEAD_DIM:, TOKENS:]], axis=0)


def rows_of(pair):
    return pl.ds(pl.multiple_of(pair * PAIR, 32), PAIR)


def folded(tile, op):
    return op(tile.reshape(tile.shape[0] // 8, 8, tile.shape[1]), axis=0)


def attended_part(query_rows, k_ref, flip, view, bias_ref, t_ref, e_ref, chunk):
    count = k_ref.shape[0]
    top = jnp.full((8, 2 * TOKENS), HIDE, F32)
    for start in range(0, count, chunk):
        rows = pl.ds(start, chunk)
        bias = bias_ref[rows, :]
        tile = nt(k_ref[rows, view], query_rows) * SCALE_LOG2
        tile = tile + jnp.concatenate([bias, bias], axis=1)
        t_ref[rows, :] = tile
        top = jnp.maximum(top, folded(tile, jnp.max))
    top = jnp.max(top, axis=0, keepdims=True)
    total = jnp.zeros((8, 2 * TOKENS), F32)
    for start in range(0, count, chunk):
        rows = pl.ds(start, chunk)
        tile = jnp.exp2(t_ref[rows, :] - top)
        total = total + folded(tile, jnp.sum)
        e_ref[rows, :] = tile.astype(BF)
    total = jnp.sum(total, axis=0, keepdims=True)
    return top, total, own_rows(product(flip, e_ref[...]))


def near_kernel(
    exists_ref, act_ref, band_ref, u_ref, d_ref, flag_ref, log_ref, wq_ref, wk_ref, wv_ref,
    all_ref, bias_ref, q_ref, k_ref, v_ref, top_ref, total_ref, sum_ref, t_ref, p_ref, flip_ref,
):
    pair = pl.program_id(0)

    @pl.when(pair == 0)
    def _():
        all_ref[:TOKENS, :] = act_ref[...]
        row = lax.broadcasted_iota(jnp.int32, (TOKENS, TOKENS), 0)
        col = lax.broadcasted_iota(jnp.int32, (TOKENS, TOKENS), 1)
        seen = jnp.where(row == col, 1.0, flag_column(flag_ref))
        bias_ref[:TOKENS, :] = jnp.where(seen > 0.5, log_ref[:TOKENS, :], HIDE)
        for i, (start, size) in enumerate(zip(STARTS, SIZES, strict=True)):
            rows = slice(start, start + size)
            moved, begin = start // BAND, start % BAND
            piece = (band_ref, u_ref, d_ref)[moved][begin : begin + size, :].astype(F32)
            all_ref[rows, :] = jnp.where(piece < LIMIT, piece, 0.0).astype(BF)
            seen = jnp.where(piece[:, :128] < LIMIT, 1.0, 0.0)[:, :1] * exists_ref[i]
            bias_ref[rows, :] = jnp.where(seen > 0.5, log_ref[rows, :], HIDE)
        q_ref[...] = product(act_ref[...], wq_ref[...]).astype(BF)
        k_ref[...] = product(all_ref[...], wk_ref[...]).astype(BF)
        values = product(all_ref[...], wv_ref[...]).astype(BF)
        v_ref[...] = values
        flip_ref[...] = values.T

    view, begin = view_of(pair)
    top, total, wide = attended_part(
        halves(q_ref[:, view], begin), k_ref, flip_ref[rows_of(pair), :], view, bias_ref, t_ref, p_ref,
        NEAR // 2,
    )
    top_ref[pair] = top
    total_ref[pair] = total
    sum_ref[pair] = wide


def attend_near(exists, act, bands, flags, log_weight, wq, wk, wv):
    return pl.pallas_call(
        near_kernel,
        grid=(PAIRS,),
        in_specs=[SCALARS] + [WHOLE] * 9,
        out_specs=[WHOLE] * 8,
        out_shape=[
            shape(NEAR, WIDTH, BF),
            shape(NEAR, TOKENS, F32),
            shape(TOKENS, WIDTH, BF),
            shape(NEAR, WIDTH, BF),
            shape(NEAR, WIDTH, BF),
            shape(PAIRS, 1, 2 * TOKENS, F32),
            shape(PAIRS, 1, 2 * TOKENS, F32),
            shape(PAIRS, PAIR, TOKENS, F32),
        ],
        scratch_shapes=[
            pltpu.VMEM((NEAR, 2 * TOKENS), F32),
            pltpu.VMEM((NEAR, 2 * TOKENS), BF),
            pltpu.VMEM((WIDTH, NEAR), BF),
        ],
        compiler_params=params(14),
        cost_estimate=pl.CostEstimate(
            flops=10_000_000_000, bytes_accessed=12_000_000, transcendentals=0
        ),
        name="attend_near",
    )(exists, act, *bands, flags, log_weight, wq, wk, wv)


def mlp_part(middle, gain, shift, grad_out, wup_ref, wdown_ref, both_ref):
    xhat, _ = normalized(middle)
    act = (xhat * gain + shift).astype(BF)
    steps = HIDDEN // MLP_CHUNK
    chunks = [slice(step * MLP_CHUNK, (step + 1) * MLP_CHUNK) for step in range(steps)]
    for half in range(2):
        both_ref[half, :, :HID] = act
        both_ref[half, :, GOUT:] = grad_out

    def first(chunk):
        return product(act, wup_ref[:, chunk]), nt(grad_out, wdown_ref[chunk, :])

    total, grad_act = middle, 0.0
    ahead = first(chunks[0])
    for step, chunk in enumerate(chunks):
        pre_act, grad_hidden = ahead
        ahead = first(chunks[step + 1]) if step + 1 < steps else None
        below = 0.5 * (1.0 + lax.erf(pre_act * math.sqrt(0.5)))
        slope = jnp.exp(-0.5 * pre_act * pre_act) * (1.0 / math.sqrt(2.0 * math.pi))
        slope = below + pre_act * slope
        hidden = (pre_act * below).astype(BF)
        grad_pre = (grad_hidden * slope).astype(BF)
        total = total + product(hidden, wdown_ref[chunk, :])
        grad_act = grad_act + nt(grad_pre, wup_ref[:, chunk])
        half, col = step // (steps // 2), step % (steps // 2) * MLP_CHUNK
        both_ref[half, :, HID + col : HID + col + MLP_CHUNK] = hidden
        both_ref[half, :, GPRE + col : GPRE + col + MLP_CHUNK] = grad_pre
    return total, grad_act


def far_kernel(
    core_ref, own_ref, other_ref, x_ref, q_ref, wk_ref, wv_ref, wo_ref, top_ref, total_ref, sum_ref,
    gain_ref, shift_ref, gout_ref, wup_hbm, wdown_hbm,
    all_ref, bias_ref, k_ref, v_ref, o_ref, lse_ref, mid_ref, mixed_ref, keep_ref, send_ref,
    gact_ref, t_ref, e_ref, flip_ref, out_ref, wup_ref, wdown_ref, both_ref, sems,
):
    pair = pl.program_id(0)

    copies = [
        pltpu.make_async_copy(wup_hbm, wup_ref, sems.at[0]),
        pltpu.make_async_copy(wdown_hbm, wdown_ref, sems.at[1]),
    ]

    @pl.when(pair == 0)
    def _():
        for copy in copies:
            copy.start()
        for start, half_ref in ((0, own_ref), (FAR_HALF, other_ref)):
            rows = slice(start, start + FAR_HALF)
            piece = half_ref[...].astype(F32)
            all_ref[rows, :] = jnp.where(piece < LIMIT, piece, 0.0).astype(BF)
            seen = jnp.where(piece[:, :128] < LIMIT, 0.0, HIDE)[:, :1]
            bias_ref[rows, :] = jnp.broadcast_to(seen, (FAR_HALF, TOKENS))
        k_ref[...] = product(all_ref[...], wk_ref[...]).astype(BF)
        values = product(all_ref[...], wv_ref[...]).astype(BF)
        v_ref[...] = values
        flip_ref[...] = values.T

    view, begin = view_of(pair)
    far_top, far_total, far_sum = attended_part(
        halves(q_ref[:, view], begin), k_ref, flip_ref[rows_of(pair), :], view, bias_ref, t_ref, e_ref,
        FAR // 2,
    )
    near_top = top_ref[pair]
    top = jnp.maximum(near_top, far_top)
    near_part, far_part = jnp.exp2(near_top - top), jnp.exp2(far_top - top)
    total = total_ref[pair] * near_part + far_total * far_part
    near_part, far_part = near_part / total, far_part / total
    near_sum = sum_ref[pair]
    out_ref[rows_of(pair), :] = jnp.concatenate(
        [
            near_sum[rows] * near_part[:, cols] + far_sum[rows] * far_part[:, cols]
            for rows, cols in (
                (slice(0, HEAD_DIM), slice(0, TOKENS)),
                (slice(HEAD_DIM, PAIR), slice(TOKENS, 2 * TOKENS)),
            )
        ],
        axis=0,
    )
    lse_ref[pair] = top + jnp.log2(total)

    @pl.when(pair == PAIRS - 1)
    def _():
        outs = out_ref[...].T
        o_ref[...] = outs
        middle = x_ref[...].astype(F32) + product(outs.astype(BF), wo_ref[...])
        mid_ref[...] = middle
        for copy in copies:
            copy.wait()
        total, grad_act = mlp_part(
            middle, gain_ref[...].reshape(1, WIDTH), shift_ref[...].reshape(1, WIDTH), gout_ref[...],
            wup_ref, wdown_ref, both_ref,
        )
        mixed_ref[...] = total.astype(BF)
        gact_ref[...] = grad_act
        for mine in range(2):

            @pl.when(core_ref[0] == mine)
            def _(mine=mine):
                keep_ref[...] = both_ref[mine]
                send_ref[...] = both_ref[1 - mine]


def attend_far(core, arrays, weights):
    return pl.pallas_call(
        far_kernel,
        grid=(PAIRS,),
        in_specs=[SCALARS] + [WHOLE] * 13 + [HBM] * 2,
        out_specs=[WHOLE] * 11,
        out_shape=[
            shape(FAR, WIDTH, BF),
            shape(FAR, TOKENS, F32),
            shape(FAR, WIDTH, BF),
            shape(FAR, WIDTH, BF),
            shape(TOKENS, WIDTH, F32),
            shape(PAIRS, 1, 2 * TOKENS, F32),
            shape(TOKENS, WIDTH, F32),
            shape(TOKENS, WIDTH, BF),
            shape(TOKENS, SWAP, BF),
            shape(TOKENS, SWAP, BF),
            shape(TOKENS, WIDTH, F32),
        ],
        scratch_shapes=[
            pltpu.VMEM((FAR, 2 * TOKENS), F32),
            pltpu.VMEM((FAR, 2 * TOKENS), BF),
            pltpu.VMEM((WIDTH, FAR), BF),
            pltpu.VMEM((WIDTH, TOKENS), F32),
            pltpu.VMEM((WIDTH, HIDDEN), BF),
            pltpu.VMEM((HIDDEN, WIDTH), BF),
            pltpu.VMEM((2, TOKENS, SWAP), BF),
            pltpu.SemaphoreType.DMA((2,)),
        ],
        compiler_params=params(32),
        cost_estimate=pl.CostEstimate(
            flops=20_000_000_000, bytes_accessed=30_000_000, transcendentals=HEADS * FAR * TOKENS
        ),
        name="attend_far_mlp",
    )(core, *arrays, *map(in_hbm, weights))


def mlp_grads_kernel(spot_ref, keep_ref, got_ref, *refs):
    outs, both_ref = refs[:4], refs[4]
    both_ref[:TOKENS, :] = keep_ref[...]
    both_ref[TOKENS:, :] = got_ref[...]
    for step, out_ref in enumerate(outs):
        col = pl.multiple_of((spot_ref[0] + step) % 4 * QUARTER, 128)
        grad_pre = both_ref[:, pl.ds(GPRE + col, QUARTER)]
        hidden = both_ref[:, pl.ds(HID + col, QUARTER)]
        out_ref[:QUARTER, :] = tn(grad_pre, both_ref[:, :HID]).astype(BF)
        out_ref[QUARTER:, :] = tn(hidden, both_ref[:, GOUT:]).astype(BF)


def mid_kernel(
    o_ref, mid_ref, gact_ref, gain_ref, gout_ref, wo_ref, kn_ref, kf_ref, alln_ref, allf_ref,
    gwo_ref, gmid_ref, small_ref, gatt_ref, inner_ref, flip_ref, kflip_ref,
):
    xhat, scale = normalized(mid_ref[...])
    inputs, grad_gain, grad_shift = norm_back(
        gact_ref[...], xhat, scale, gain_ref[...].reshape(1, WIDTH)
    )
    grad_mid = gout_ref[...].astype(F32) + inputs
    gmid_ref[...] = grad_mid
    small_ref[...] = jnp.concatenate([grad_gain, grad_shift, jnp.zeros((6, WIDTH), F32)], axis=0)
    branch = grad_mid.astype(BF)
    grads = nt(branch, wo_ref[...]).astype(BF)
    gatt_ref[...] = grads
    gwo_ref[...] = tn(o_ref[...].astype(BF), branch).astype(BF)
    inner_ref[...] = (grads.astype(F32) * o_ref[...]).T
    flip_ref[:, :NEAR] = alln_ref[...].T
    flip_ref[:, NEAR:] = allf_ref[...].T
    kflip_ref[:, :NEAR] = kn_ref[...].T
    kflip_ref[:, NEAR:] = kf_ref[...].T


def back_kernel(
    q_ref, gatt_ref, inner_ref, lse_ref, kn_ref, vn_ref, kf_ref, vf_ref, biasn_ref, biasf_ref,
    flip_ref, kflip_ref, wq_ref, wk_ref, wv_ref,
    gwq_ref, gwk_ref, gwv_ref, gown_ref, l_ref, r_ref, u_ref, d_ref, gfar_ref,
    s_ref, p_ref, gq_ref, gk_ref, gv_ref, acc_ref,
):
    pair = pl.program_id(0)

    @pl.when(pair == 0)
    def _():
        gk_ref[...] = jnp.zeros_like(gk_ref)
        gv_ref[...] = jnp.zeros_like(gv_ref)

    view, begin = view_of(pair)
    query_rows = halves(q_ref[:, view], begin)
    grad_rows = halves(gatt_ref[:, view], begin)
    inner = inner_ref[rows_of(pair), :]
    inner = jnp.concatenate(
        [
            jnp.sum(inner[:HEAD_DIM], axis=0, keepdims=True),
            jnp.sum(inner[HEAD_DIM:], axis=0, keepdims=True),
        ],
        axis=1,
    )
    lse = lse_ref[pair]
    for k_ref, v_ref, bias_ref, offset in (
        (kn_ref, vn_ref, biasn_ref, 0),
        (kf_ref, vf_ref, biasf_ref, NEAR),
    ):
        for start in range(0, k_ref.shape[0], CHUNK):
            rows = pl.ds(start, CHUNK)
            bias = bias_ref[rows, :]
            tile = nt(k_ref[rows, view], query_rows) * SCALE_LOG2
            probs = jnp.exp2(tile + jnp.concatenate([bias, bias], axis=1) - lse)
            grad_probs = nt(v_ref[rows, view], grad_rows)
            there = pl.ds(offset + start, CHUNK)
            s_ref[there, :] = (probs * (grad_probs - inner)).astype(BF)
            p_ref[there, :] = probs.astype(BF)
    gk_ref[:, view] += (product(s_ref[...], query_rows) * SCALE).astype(BF)
    gv_ref[:, view] += product(p_ref[...], grad_rows).astype(BF)
    gq_ref[rows_of(pair), :] = own_rows(product(kflip_ref[rows_of(pair), :], s_ref[...])) * SCALE

    @pl.when(pair == PAIRS - 1)
    def _():
        grad_query = gq_ref[...].T.astype(BF)
        acc_ref[...] = nt(gk_ref[...], wk_ref[...])
        acc_ref[...] += nt(gv_ref[...], wv_ref[...])
        gown_ref[...] = acc_ref[:TOKENS, :] + nt(grad_query, wq_ref[...])
        for piece_ref, start, size in zip(
            (l_ref, r_ref, u_ref, d_ref), MOVED_STARTS, MOVED, strict=True
        ):
            piece_ref[...] = acc_ref[start : start + size, :].astype(BF)
        gfar_ref[...] = acc_ref[NEAR:, :]
        gwk_ref[...] = product(flip_ref[...], gk_ref[...]).astype(BF)
        gwv_ref[...] = product(flip_ref[...], gv_ref[...]).astype(BF)
        gwq_ref[...] = product(flip_ref[:, :TOKENS], grad_query).astype(BF)


def attend_back(arrays):
    count = NEAR + FAR
    return pl.pallas_call(
        back_kernel,
        grid=(PAIRS,),
        in_specs=[WHOLE] * 15,
        out_specs=[WHOLE] * 9,
        out_shape=[shape(WIDTH, WIDTH, BF)] * 3
        + [shape(TOKENS, WIDTH, F32)]
        + [shape(size, WIDTH, BF) for size in MOVED]
        + [shape(FAR, WIDTH, F32)],
        scratch_shapes=[
            pltpu.VMEM((count, 2 * TOKENS), BF),
            pltpu.VMEM((count, 2 * TOKENS), BF),
            pltpu.VMEM((WIDTH, TOKENS), F32),
            pltpu.VMEM((count, WIDTH), BF),
            pltpu.VMEM((count, WIDTH), BF),
            pltpu.VMEM((count, WIDTH), F32),
        ],
        compiler_params=params(26),
        cost_estimate=pl.CostEstimate(flops=0, bytes_accessed=0, transcendentals=0),
        name="attend_back",
    )(*arrays)


def small_call(kernel, name, scalars, arrays, outs, scratch=(), flops=5_000_000_000):
    return pl.pallas_call(
        kernel,
        in_specs=[SCALARS] * len(scalars) + [WHOLE] * len(arrays),
        out_specs=[WHOLE] * len(outs),
        out_shape=outs,
        scratch_shapes=list(scratch),
        compiler_params=params(20),
        cost_estimate=pl.CostEstimate(flops=flops, bytes_accessed=0, transcendentals=0),
        name=name,
    )(*scalars, *arrays)


def far_place(core, cell):
    where = [0, 0, 0]
    for stage, axis in enumerate(ORDER[core]):
        where[axis] = cell // 4 ** (2 - stage) % 4
    return flat_of((*where, core)) // 2


def pack_kernel(core_ref, wq_ref, wk_ref, wv_ref, wo_ref, gfar_ref, keep_ref, send_ref):
    for mine, first_ref, second_ref in ((0, keep_ref, send_ref), (1, send_ref, keep_ref)):

        @pl.when(core_ref[0] == mine)
        def _(mine=mine, first_ref=first_ref, second_ref=second_ref):
            for core, out_ref, weights in (
                (0, first_ref, (wq_ref, wk_ref)),
                (1, second_ref, (wv_ref, wo_ref)),
            ):
                for group in range(16):
                    row = 4 * SHARE * group
                    start = 4 * (SHARE + FAR_OWN) * group
                    out_ref[start : start + 4 * SHARE, :] = weights[row // WIDTH][
                        row % WIDTH : row % WIDTH + 4 * SHARE, :
                    ]
                    base = 0 if core == mine else FAR_HALF
                    far = [base + FAR_OWN * far_place(core, 4 * group + k) for k in range(4)]
                    out_ref[start + 4 * SHARE : start + 4 * (SHARE + FAR_OWN), :] = jnp.concatenate(
                        [gfar_ref[f : f + FAR_OWN, :] for f in far], axis=0
                    ).astype(BF)


def split_kernel(layout, spot_ref, *refs):
    ins, outs, total_ref = refs[:-5], refs[-5:-1], refs[-1]
    if len(layout) == 1:
        rows = outs[0].shape[0]
        for step, out_ref in enumerate(outs):
            run = pl.ds(pl.multiple_of((spot_ref[0] + step) % 4 * rows, rows), rows)
            total = ins[0][run, :].astype(F32)
            for in_ref in ins[1:]:
                total = total + in_ref[run, :].astype(F32)
            out_ref[...] = total.astype(BF)
        return
    total = ins[0][...].astype(F32)
    for in_ref in ins[1:]:
        total = total + in_ref[...].astype(F32)
    total_ref[...] = total
    for step, out_ref in enumerate(outs):
        place = (spot_ref[0] + step) % 4
        runs = [
            total_ref[pl.ds(pl.multiple_of(start + place * (length // 4), 8), length // 4), :]
            for start, length in layout
        ]
        out_ref[...] = jnp.concatenate(runs, axis=0).astype(BF)


def split(spot, arrays, layout=None):
    rows, cols = arrays[0].shape
    return small_call(
        functools.partial(split_kernel, layout or ((0, rows),)),
        "split",
        [spot],
        arrays,
        [shape(rows // 4, cols, BF)] * 4,
        [pltpu.VMEM((rows if layout else 8, cols), F32)],
    )


def first_split_kernel(spot_ref, first_ref, second_ref, *outs):
    for step, out_ref in enumerate(outs):

        @pl.when(pl.program_id(0) == step)
        def _(out_ref=out_ref):
            out_ref[...] = (first_ref[...].astype(F32) + second_ref[...].astype(F32)).astype(BF)


def first_split(spot, arrays):
    rows, cols = arrays[0].shape[0] // 4, arrays[0].shape[1]
    return pl.pallas_call(
        first_split_kernel,
        grid_spec=pltpu.PrefetchScalarGridSpec(
            num_scalar_prefetch=1,
            grid=(4,),
            in_specs=[pl.BlockSpec((rows, cols), lambda k, spot: ((spot[0] + k) % 4, 0))] * 2,
            out_specs=[pl.BlockSpec((rows, cols), lambda k, spot: (0, 0))] * 4,
        ),
        out_shape=[shape(rows, cols, BF)] * 4,
        compiler_params=params(20),
        cost_estimate=pl.CostEstimate(flops=0, bytes_accessed=0, transcendentals=0),
        name="first_split",
    )(spot, *map(in_hbm, arrays))


def join_kernel(extra, spot_ref, *refs):
    ins, out_ref, whole_ref = refs[:4], refs[4], refs[5]
    rows = ins[0].shape[0] - extra
    rest = 0.0
    for step, in_ref in enumerate(ins):
        start = pl.multiple_of((spot_ref[0] + step) % 4 * rows, 8)
        part = in_ref[...].astype(F32)
        whole_ref[pl.ds(start, rows), :] = part[:rows]
        rest = rest + part[rows:]
    if extra:
        whole_ref[4 * rows :, :] = rest
    out_ref[...] = whole_ref[...].astype(BF)


def join(spot, arrays, extra=0):
    rows, cols = arrays[0].shape
    out = 4 * (rows - extra) + extra
    return small_call(
        functools.partial(join_kernel, extra), "join", [spot], arrays, [shape(out, cols, BF)],
        [pltpu.VMEM((out, cols), F32)],
    )[0]


def add_kernel(*refs):
    total = refs[0][...].astype(F32)
    for in_ref in refs[1:-1]:
        total = total + in_ref[...].astype(F32)
    refs[-1][...] = total.astype(BF)


def add(arrays):
    return small_call(add_kernel, "add", [], arrays, [shape(*arrays[0].shape, BF)])[0]


def fold_kernel(l_ref, r_ref, above_ref, below_ref, left_ref, right_ref):
    for piece_ref, out_ref, start in ((l_ref, left_ref, TOKENS), (r_ref, right_ref, TOKENS + SIDE)):
        total = piece_ref[...].astype(F32)
        for band_ref in (above_ref, below_ref):
            total = total + band_ref[start : start + SIDE, :].astype(F32)
        out_ref[...] = total.astype(BF)


def tail_kernel(
    cell_ref, cell1_ref, cell2_ref, cell3_ref, gown_ref, above_ref, below_ref, left_ref, right_ref, x_ref, gain_ref, gmid_ref,
    small_ref, gx_ref, out_ref,
):
    total = gown_ref[...]
    for band_ref in (above_ref, below_ref):
        total = total + band_ref[:TOKENS, :].astype(F32)
    left, right = left_ref[...].astype(F32), right_ref[...].astype(F32)
    sides = []
    for r in range(ROWS):
        sides += [left[WINDOW * r : WINDOW * (r + 1)], right[WINDOW * r : WINDOW * (r + 1)]]
    total = total + jnp.concatenate(sides, axis=0)
    summed = cell_ref[...].astype(F32)
    for other_ref in (cell1_ref, cell2_ref, cell3_ref):
        summed = summed + other_ref[...].astype(F32)
    far = summed[SHARE:]
    token = lax.broadcasted_iota(jnp.int32, (TOKENS, WIDTH), 0)
    for k, where in enumerate(FAR_ROWS):
        total = total + jnp.where(token == where, far[k : k + 1, :], 0.0)
    xhat, scale = normalized(x_ref[...].astype(F32))
    inputs, grad_gain, grad_shift = norm_back(
        total, xhat, scale, gain_ref[...].reshape(1, WIDTH)
    )
    gx_ref[...] = gmid_ref[...] + inputs
    small = jnp.concatenate(
        [grad_gain, grad_shift, small_ref[0:2, :], jnp.zeros((4, WIDTH), F32)], axis=0
    )
    out_ref[...] = jnp.concatenate([summed[:SHARE], small], axis=0).astype(BF)


def fetched_call(kernel, name, arrays, outs):
    return pl.pallas_call(
        kernel,
        grid=(1,),
        in_specs=[fixed(*a.shape) for a in arrays],
        out_specs=[fixed(*out.shape) for out in outs],
        out_shape=outs,
        compiler_params=params(20),
        cost_estimate=pl.CostEstimate(flops=5_000_000_000, bytes_accessed=0, transcendentals=0),
        name=name,
    )(*map(in_hbm, arrays))


def finish_kernel(core_ref, own_ref, other_ref, wq_ref, wk_ref, wv_ref, wo_ref, vectors_ref):
    for mine, first_ref, second_ref in ((0, own_ref, other_ref), (1, other_ref, own_ref)):

        @pl.when(core_ref[0] == mine)
        def _(first_ref=first_ref, second_ref=second_ref):
            wq_ref[...] = first_ref[:WIDTH, :].astype(F32)
            wk_ref[...] = first_ref[WIDTH:HALF, :].astype(F32)
            wv_ref[...] = second_ref[:WIDTH, :].astype(F32)
            wo_ref[...] = second_ref[WIDTH:HALF, :].astype(F32)

    vectors_ref[...] = own_ref[...].astype(F32)[HALF:] + other_ref[...].astype(F32)[HALF:]


def plane_sum_kernel(cells_ref, out_ref):
    total = cells_ref[:PLANE_ROWS, :].astype(F32)
    for k in range(1, PLANE):
        total = total + cells_ref[PLANE_ROWS * k : PLANE_ROWS * (k + 1), :].astype(F32)
    total = total.astype(BF)
    for k in range(PLANE):
        out_ref[PLANE_ROWS * k : PLANE_ROWS * (k + 1), :] = total


def finish_mlp_kernel(place_ref, *refs):
    ins, (up_ref, down_ref) = refs[:8], refs[8:]
    for k, in_ref in enumerate(ins):

        @pl.when(pl.program_id(0) == k)
        def _(in_ref=in_ref):
            up_ref[...] = in_ref[:QUARTER, :].T.astype(F32)
            down_ref[...] = in_ref[QUARTER:, :].astype(F32)


def finish_mlp(places, pieces):
    return pl.pallas_call(
        finish_mlp_kernel,
        grid_spec=pltpu.PrefetchScalarGridSpec(
            num_scalar_prefetch=1,
            grid=(8,),
            in_specs=[WHOLE] * 8,
            out_specs=[
                pl.BlockSpec((WIDTH, QUARTER), lambda k, place: (0, place[k])),
                pl.BlockSpec((QUARTER, WIDTH), lambda k, place: (place[k], 0)),
            ],
        ),
        out_shape=[shape(WIDTH, HIDDEN, F32), shape(HIDDEN, WIDTH, F32)],
        compiler_params=params(20),
        cost_estimate=pl.CostEstimate(flops=0, bytes_accessed=0, transcendentals=0),
        name="finish_mlp",
    )(places, *pieces)


def after(*values):
    return lax.optimization_barrier(values)


def piece_of(block, col_step):
    if col_step == 0:
        return block
    return block[:, WINDOW:] if col_step < 0 else block[:, : COLS - WINDOW]


def window_weights():
    rows, cols = np.mgrid[0:ROWS, 0:COLS]
    query = (rows.reshape(-1), cols.reshape(-1))
    key_rows, key_cols = [rows.reshape(-1)], [cols.reshape(-1)]
    for row_step, col_step in PIECES:
        key_rows.append(piece_of(rows, col_step).reshape(-1) + row_step * ROWS)
        key_cols.append(piece_of(cols, col_step).reshape(-1) + col_step * COLS)
    row_gap = np.concatenate(key_rows)[:, None] - query[0][None]
    col_gap = np.concatenate(key_cols)[:, None] - query[1][None]
    dense = (np.abs(row_gap) <= WINDOW) & (np.abs(col_gap) <= WINDOW)
    dilated = dense & (row_gap % 2 == 0) & (col_gap % 2 == 0)
    return np.where(dense, np.where(dilated, 1.0, 0.0), HIDE).astype(np.float32)


def local(
    embeddings,
    tile_valid,
    w_query,
    w_key,
    w_value,
    w_out,
    w_up,
    w_down,
    gain_attn,
    shift_attn,
    gain_mlp,
    shift_mlp,
    cotangent,
):
    gx, gy = lax.axis_index("gx"), lax.axis_index("gy")
    x, y, z, core = (v.astype(jnp.int32) for v in coords(lax.axis_index(AXES)))
    spots = [
        jnp.where(core == 0, (x, y, z)[ORDER[0][stage]], (x, y, z)[ORDER[1][stage]]).reshape(1)
        for stage in range(3)
    ]
    core = core.reshape(1)
    their_spot = jnp.where(core == 0, (x, y, z)[ORDER[1][0]], (x, y, z)[ORDER[0][0]])
    steps = jnp.arange(4, dtype=jnp.int32)
    places = jnp.concatenate(
        [4 * core + (spots[0] + steps) % 4, 4 * (1 - core) + (their_spot + steps) % 4]
    )
    exists = jnp.stack(
        [
            (gy + row_step >= 0)
            & (gy + row_step < N_GY)
            & (gx + col_step >= 0)
            & (gx + col_step < N_GX)
            for row_step, col_step in PIECES
        ]
    ).astype(F32)
    tokens = embeddings.reshape(TOKENS, WIDTH)

    raw = jnp.where(tile_valid[:, :, None] > 0, embeddings, jnp.asarray(MARK, BF))
    left = sent(raw[:, WINDOW:].reshape(SIDE, WIDTH), grid_pairs(0, -1))
    right = sent(raw[:, :WINDOW].reshape(SIDE, WIDTH), grid_pairs(0, 1))
    act, marked, spread = pre([tokens, tile_valid, gain_attn, shift_attn])
    band = small_call(
        band_kernel,
        "band",
        [],
        [marked, left, right, gain_attn, shift_attn],
        [shape(BAND, WIDTH, BF)],
    )[0]
    spread, band = after(spread, band)
    far_own = exchanged(spread.reshape(GROUP, FAR_OWN, WIDTH)).reshape(FAR_HALF, WIDTH)
    bands = [band, sent(band, grid_pairs(-1, 0)), sent(band, grid_pairs(1, 0))]
    near, bias_near, queries, k_near, v_near, tops, totals, sums = attend_near(
        exists, act, bands, tile_valid, jnp.asarray(window_weights()), w_query, w_key, w_value
    )
    far_own, sums = after(far_own, sums)
    far_other = sent(far_own, CORE_PAIRS)
    grad_out = cotangent.reshape(TOKENS, WIDTH)
    (
        far, bias_far, k_far, v_far, outs, lse, middle, mixed, keep, send, grad_act
    ) = attend_far(
        core,
        [
            far_own, far_other, tokens, queries, w_key, w_value, w_out, tops, totals, sums,
            gain_mlp, shift_mlp, grad_out,
        ],
        [w_up, w_down],
    )
    swapped = sent(send, CORE_PAIRS)

    def rest(operands):
        (
            keep, swapped, outs, middle, grad_act, gain_mlp, gain_attn, grad_out, tokens, queries, lse,
            k_near, v_near, k_far, v_far, bias_near, bias_far, near, far,
            w_query, w_key, w_value, w_out, core, spots, places,
        ) = operands
        quarter = shape(2 * QUARTER, WIDTH, BF)
        mlp_parts = small_call(
            mlp_grads_kernel,
            "mlp_grads",
            [spots[0]],
            [keep, swapped],
            [quarter] * 4,
            [pltpu.VMEM((2 * TOKENS, SWAP), BF)],
        )

        def around(stage, parts):
            return [parts[0]] + [sent(parts[step], ring_pairs(stage, step)) for step in (2, 1, 3)]

        def gathered(stage, part):
            got = {step: sent(part, ring_pairs(stage, -step)) for step in (2, 1, 3)}
            return [part, got[1], got[2], got[3]]

        def in_plane(cells):
            return lax.all_to_all(
                cells.reshape(PLANE, PLANE_ROWS, WIDTH), AXES, 0, 0, tiled=True,
                axis_index_groups=plane_groups(),
            ).reshape(2 * QUARTER, WIDTH)

        mlp_held = around(0, mlp_parts)
        grad_act, _ = after(grad_act, mlp_parts[0])
        grad_wo, grad_mid, small, grad_att, inner, flip, key_flip = small_call(
            mid_kernel,
            "mid",
            [],
            [outs, middle, grad_act, gain_mlp, grad_out, w_out, k_near, k_far, near, far],
            [shape(WIDTH, WIDTH, BF), shape(TOKENS, WIDTH, F32), shape(8, WIDTH, F32)]
            + [shape(TOKENS, WIDTH, BF), shape(WIDTH, TOKENS, F32)]
            + [shape(WIDTH, NEAR + FAR, BF)] * 2,
            flops=30_000_000_000,
        )
        grad_wq, grad_wk, grad_wv, grad_own, piece_left, piece_right, piece_up, piece_down, grad_far = (
            attend_back(
                [
                    queries, grad_att, inner, lse, k_near, v_near, k_far, v_far, bias_near, bias_far,
                    flip, key_flip, w_query, w_key, w_value,
                ]
            )
        )
        mlp_held[0], grad_own = after(mlp_held[0], grad_own)
        mlp_sum = add(mlp_held)
        mlp_cells = in_plane(mlp_sum)
        grad_far, piece_up, piece_down, _ = after(grad_far, piece_up, piece_down, mlp_sum)
        packed = small_call(
            pack_kernel,
            "pack",
            [core],
            [grad_wq, grad_wk, grad_wv, grad_wo, grad_far],
            [shape(HALF + FAR_HALF, WIDTH, BF)] * 2,
        )
        held = [packed[0], sent(packed[1], CORE_PAIRS)]
        above = sent(piece_down, grid_pairs(-1, 0))
        below = sent(piece_up, grid_pairs(1, 0))
        parts = first_split(spots[0], held)
        held = around(0, parts)
        mlp_cells, _ = after(mlp_cells, parts[0])
        mlp_cells = small_call(plane_sum_kernel, "plane_sum", [], [mlp_cells], [quarter])[0]
        mlp_own = in_plane(mlp_cells)
        piece_left, _ = after(piece_left, mlp_cells)
        side = shape(SIDE, WIDTH, BF)
        piece_left, piece_right = fetched_call(
            fold_kernel, "fold", [piece_left, piece_right, above, below], [side, side]
        )
        from_right = sent(piece_left, grid_pairs(0, 1))
        from_left = sent(piece_right, grid_pairs(0, -1))
        held[0], _ = after(held[0], piece_left)
        parts = split(spots[1], held)
        held = around(1, parts)
        held[0], mlp_own = after(held[0], mlp_own)
        parts = split(spots[2], held, ((0, 4 * SHARE), (4 * SHARE, 4 * FAR_OWN)))
        held = around(2, parts)
        mlp_own, _ = after(mlp_own, parts[0])
        mlp_held = gathered(0, mlp_own)
        grad_inputs, cell = fetched_call(
            tail_kernel,
            "tail",
            held
            + [grad_own, above, below, from_left, from_right, tokens, gain_attn, grad_mid, small],
            [shape(TOKENS, WIDTH, F32), shape(SHARE + 8, WIDTH, BF)],
        )
        cell = join(spots[2], gathered(2, cell), 8)
        held = gathered(1, cell)
        held[0], *mlp_held = after(held[0], *mlp_held)
        cell = join(spots[1], held, 8)
        others = [sent(piece, CORE_PAIRS) for piece in mlp_held]
        held = gathered(0, cell)
        grad_up, grad_down = finish_mlp(places, mlp_held + others)
        held[0], _ = after(held[0], grad_up)
        cell = join(spots[0], held, 8)
        other = sent(cell, CORE_PAIRS)
        grad_wq, grad_wk, grad_wv, grad_wo, vectors = small_call(
            finish_kernel,
            "finish",
            [core],
            [cell, other],
            [shape(WIDTH, WIDTH, F32)] * 4 + [shape(8, WIDTH, F32)],
        )
        return grad_inputs, grad_up, grad_down, grad_wq, grad_wk, grad_wv, grad_wo, vectors

    def never(operands):
        return (
            jnp.zeros((TOKENS, WIDTH), F32),
            jnp.zeros((WIDTH, HIDDEN), F32),
            jnp.zeros((HIDDEN, WIDTH), F32),
            *[jnp.zeros((WIDTH, WIDTH), F32)] * 4,
            jnp.zeros((8, WIDTH), F32),
        )

    grad_inputs, grad_up, grad_down, grad_wq, grad_wk, grad_wv, grad_wo, vectors = lax.cond(
        gx < N_GX,
        rest,
        never,
        (
            keep, swapped, outs, middle, grad_act, gain_mlp, gain_attn, grad_out, tokens, queries, lse,
            k_near, v_near, k_far, v_far, bias_near, bias_far, near, far,
            w_query, w_key, w_value, w_out, core, spots, places,
        ),
    )
    return (
        mixed.reshape(ROWS, COLS, WIDTH),
        grad_inputs.reshape(ROWS, COLS, WIDTH),
        grad_wq,
        grad_wk,
        grad_wv,
        grad_wo,
        grad_up,
        grad_down,
        vectors[0],
        vectors[1],
        vectors[2],
        vectors[3],
    )


def solution(mesh):
    grid = P("gy", "gx", None)
    in_specs = (grid, P("gy", "gx")) + (P(),) * 10 + (grid,)
    out_specs = (grid, grid) + (P(),) * 10
    return jax.shard_map(local, mesh=mesh, in_specs=in_specs, out_specs=out_specs, check_vma=False)
```

```python
import functools
import math

import jax
import jax.numpy as jnp
import numpy as np
from jax import lax
from jax.experimental import pallas as pl
from jax.experimental.pallas import tpu as pltpu
from jax.sharding import PartitionSpec as P

HEADS = 16
HEAD_DIM = 48
PAIRS = HEADS // 2
PAIR = 2 * HEAD_DIM
VIEW = 256
STRIDE = 4
WINDOW = 8
ROWS = 8
COLS = 16
TOKENS = ROWS * COLS
WIDTH = 768
HIDDEN = 3072
N_GX = 32
N_GY = 4
N_DEV = N_GX * N_GY
GROUP = N_DEV // 2
AXES = ("gx", "gy")
BF = jnp.bfloat16
F32 = jnp.float32
SCALE = 1.0 / math.sqrt(HEAD_DIM)
SCALE_LOG2 = SCALE * math.log2(math.e)
MARK = 1e30
LIMIT = 1e29
HIDE = -1e30
CHUNK = 256
MLP_CHUNK = 512
epsilon = 1e-05

PIECES = ((0, -1), (0, 1), (-1, 0), (-1, -1), (-1, 1), (1, 0), (1, -1), (1, 1))
SIZES = [TOKENS if col_step == 0 else TOKENS // 2 for _, col_step in PIECES]
STARTS = [TOKENS + sum(SIZES[:i]) for i in range(len(SIZES))]
NEAR = TOKENS + sum(SIZES)
SIDE = TOKENS // 2
BAND = TOKENS + 2 * SIDE
MOVED = (SIDE, SIDE, BAND, BAND)
MOVED_STARTS = [TOKENS + sum(MOVED[:i]) for i in range(4)]
FAR_OWN = (ROWS // STRIDE) * (COLS // STRIDE)
FAR_HALF = GROUP * FAR_OWN
FAR = 2 * FAR_HALF
FAR_ROWS = [COLS * STRIDE * r + STRIDE * c for r in range(ROWS // STRIDE) for c in range(COLS // STRIDE)]
HALF = 2 * WIDTH
PART = HIDDEN // 2
HID, GPRE, GOUT, SWAP = WIDTH, WIDTH + PART, WIDTH + 2 * PART, 2 * WIDTH + 2 * PART
QUARTER = PART // 4
SHARE = HALF // GROUP
PLANE = GROUP // 4
PLANE_ROWS = 2 * QUARTER // PLANE


def nt(left_op, right_op):
    return lax.dot_general(left_op, right_op, (((1,), (1,)), ((), ())), preferred_element_type=F32)


def tn(left_op, right_op):
    return lax.dot_general(left_op, right_op, (((0,), (0,)), ((), ())), preferred_element_type=F32)


def product(left_op, right_op):
    return jnp.dot(left_op, right_op, preferred_element_type=F32)


CORE_PAIRS = [(i, i ^ 1) for i in range(N_DEV)]
SAME_CORE = [[i for i in range(N_DEV) if i % 2 == core] for core in (0, 1)]


def sent(value, pairs):
    return lax.ppermute(value, AXES, pairs)


def grid_pairs(row_step, col_step):
    pairs = []
    for gx in range(N_GX):
        for gy in range(N_GY):
            sx, sy = gx + col_step, gy + row_step
            if 0 <= sx < N_GX and 0 <= sy < N_GY:
                pairs.append((sx * N_GY + sy, gx * N_GY + gy))
    return pairs


def exchanged(cells):
    return lax.all_to_all(cells, AXES, 0, 0, tiled=True, axis_index_groups=SAME_CORE)


def coords(flat):
    core, x_hi, z, x_lo, y = flat & 1, (flat >> 1) & 1, (flat >> 2) & 3, (flat >> 4) & 1, flat >> 5
    return (x_hi * 2 + x_lo, y, z, core)


def flat_of(place):
    x, y, z, core = place
    return y * 32 + (x & 1) * 16 + z * 4 + (x >> 1) * 2 + core


ORDER = {0: (2, 1, 0), 1: (1, 2, 0)}


def ring_pairs(stage, shift):
    pairs = []
    for i in range(N_DEV):
        place = list(coords(i))
        axis = ORDER[place[3]][stage]
        place[axis] = (place[axis] + shift) % 4
        pairs.append((i, flat_of(place)))
    return pairs


def plane_groups():
    groups = {}
    for i in range(N_DEV):
        place = coords(i)
        first, second, third = ORDER[place[3]]
        key = (place[3], place[first])
        groups.setdefault(key, []).append((place[second], place[third], i))
    return [[i for *_, i in sorted(group)] for group in groups.values()]


WHOLE = pl.BlockSpec(memory_space=pltpu.VMEM)
HBM = pl.BlockSpec(memory_space=pltpu.HBM)
SCALARS = pl.BlockSpec(memory_space=pltpu.SMEM)


def params(mebibytes):
    return pltpu.CompilerParams(vmem_limit_bytes=mebibytes * 1024 * 1024)


def shape(*dims_and_type):
    return jax.ShapeDtypeStruct(dims_and_type[:-1], dims_and_type[-1])


def in_hbm(array):
    return pltpu.with_memory_space_constraint(array, pltpu.HBM)


def fixed(*dims):
    return pl.BlockSpec(dims, lambda p: (0,) * len(dims))


def lanes(rows, cols):
    return pl.BlockSpec((rows, cols), lambda p: (0, p))


def sublanes(rows, cols):
    return pl.BlockSpec((rows, cols), lambda p: (p, 0))


def normalized(inputs):
    centered = inputs - jnp.mean(inputs, axis=1, keepdims=True)
    scale = lax.rsqrt(jnp.mean(centered * centered, axis=1, keepdims=True) + epsilon)
    return centered * scale, scale


def norm_back(grads, xhat, scale, gain):
    scaled = grads * gain
    inputs = scale * (
        scaled
        - jnp.mean(scaled, axis=1, keepdims=True)
        - xhat * jnp.mean(scaled * xhat, axis=1, keepdims=True)
    )
    return (
        inputs,
        jnp.sum(grads * xhat, axis=0, keepdims=True),
        jnp.sum(grads, axis=0, keepdims=True),
    )


def flag_column(flag_ref):
    row = lax.broadcasted_iota(jnp.int32, (TOKENS, ROWS), 0) // COLS
    block = lax.broadcasted_iota(jnp.int32, (TOKENS, ROWS), 1)
    rows = product(jnp.where(row == block, 1.0, 0.0).astype(BF), flag_ref[...].astype(F32).astype(BF))
    token = lax.broadcasted_iota(jnp.int32, (TOKENS, COLS), 0) % COLS
    col = lax.broadcasted_iota(jnp.int32, (TOKENS, COLS), 1)
    return jnp.sum(jnp.where(token == col, rows, 0.0), axis=1, keepdims=True)


def pre_kernel(x_ref, flag_ref, gain_ref, shift_ref, act_ref, marked_ref, spread_ref):
    gain, shift = gain_ref[...].reshape(1, WIDTH), shift_ref[...].reshape(1, WIDTH)
    xhat, _ = normalized(x_ref[...].astype(F32))
    act = (xhat * gain + shift).astype(BF)
    act_ref[...] = act
    marked = jnp.where(flag_column(flag_ref) > 0.5, act.astype(F32), MARK).astype(BF)
    marked_ref[...] = marked
    number = lax.broadcasted_iota(jnp.int32, (2 * FAR_OWN, TOKENS), 0) % FAR_OWN
    token = lax.broadcasted_iota(jnp.int32, (2 * FAR_OWN, TOKENS), 1)
    wanted = number // STRIDE * (COLS * STRIDE) + number % STRIDE * STRIDE
    chosen = product(jnp.where(token == wanted, 1.0, 0.0).astype(BF), marked).astype(BF)
    for k in range(GROUP // 2):
        spread_ref[2 * FAR_OWN * k : 2 * FAR_OWN * (k + 1), :] = chosen


def pre(arrays):
    return pl.pallas_call(
        pre_kernel,
        grid=(1,),
        in_specs=[fixed(*a.shape) for a in arrays],
        out_specs=[fixed(TOKENS, WIDTH), fixed(TOKENS, WIDTH), fixed(FAR_HALF, WIDTH)],
        out_shape=[shape(TOKENS, WIDTH, BF), shape(TOKENS, WIDTH, BF), shape(FAR_HALF, WIDTH, BF)],
        compiler_params=params(16),
        cost_estimate=pl.CostEstimate(
            flops=10_000_000_000, bytes_accessed=2_000_000, transcendentals=TOKENS
        ),
        name="pre",
    )(*map(in_hbm, arrays))


def band_kernel(marked_ref, l_ref, r_ref, gain_ref, shift_ref, band_ref):
    gain, shift = gain_ref[...].reshape(1, WIDTH), shift_ref[...].reshape(1, WIDTH)
    band_ref[:TOKENS, :] = marked_ref[...]
    for side_ref, start in ((l_ref, TOKENS), (r_ref, TOKENS + SIDE)):
        side = side_ref[...].astype(F32)
        xhat, _ = normalized(jnp.where(side < LIMIT, side, 0.0))
        side = jnp.where(side < LIMIT, xhat * gain + shift, MARK)
        band_ref[start : start + SIDE, :] = side.astype(BF)


def view_of(pair):
    start = jnp.minimum(pair * PAIR // 128 * 128, WIDTH - VIEW)
    return pl.ds(pl.multiple_of(start, 128), VIEW), pair * PAIR - start


def halves(block, begin):
    wide = block.astype(F32)
    lane = lax.broadcasted_iota(jnp.int32, wide.shape, 1) - begin
    first = jnp.where((lane >= 0) & (lane < HEAD_DIM), wide, 0.0).astype(BF)
    second = jnp.where((lane >= HEAD_DIM) & (lane < PAIR), wide, 0.0).astype(BF)
    return jnp.concatenate([first, second], axis=0)


def own_rows(wide):
    return jnp.concatenate([wide[:HEAD_DIM, :TOKENS], wide[HEAD_DIM:, TOKENS:]], axis=0)


def rows_of(pair):
    return pl.ds(pl.multiple_of(pair * PAIR, 32), PAIR)


def folded(tile, op):
    return op(tile.reshape(tile.shape[0] // 8, 8, tile.shape[1]), axis=0)


def attended_part(query_rows, k_ref, flip, view, bias_ref, t_ref, e_ref, chunk):
    count = k_ref.shape[0]
    top = jnp.full((8, 2 * TOKENS), HIDE, F32)
    for start in range(0, count, chunk):
        rows = pl.ds(start, chunk)
        bias = bias_ref[rows, :]
        tile = nt(k_ref[rows, view], query_rows) * SCALE_LOG2
        tile = tile + jnp.concatenate([bias, bias], axis=1)
        t_ref[rows, :] = tile
        top = jnp.maximum(top, folded(tile, jnp.max))
    top = jnp.max(top, axis=0, keepdims=True)
    total = jnp.zeros((8, 2 * TOKENS), F32)
    for start in range(0, count, chunk):
        rows = pl.ds(start, chunk)
        tile = jnp.exp2(t_ref[rows, :] - top)
        total = total + folded(tile, jnp.sum)
        e_ref[rows, :] = tile.astype(BF)
    total = jnp.sum(total, axis=0, keepdims=True)
    return top, total, own_rows(product(flip, e_ref[...]))


def near_kernel(
    exists_ref, act_ref, band_ref, u_ref, d_ref, flag_ref, log_ref, wq_ref, wk_ref, wv_ref,
    all_ref, bias_ref, q_ref, k_ref, v_ref, top_ref, total_ref, sum_ref, t_ref, p_ref, flip_ref,
):
    pair = pl.program_id(0)

    @pl.when(pair == 0)
    def _():
        all_ref[:TOKENS, :] = act_ref[...]
        row = lax.broadcasted_iota(jnp.int32, (TOKENS, TOKENS), 0)
        col = lax.broadcasted_iota(jnp.int32, (TOKENS, TOKENS), 1)
        seen = jnp.where(row == col, 1.0, flag_column(flag_ref))
        bias_ref[:TOKENS, :] = jnp.where(seen > 0.5, log_ref[:TOKENS, :], HIDE)
        for i, (start, size) in enumerate(zip(STARTS, SIZES, strict=True)):
            rows = slice(start, start + size)
            moved, begin = start // BAND, start % BAND
            piece = (band_ref, u_ref, d_ref)[moved][begin : begin + size, :].astype(F32)
            all_ref[rows, :] = jnp.where(piece < LIMIT, piece, 0.0).astype(BF)
            seen = jnp.where(piece[:, :128] < LIMIT, 1.0, 0.0)[:, :1] * exists_ref[i]
            bias_ref[rows, :] = jnp.where(seen > 0.5, log_ref[rows, :], HIDE)
        q_ref[...] = product(act_ref[...], wq_ref[...]).astype(BF)
        k_ref[...] = product(all_ref[...], wk_ref[...]).astype(BF)
        values = product(all_ref[...], wv_ref[...]).astype(BF)
        v_ref[...] = values
        flip_ref[...] = values.T

    view, begin = view_of(pair)
    top, total, wide = attended_part(
        halves(q_ref[:, view], begin), k_ref, flip_ref[rows_of(pair), :], view, bias_ref, t_ref, p_ref,
        NEAR // 2,
    )
    top_ref[pair] = top
    total_ref[pair] = total
    sum_ref[pair] = wide


def attend_near(exists, act, bands, flags, log_weight, wq, wk, wv):
    return pl.pallas_call(
        near_kernel,
        grid=(PAIRS,),
        in_specs=[SCALARS] + [WHOLE] * 9,
        out_specs=[WHOLE] * 8,
        out_shape=[
            shape(NEAR, WIDTH, BF),
            shape(NEAR, TOKENS, F32),
            shape(TOKENS, WIDTH, BF),
            shape(NEAR, WIDTH, BF),
            shape(NEAR, WIDTH, BF),
            shape(PAIRS, 1, 2 * TOKENS, F32),
            shape(PAIRS, 1, 2 * TOKENS, F32),
            shape(PAIRS, PAIR, TOKENS, F32),
        ],
        scratch_shapes=[
            pltpu.VMEM((NEAR, 2 * TOKENS), F32),
            pltpu.VMEM((NEAR, 2 * TOKENS), BF),
            pltpu.VMEM((WIDTH, NEAR), BF),
        ],
        compiler_params=params(14),
        cost_estimate=pl.CostEstimate(
            flops=10_000_000_000, bytes_accessed=12_000_000, transcendentals=0
        ),
        name="attend_near",
    )(exists, act, *bands, flags, log_weight, wq, wk, wv)


def mlp_part(middle, gain, shift, grad_out, wup_ref, wdown_ref, both_ref):
    xhat, _ = normalized(middle)
    act = (xhat * gain + shift).astype(BF)
    steps = HIDDEN // MLP_CHUNK
    chunks = [slice(step * MLP_CHUNK, (step + 1) * MLP_CHUNK) for step in range(steps)]
    for half in range(2):
        both_ref[half, :, :HID] = act
        both_ref[half, :, GOUT:] = grad_out

    def first(chunk):
        return product(act, wup_ref[:, chunk]), nt(grad_out, wdown_ref[chunk, :])

    total, grad_act = middle, 0.0
    ahead = first(chunks[0])
    for step, chunk in enumerate(chunks):
        pre_act, grad_hidden = ahead
        ahead = first(chunks[step + 1]) if step + 1 < steps else None
        below = 0.5 * (1.0 + lax.erf(pre_act * math.sqrt(0.5)))
        slope = jnp.exp(-0.5 * pre_act * pre_act) * (1.0 / math.sqrt(2.0 * math.pi))
        slope = below + pre_act * slope
        hidden = (pre_act * below).astype(BF)
        grad_pre = (grad_hidden * slope).astype(BF)
        total = total + product(hidden, wdown_ref[chunk, :])
        grad_act = grad_act + nt(grad_pre, wup_ref[:, chunk])
        half, col = step // (steps // 2), step % (steps // 2) * MLP_CHUNK
        both_ref[half, :, HID + col : HID + col + MLP_CHUNK] = hidden
        both_ref[half, :, GPRE + col : GPRE + col + MLP_CHUNK] = grad_pre
    return total, grad_act


def far_kernel(
    core_ref, own_ref, other_ref, x_ref, q_ref, wk_ref, wv_ref, wo_ref, top_ref, total_ref, sum_ref,
    gain_ref, shift_ref, gout_ref, wup_hbm, wdown_hbm,
    all_ref, bias_ref, k_ref, v_ref, o_ref, lse_ref, mid_ref, mixed_ref, keep_ref, send_ref,
    gact_ref, t_ref, e_ref, flip_ref, out_ref, wup_ref, wdown_ref, both_ref, sems,
):
    pair = pl.program_id(0)

    copies = [
        pltpu.make_async_copy(wup_hbm, wup_ref, sems.at[0]),
        pltpu.make_async_copy(wdown_hbm, wdown_ref, sems.at[1]),
    ]

    @pl.when(pair == 0)
    def _():
        for copy in copies:
            copy.start()
        for start, half_ref in ((0, own_ref), (FAR_HALF, other_ref)):
            rows = slice(start, start + FAR_HALF)
            piece = half_ref[...].astype(F32)
            all_ref[rows, :] = jnp.where(piece < LIMIT, piece, 0.0).astype(BF)
            seen = jnp.where(piece[:, :128] < LIMIT, 0.0, HIDE)[:, :1]
            bias_ref[rows, :] = jnp.broadcast_to(seen, (FAR_HALF, TOKENS))
        k_ref[...] = product(all_ref[...], wk_ref[...]).astype(BF)
        values = product(all_ref[...], wv_ref[...]).astype(BF)
        v_ref[...] = values
        flip_ref[...] = values.T

    view, begin = view_of(pair)
    far_top, far_total, far_sum = attended_part(
        halves(q_ref[:, view], begin), k_ref, flip_ref[rows_of(pair), :], view, bias_ref, t_ref, e_ref,
        FAR // 2,
    )
    near_top = top_ref[pair]
    top = jnp.maximum(near_top, far_top)
    near_part, far_part = jnp.exp2(near_top - top), jnp.exp2(far_top - top)
    total = total_ref[pair] * near_part + far_total * far_part
    near_part, far_part = near_part / total, far_part / total
    near_sum = sum_ref[pair]
    out_ref[rows_of(pair), :] = jnp.concatenate(
        [
            near_sum[rows] * near_part[:, cols] + far_sum[rows] * far_part[:, cols]
            for rows, cols in (
                (slice(0, HEAD_DIM), slice(0, TOKENS)),
                (slice(HEAD_DIM, PAIR), slice(TOKENS, 2 * TOKENS)),
            )
        ],
        axis=0,
    )
    lse_ref[pair] = top + jnp.log2(total)

    @pl.when(pair == PAIRS - 1)
    def _():
        outs = out_ref[...].T
        o_ref[...] = outs
        middle = x_ref[...].astype(F32) + product(outs.astype(BF), wo_ref[...])
        mid_ref[...] = middle
        for copy in copies:
            copy.wait()
        total, grad_act = mlp_part(
            middle, gain_ref[...].reshape(1, WIDTH), shift_ref[...].reshape(1, WIDTH), gout_ref[...],
            wup_ref, wdown_ref, both_ref,
        )
        mixed_ref[...] = total.astype(BF)
        gact_ref[...] = grad_act
        for mine in range(2):

            @pl.when(core_ref[0] == mine)
            def _(mine=mine):
                keep_ref[...] = both_ref[mine]
                send_ref[...] = both_ref[1 - mine]


def attend_far(core, arrays, weights):
    return pl.pallas_call(
        far_kernel,
        grid=(PAIRS,),
        in_specs=[SCALARS] + [WHOLE] * 13 + [HBM] * 2,
        out_specs=[WHOLE] * 11,
        out_shape=[
            shape(FAR, WIDTH, BF),
            shape(FAR, TOKENS, F32),
            shape(FAR, WIDTH, BF),
            shape(FAR, WIDTH, BF),
            shape(TOKENS, WIDTH, F32),
            shape(PAIRS, 1, 2 * TOKENS, F32),
            shape(TOKENS, WIDTH, F32),
            shape(TOKENS, WIDTH, BF),
            shape(TOKENS, SWAP, BF),
            shape(TOKENS, SWAP, BF),
            shape(TOKENS, WIDTH, F32),
        ],
        scratch_shapes=[
            pltpu.VMEM((FAR, 2 * TOKENS), F32),
            pltpu.VMEM((FAR, 2 * TOKENS), BF),
            pltpu.VMEM((WIDTH, FAR), BF),
            pltpu.VMEM((WIDTH, TOKENS), F32),
            pltpu.VMEM((WIDTH, HIDDEN), BF),
            pltpu.VMEM((HIDDEN, WIDTH), BF),
            pltpu.VMEM((2, TOKENS, SWAP), BF),
            pltpu.SemaphoreType.DMA((2,)),
        ],
        compiler_params=params(32),
        cost_estimate=pl.CostEstimate(
            flops=20_000_000_000, bytes_accessed=30_000_000, transcendentals=HEADS * FAR * TOKENS
        ),
        name="attend_far_mlp",
    )(core, *arrays, *map(in_hbm, weights))


def mlp_grads_kernel(spot_ref, keep_ref, got_ref, *refs):
    outs, both_ref = refs[:4], refs[4]
    both_ref[:TOKENS, :] = keep_ref[...]
    both_ref[TOKENS:, :] = got_ref[...]
    for step, out_ref in enumerate(outs):
        col = pl.multiple_of((spot_ref[0] + step) % 4 * QUARTER, 128)
        grad_pre = both_ref[:, pl.ds(GPRE + col, QUARTER)]
        hidden = both_ref[:, pl.ds(HID + col, QUARTER)]
        out_ref[:QUARTER, :] = tn(grad_pre, both_ref[:, :HID]).astype(BF)
        out_ref[QUARTER:, :] = tn(hidden, both_ref[:, GOUT:]).astype(BF)


def mid_kernel(
    o_ref, mid_ref, gact_ref, gain_ref, gout_ref, wo_ref, kn_ref, kf_ref, alln_ref, allf_ref,
    gwo_ref, gmid_ref, small_ref, gatt_ref, inner_ref, flip_ref, kflip_ref,
):
    xhat, scale = normalized(mid_ref[...])
    inputs, grad_gain, grad_shift = norm_back(
        gact_ref[...], xhat, scale, gain_ref[...].reshape(1, WIDTH)
    )
    grad_mid = gout_ref[...].astype(F32) + inputs
    gmid_ref[...] = grad_mid
    small_ref[...] = jnp.concatenate([grad_gain, grad_shift, jnp.zeros((6, WIDTH), F32)], axis=0)
    branch = grad_mid.astype(BF)
    grads = nt(branch, wo_ref[...]).astype(BF)
    gatt_ref[...] = grads
    gwo_ref[...] = tn(o_ref[...].astype(BF), branch).astype(BF)
    inner_ref[...] = (grads.astype(F32) * o_ref[...]).T
    flip_ref[:, :NEAR] = alln_ref[...].T
    flip_ref[:, NEAR:] = allf_ref[...].T
    kflip_ref[:, :NEAR] = kn_ref[...].T
    kflip_ref[:, NEAR:] = kf_ref[...].T


def back_kernel(
    q_ref, gatt_ref, inner_ref, lse_ref, kn_ref, vn_ref, kf_ref, vf_ref, biasn_ref, biasf_ref,
    flip_ref, kflip_ref, wq_ref, wk_ref, wv_ref,
    gwq_ref, gwk_ref, gwv_ref, gown_ref, l_ref, r_ref, u_ref, d_ref, gfar_ref,
    s_ref, p_ref, gq_ref, gk_ref, gv_ref, acc_ref,
):
    pair = pl.program_id(0)

    @pl.when(pair == 0)
    def _():
        gk_ref[...] = jnp.zeros_like(gk_ref)
        gv_ref[...] = jnp.zeros_like(gv_ref)

    view, begin = view_of(pair)
    query_rows = halves(q_ref[:, view], begin)
    grad_rows = halves(gatt_ref[:, view], begin)
    inner = inner_ref[rows_of(pair), :]
    inner = jnp.concatenate(
        [
            jnp.sum(inner[:HEAD_DIM], axis=0, keepdims=True),
            jnp.sum(inner[HEAD_DIM:], axis=0, keepdims=True),
        ],
        axis=1,
    )
    lse = lse_ref[pair]
    for k_ref, v_ref, bias_ref, offset in (
        (kn_ref, vn_ref, biasn_ref, 0),
        (kf_ref, vf_ref, biasf_ref, NEAR),
    ):
        for start in range(0, k_ref.shape[0], CHUNK):
            rows = pl.ds(start, CHUNK)
            bias = bias_ref[rows, :]
            tile = nt(k_ref[rows, view], query_rows) * SCALE_LOG2
            probs = jnp.exp2(tile + jnp.concatenate([bias, bias], axis=1) - lse)
            grad_probs = nt(v_ref[rows, view], grad_rows)
            there = pl.ds(offset + start, CHUNK)
            s_ref[there, :] = (probs * (grad_probs - inner)).astype(BF)
            p_ref[there, :] = probs.astype(BF)
    gk_ref[:, view] += (product(s_ref[...], query_rows) * SCALE).astype(BF)
    gv_ref[:, view] += product(p_ref[...], grad_rows).astype(BF)
    gq_ref[rows_of(pair), :] = own_rows(product(kflip_ref[rows_of(pair), :], s_ref[...])) * SCALE

    @pl.when(pair == PAIRS - 1)
    def _():
        grad_query = gq_ref[...].T.astype(BF)
        acc_ref[...] = nt(gk_ref[...], wk_ref[...])
        acc_ref[...] += nt(gv_ref[...], wv_ref[...])
        gown_ref[...] = acc_ref[:TOKENS, :] + nt(grad_query, wq_ref[...])
        for piece_ref, start, size in zip(
            (l_ref, r_ref, u_ref, d_ref), MOVED_STARTS, MOVED, strict=True
        ):
            piece_ref[...] = acc_ref[start : start + size, :].astype(BF)
        gfar_ref[...] = acc_ref[NEAR:, :]
        gwk_ref[...] = product(flip_ref[...], gk_ref[...]).astype(BF)
        gwv_ref[...] = product(flip_ref[...], gv_ref[...]).astype(BF)
        gwq_ref[...] = product(flip_ref[:, :TOKENS], grad_query).astype(BF)


def attend_back(arrays):
    count = NEAR + FAR
    return pl.pallas_call(
        back_kernel,
        grid=(PAIRS,),
        in_specs=[WHOLE] * 15,
        out_specs=[WHOLE] * 9,
        out_shape=[shape(WIDTH, WIDTH, BF)] * 3
        + [shape(TOKENS, WIDTH, F32)]
        + [shape(size, WIDTH, BF) for size in MOVED]
        + [shape(FAR, WIDTH, F32)],
        scratch_shapes=[
            pltpu.VMEM((count, 2 * TOKENS), BF),
            pltpu.VMEM((count, 2 * TOKENS), BF),
            pltpu.VMEM((WIDTH, TOKENS), F32),
            pltpu.VMEM((count, WIDTH), BF),
            pltpu.VMEM((count, WIDTH), BF),
            pltpu.VMEM((count, WIDTH), F32),
        ],
        compiler_params=params(26),
        cost_estimate=pl.CostEstimate(flops=0, bytes_accessed=0, transcendentals=0),
        name="attend_back",
    )(*arrays)


def small_call(kernel, name, scalars, arrays, outs, scratch=(), flops=5_000_000_000):
    return pl.pallas_call(
        kernel,
        in_specs=[SCALARS] * len(scalars) + [WHOLE] * len(arrays),
        out_specs=[WHOLE] * len(outs),
        out_shape=outs,
        scratch_shapes=list(scratch),
        compiler_params=params(20),
        cost_estimate=pl.CostEstimate(flops=flops, bytes_accessed=0, transcendentals=0),
        name=name,
    )(*scalars, *arrays)


def far_place(core, cell):
    where = [0, 0, 0]
    for stage, axis in enumerate(ORDER[core]):
        where[axis] = cell // 4 ** (2 - stage) % 4
    return flat_of((*where, core)) // 2


def pack_kernel(core_ref, wq_ref, wk_ref, wv_ref, wo_ref, gfar_ref, keep_ref, send_ref):
    for mine, first_ref, second_ref in ((0, keep_ref, send_ref), (1, send_ref, keep_ref)):

        @pl.when(core_ref[0] == mine)
        def _(mine=mine, first_ref=first_ref, second_ref=second_ref):
            for core, out_ref, weights in (
                (0, first_ref, (wq_ref, wk_ref)),
                (1, second_ref, (wv_ref, wo_ref)),
            ):
                for group in range(16):
                    row = 4 * SHARE * group
                    start = 4 * (SHARE + FAR_OWN) * group
                    out_ref[start : start + 4 * SHARE, :] = weights[row // WIDTH][
                        row % WIDTH : row % WIDTH + 4 * SHARE, :
                    ]
                    base = 0 if core == mine else FAR_HALF
                    far = [base + FAR_OWN * far_place(core, 4 * group + k) for k in range(4)]
                    out_ref[start + 4 * SHARE : start + 4 * (SHARE + FAR_OWN), :] = jnp.concatenate(
                        [gfar_ref[f : f + FAR_OWN, :] for f in far], axis=0
                    ).astype(BF)


def split_kernel(layout, spot_ref, *refs):
    ins, outs, total_ref = refs[:-5], refs[-5:-1], refs[-1]
    if len(layout) == 1:
        rows = outs[0].shape[0]
        for step, out_ref in enumerate(outs):
            run = pl.ds(pl.multiple_of((spot_ref[0] + step) % 4 * rows, rows), rows)
            total = ins[0][run, :].astype(F32)
            for in_ref in ins[1:]:
                total = total + in_ref[run, :].astype(F32)
            out_ref[...] = total.astype(BF)
        return
    total = ins[0][...].astype(F32)
    for in_ref in ins[1:]:
        total = total + in_ref[...].astype(F32)
    total_ref[...] = total
    for step, out_ref in enumerate(outs):
        place = (spot_ref[0] + step) % 4
        runs = [
            total_ref[pl.ds(pl.multiple_of(start + place * (length // 4), 8), length // 4), :]
            for start, length in layout
        ]
        out_ref[...] = jnp.concatenate(runs, axis=0).astype(BF)


def split(spot, arrays, layout=None):
    rows, cols = arrays[0].shape
    return small_call(
        functools.partial(split_kernel, layout or ((0, rows),)),
        "split",
        [spot],
        arrays,
        [shape(rows // 4, cols, BF)] * 4,
        [pltpu.VMEM((rows if layout else 8, cols), F32)],
    )


def first_split_kernel(spot_ref, first_ref, second_ref, *outs):
    for step, out_ref in enumerate(outs):

        @pl.when(pl.program_id(0) == step)
        def _(out_ref=out_ref):
            out_ref[...] = (first_ref[...].astype(F32) + second_ref[...].astype(F32)).astype(BF)


def first_split(spot, arrays):
    rows, cols = arrays[0].shape[0] // 4, arrays[0].shape[1]
    return pl.pallas_call(
        first_split_kernel,
        grid_spec=pltpu.PrefetchScalarGridSpec(
            num_scalar_prefetch=1,
            grid=(4,),
            in_specs=[pl.BlockSpec((rows, cols), lambda k, spot: ((spot[0] + k) % 4, 0))] * 2,
            out_specs=[pl.BlockSpec((rows, cols), lambda k, spot: (0, 0))] * 4,
        ),
        out_shape=[shape(rows, cols, BF)] * 4,
        compiler_params=params(20),
        cost_estimate=pl.CostEstimate(flops=0, bytes_accessed=0, transcendentals=0),
        name="first_split",
    )(spot, *map(in_hbm, arrays))


def join_kernel(extra, spot_ref, *refs):
    ins, out_ref, whole_ref = refs[:4], refs[4], refs[5]
    rows = ins[0].shape[0] - extra
    rest = 0.0
    for step, in_ref in enumerate(ins):
        start = pl.multiple_of((spot_ref[0] + step) % 4 * rows, 8)
        part = in_ref[...].astype(F32)
        whole_ref[pl.ds(start, rows), :] = part[:rows]
        rest = rest + part[rows:]
    if extra:
        whole_ref[4 * rows :, :] = rest
    out_ref[...] = whole_ref[...].astype(BF)


def join(spot, arrays, extra=0):
    rows, cols = arrays[0].shape
    out = 4 * (rows - extra) + extra
    return small_call(
        functools.partial(join_kernel, extra), "join", [spot], arrays, [shape(out, cols, BF)],
        [pltpu.VMEM((out, cols), F32)],
    )[0]


def add_kernel(*refs):
    total = refs[0][...].astype(F32)
    for in_ref in refs[1:-1]:
        total = total + in_ref[...].astype(F32)
    refs[-1][...] = total.astype(BF)


def add(arrays):
    return small_call(add_kernel, "add", [], arrays, [shape(*arrays[0].shape, BF)])[0]


def fold_kernel(l_ref, r_ref, above_ref, below_ref, left_ref, right_ref):
    for piece_ref, out_ref, start in ((l_ref, left_ref, TOKENS), (r_ref, right_ref, TOKENS + SIDE)):
        total = piece_ref[...].astype(F32)
        for band_ref in (above_ref, below_ref):
            total = total + band_ref[start : start + SIDE, :].astype(F32)
        out_ref[...] = total.astype(BF)


def tail_kernel(
    cell_ref, cell1_ref, cell2_ref, cell3_ref, gown_ref, above_ref, below_ref, left_ref, right_ref, x_ref, gain_ref, gmid_ref,
    small_ref, gx_ref, out_ref,
):
    total = gown_ref[...]
    for band_ref in (above_ref, below_ref):
        total = total + band_ref[:TOKENS, :].astype(F32)
    left, right = left_ref[...].astype(F32), right_ref[...].astype(F32)
    sides = []
    for r in range(ROWS):
        sides += [left[WINDOW * r : WINDOW * (r + 1)], right[WINDOW * r : WINDOW * (r + 1)]]
    total = total + jnp.concatenate(sides, axis=0)
    summed = cell_ref[...].astype(F32)
    for other_ref in (cell1_ref, cell2_ref, cell3_ref):
        summed = summed + other_ref[...].astype(F32)
    far = summed[SHARE:]
    token = lax.broadcasted_iota(jnp.int32, (TOKENS, WIDTH), 0)
    for k, where in enumerate(FAR_ROWS):
        total = total + jnp.where(token == where, far[k : k + 1, :], 0.0)
    xhat, scale = normalized(x_ref[...].astype(F32))
    inputs, grad_gain, grad_shift = norm_back(
        total, xhat, scale, gain_ref[...].reshape(1, WIDTH)
    )
    gx_ref[...] = gmid_ref[...] + inputs
    small = jnp.concatenate(
        [grad_gain, grad_shift, small_ref[0:2, :], jnp.zeros((4, WIDTH), F32)], axis=0
    )
    out_ref[...] = jnp.concatenate([summed[:SHARE], small], axis=0).astype(BF)


def fetched_call(kernel, name, arrays, outs):
    return pl.pallas_call(
        kernel,
        grid=(1,),
        in_specs=[fixed(*a.shape) for a in arrays],
        out_specs=[fixed(*out.shape) for out in outs],
        out_shape=outs,
        compiler_params=params(20),
        cost_estimate=pl.CostEstimate(flops=5_000_000_000, bytes_accessed=0, transcendentals=0),
        name=name,
    )(*map(in_hbm, arrays))


def widen_half(mine, core_ref, half_ref, outs, wide_ref, sems):
    rows = WIDTH // 2
    for core in range(2):

        @pl.when(core_ref[0] == core)
        def _(core=core):
            first = 2 * (core if mine else 1 - core)
            copies = []
            for k in range(4):
                wide = wide_ref.at[pl.ds(rows * k, rows), :]
                wide[...] = half_ref[rows * k : rows * (k + 1), :].astype(F32)
                out = outs[first + k // 2].at[pl.ds(rows * (k % 2), rows), :]
                copies.append(pltpu.make_async_copy(wide, out, sems.at[k]))
                copies[-1].start()
            for copy in copies:
                copy.wait()


def finish_own_kernel(core_ref, own_ref, *refs):
    widen_half(True, core_ref, own_ref, refs[:4], refs[4], refs[5])


def finish_kernel(core_ref, own_ref, other_ref, *refs):
    outs, vector_refs, wide_ref, sems = refs[4:8], refs[8:12], refs[12], refs[13]
    vectors = own_ref[...].astype(F32)[HALF:] + other_ref[...].astype(F32)[HALF:]
    for i, vector_ref in enumerate(vector_refs):
        vector_ref[...] = vectors[i : i + 1].reshape(WIDTH)
    widen_half(False, core_ref, other_ref, outs, wide_ref, sems)


def finish(core, own):
    other = sent(own, CORE_PAIRS)
    scratch = [pltpu.VMEM((HALF, WIDTH), F32), pltpu.SemaphoreType.DMA((4,))]
    outs = [pltpu.HBM((WIDTH, WIDTH), F32)] * 4
    begun = pl.pallas_call(
        finish_own_kernel,
        in_specs=[SCALARS, WHOLE],
        out_specs=[HBM] * 4,
        out_shape=outs,
        scratch_shapes=scratch,
        compiler_params=params(20),
        cost_estimate=pl.CostEstimate(
            flops=20_000_000_000, bytes_accessed=0, transcendentals=0
        ),
        name="finish_own",
    )(core, own)
    return pl.pallas_call(
        finish_kernel,
        in_specs=[SCALARS] + [WHOLE] * 2 + [HBM] * 4,
        out_specs=[HBM] * 4 + [WHOLE] * 4,
        out_shape=outs + [shape(WIDTH, F32)] * 4,
        input_output_aliases={3 + i: i for i in range(4)},
        scratch_shapes=scratch,
        compiler_params=params(20),
        cost_estimate=pl.CostEstimate(flops=0, bytes_accessed=0, transcendentals=0),
        name="finish",
    )(core, own, other, *begun)


def plane_sum_kernel(cells_ref, out_ref):
    total = cells_ref[:PLANE_ROWS, :].astype(F32)
    for k in range(1, PLANE):
        total = total + cells_ref[PLANE_ROWS * k : PLANE_ROWS * (k + 1), :].astype(F32)
    total = total.astype(BF)
    for k in range(PLANE):
        out_ref[PLANE_ROWS * k : PLANE_ROWS * (k + 1), :] = total


def finish_mlp_kernel(place_ref, *refs):
    ins, (up_ref, down_ref) = refs[:8], refs[8:]
    for k, in_ref in enumerate(ins):

        @pl.when(pl.program_id(0) == k)
        def _(in_ref=in_ref):
            up_ref[...] = in_ref[:QUARTER, :].T.astype(F32)
            down_ref[...] = in_ref[QUARTER:, :].astype(F32)


def finish_mlp(places, pieces):
    return pl.pallas_call(
        finish_mlp_kernel,
        grid_spec=pltpu.PrefetchScalarGridSpec(
            num_scalar_prefetch=1,
            grid=(8,),
            in_specs=[WHOLE] * 8,
            out_specs=[
                pl.BlockSpec((WIDTH, QUARTER), lambda k, place: (0, place[k])),
                pl.BlockSpec((QUARTER, WIDTH), lambda k, place: (place[k], 0)),
            ],
        ),
        out_shape=[shape(WIDTH, HIDDEN, F32), shape(HIDDEN, WIDTH, F32)],
        compiler_params=params(20),
        cost_estimate=pl.CostEstimate(flops=0, bytes_accessed=0, transcendentals=0),
        name="finish_mlp",
    )(places, *pieces)


def after(*values):
    return lax.optimization_barrier(values)


def piece_of(block, col_step):
    if col_step == 0:
        return block
    return block[:, WINDOW:] if col_step < 0 else block[:, : COLS - WINDOW]


def window_weights():
    rows, cols = np.mgrid[0:ROWS, 0:COLS]
    query = (rows.reshape(-1), cols.reshape(-1))
    key_rows, key_cols = [rows.reshape(-1)], [cols.reshape(-1)]
    for row_step, col_step in PIECES:
        key_rows.append(piece_of(rows, col_step).reshape(-1) + row_step * ROWS)
        key_cols.append(piece_of(cols, col_step).reshape(-1) + col_step * COLS)
    row_gap = np.concatenate(key_rows)[:, None] - query[0][None]
    col_gap = np.concatenate(key_cols)[:, None] - query[1][None]
    dense = (np.abs(row_gap) <= WINDOW) & (np.abs(col_gap) <= WINDOW)
    dilated = dense & (row_gap % 2 == 0) & (col_gap % 2 == 0)
    return np.where(dense, np.where(dilated, 1.0, 0.0), HIDE).astype(np.float32)


def local(
    embeddings,
    tile_valid,
    w_query,
    w_key,
    w_value,
    w_out,
    w_up,
    w_down,
    gain_attn,
    shift_attn,
    gain_mlp,
    shift_mlp,
    cotangent,
):
    gx, gy = lax.axis_index("gx"), lax.axis_index("gy")
    x, y, z, core = (v.astype(jnp.int32) for v in coords(lax.axis_index(AXES)))
    spots = [
        jnp.where(core == 0, (x, y, z)[ORDER[0][stage]], (x, y, z)[ORDER[1][stage]]).reshape(1)
        for stage in range(3)
    ]
    core = core.reshape(1)
    their_spot = jnp.where(core == 0, (x, y, z)[ORDER[1][0]], (x, y, z)[ORDER[0][0]])
    steps = jnp.arange(4, dtype=jnp.int32)
    places = jnp.concatenate(
        [4 * core + (spots[0] + steps) % 4, 4 * (1 - core) + (their_spot + steps) % 4]
    )
    exists = jnp.stack(
        [
            (gy + row_step >= 0)
            & (gy + row_step < N_GY)
            & (gx + col_step >= 0)
            & (gx + col_step < N_GX)
            for row_step, col_step in PIECES
        ]
    ).astype(F32)
    tokens = embeddings.reshape(TOKENS, WIDTH)

    raw = jnp.where(tile_valid[:, :, None] > 0, embeddings, jnp.asarray(MARK, BF))
    left = sent(raw[:, WINDOW:].reshape(SIDE, WIDTH), grid_pairs(0, -1))
    right = sent(raw[:, :WINDOW].reshape(SIDE, WIDTH), grid_pairs(0, 1))
    act, marked, spread = pre([tokens, tile_valid, gain_attn, shift_attn])
    band = small_call(
        band_kernel,
        "band",
        [],
        [marked, left, right, gain_attn, shift_attn],
        [shape(BAND, WIDTH, BF)],
    )[0]
    spread, band = after(spread, band)
    far_own = exchanged(spread.reshape(GROUP, FAR_OWN, WIDTH)).reshape(FAR_HALF, WIDTH)
    bands = [band, sent(band, grid_pairs(-1, 0)), sent(band, grid_pairs(1, 0))]
    near, bias_near, queries, k_near, v_near, tops, totals, sums = attend_near(
        exists, act, bands, tile_valid, jnp.asarray(window_weights()), w_query, w_key, w_value
    )
    far_own, sums = after(far_own, sums)
    far_other = sent(far_own, CORE_PAIRS)
    grad_out = cotangent.reshape(TOKENS, WIDTH)
    (
        far, bias_far, k_far, v_far, outs, lse, middle, mixed, keep, send, grad_act
    ) = attend_far(
        core,
        [
            far_own, far_other, tokens, queries, w_key, w_value, w_out, tops, totals, sums,
            gain_mlp, shift_mlp, grad_out,
        ],
        [w_up, w_down],
    )
    swapped = sent(send, CORE_PAIRS)

    def rest(operands):
        (
            keep, swapped, outs, middle, grad_act, gain_mlp, gain_attn, grad_out, tokens, queries, lse,
            k_near, v_near, k_far, v_far, bias_near, bias_far, near, far,
            w_query, w_key, w_value, w_out, core, spots, places,
        ) = operands
        quarter = shape(2 * QUARTER, WIDTH, BF)
        mlp_parts = small_call(
            mlp_grads_kernel,
            "mlp_grads",
            [spots[0]],
            [keep, swapped],
            [quarter] * 4,
            [pltpu.VMEM((2 * TOKENS, SWAP), BF)],
        )

        def around(stage, parts):
            return [parts[0]] + [sent(parts[step], ring_pairs(stage, step)) for step in (2, 1, 3)]

        def gathered(stage, part):
            got = {step: sent(part, ring_pairs(stage, -step)) for step in (2, 1, 3)}
            return [part, got[1], got[2], got[3]]

        def in_plane(cells):
            return lax.all_to_all(
                cells.reshape(PLANE, PLANE_ROWS, WIDTH), AXES, 0, 0, tiled=True,
                axis_index_groups=plane_groups(),
            ).reshape(2 * QUARTER, WIDTH)

        mlp_held = around(0, mlp_parts)
        grad_act, _ = after(grad_act, mlp_parts[0])
        grad_wo, grad_mid, small, grad_att, inner, flip, key_flip = small_call(
            mid_kernel,
            "mid",
            [],
            [outs, middle, grad_act, gain_mlp, grad_out, w_out, k_near, k_far, near, far],
            [shape(WIDTH, WIDTH, BF), shape(TOKENS, WIDTH, F32), shape(8, WIDTH, F32)]
            + [shape(TOKENS, WIDTH, BF), shape(WIDTH, TOKENS, F32)]
            + [shape(WIDTH, NEAR + FAR, BF)] * 2,
            flops=30_000_000_000,
        )
        grad_wq, grad_wk, grad_wv, grad_own, piece_left, piece_right, piece_up, piece_down, grad_far = (
            attend_back(
                [
                    queries, grad_att, inner, lse, k_near, v_near, k_far, v_far, bias_near, bias_far,
                    flip, key_flip, w_query, w_key, w_value,
                ]
            )
        )
        mlp_held[0], grad_own = after(mlp_held[0], grad_own)
        mlp_sum = add(mlp_held)
        mlp_cells = in_plane(mlp_sum)
        grad_far, piece_up, piece_down, _ = after(grad_far, piece_up, piece_down, mlp_sum)
        packed = small_call(
            pack_kernel,
            "pack",
            [core],
            [grad_wq, grad_wk, grad_wv, grad_wo, grad_far],
            [shape(HALF + FAR_HALF, WIDTH, BF)] * 2,
        )
        held = [packed[0], sent(packed[1], CORE_PAIRS)]
        above = sent(piece_down, grid_pairs(-1, 0))
        below = sent(piece_up, grid_pairs(1, 0))
        parts = first_split(spots[0], held)
        held = around(0, parts)
        mlp_cells, _ = after(mlp_cells, parts[0])
        mlp_cells = small_call(plane_sum_kernel, "plane_sum", [], [mlp_cells], [quarter])[0]
        mlp_own = in_plane(mlp_cells)
        piece_left, _ = after(piece_left, mlp_cells)
        side = shape(SIDE, WIDTH, BF)
        piece_left, piece_right = fetched_call(
            fold_kernel, "fold", [piece_left, piece_right, above, below], [side, side]
        )
        from_right = sent(piece_left, grid_pairs(0, 1))
        from_left = sent(piece_right, grid_pairs(0, -1))
        held[0], _ = after(held[0], piece_left)
        parts = split(spots[1], held)
        held = around(1, parts)
        held[0], mlp_own = after(held[0], mlp_own)
        parts = split(spots[2], held, ((0, 4 * SHARE), (4 * SHARE, 4 * FAR_OWN)))
        held = around(2, parts)
        mlp_own, _ = after(mlp_own, parts[0])
        mlp_held = gathered(0, mlp_own)
        grad_inputs, cell = fetched_call(
            tail_kernel,
            "tail",
            held
            + [grad_own, above, below, from_left, from_right, tokens, gain_attn, grad_mid, small],
            [shape(TOKENS, WIDTH, F32), shape(SHARE + 8, WIDTH, BF)],
        )
        cell = join(spots[2], gathered(2, cell), 8)
        held = gathered(1, cell)
        held[0], *mlp_held = after(held[0], *mlp_held)
        cell = join(spots[1], held, 8)
        others = [sent(piece, CORE_PAIRS) for piece in mlp_held]
        held = gathered(0, cell)
        grad_up, grad_down = finish_mlp(places, mlp_held + others)
        held[0], _ = after(held[0], grad_up)
        cell = join(spots[0], held, 8)
        grad_wq, grad_wk, grad_wv, grad_wo, *vectors = finish(core, cell)
        return grad_inputs, grad_up, grad_down, grad_wq, grad_wk, grad_wv, grad_wo, *vectors

    def never(operands):
        return (
            jnp.zeros((TOKENS, WIDTH), F32),
            jnp.zeros((WIDTH, HIDDEN), F32),
            jnp.zeros((HIDDEN, WIDTH), F32),
            *[jnp.zeros((WIDTH, WIDTH), F32)] * 4,
            *[jnp.zeros((WIDTH,), F32)] * 4,
        )

    grad_inputs, grad_up, grad_down, grad_wq, grad_wk, grad_wv, grad_wo, *vectors = lax.cond(
        gx < N_GX,
        rest,
        never,
        (
            keep, swapped, outs, middle, grad_act, gain_mlp, gain_attn, grad_out, tokens, queries, lse,
            k_near, v_near, k_far, v_far, bias_near, bias_far, near, far,
            w_query, w_key, w_value, w_out, core, spots, places,
        ),
    )
    return (
        mixed.reshape(ROWS, COLS, WIDTH),
        grad_inputs.reshape(ROWS, COLS, WIDTH),
        grad_wq,
        grad_wk,
        grad_wv,
        grad_wo,
        grad_up,
        grad_down,
        vectors[0],
        vectors[1],
        vectors[2],
        vectors[3],
    )


def solution(mesh):
    grid = P("gy", "gx", None)
    in_specs = (grid, P("gy", "gx")) + (P(),) * 10 + (grid,)
    out_specs = (grid, grid) + (P(),) * 10
    return jax.shard_map(local, mesh=mesh, in_specs=in_specs, out_specs=out_specs, check_vma=False)
```
